512 devices in a mesh: prefix: 8 (over y, core), branch: 16 (over z), tensor: 4 (over x).
Axes of the slice: x: 4, y: 4, z: 16, core: 2. Of those that a mesh axis runs over, the one named last changes fastest.
Arguments:
- prompt_x: bfloat16 [2048, 16, 4, 128], P('prefix', 'branch', 'tensor'), may hold values from -6 to 6
- prompt_bc: bfloat16 [2048, 4, 256], P('prefix', 'tensor'), may hold values from -6 to 6
- prompt_dt: float32 [16, 4, 2, 2048], P('branch', 'tensor', None, 'prefix'), may hold values from -4 to 4
- branch_x: bfloat16 [16, 1024, 16, 4, 128], P('branch', 'prefix', None, 'tensor'), may hold values from -6 to 6
- branch_bc: bfloat16 [16, 1024, 4, 256], P('branch', 'prefix', 'tensor'), may hold values from -6 to 6
- branch_dt: float32 [16, 16, 4, 2, 1024], P('branch', None, 'tensor', None, 'prefix'), may hold values from -4 to 4
- conv_x: float32 [4, 16, 4, 128], P(None, None, 'tensor'), may hold values from -3 to 3
- conv_bc: float32 [4, 4, 256], P(None, 'tensor'), may hold values from -3 to 3
- a_log: float32 [16, 4, 2], P(None, 'tensor'), may hold values from -4 to 1.5
- dt_bias: float32 [16, 4, 2], P(None, 'tensor'), may hold values from -6 to -2
- d_skip: float32 [16, 4, 2], P(None, 'tensor'), may hold values from 0.5 to 1.5
- lengths: int32 [16], replicated, may hold values from 1 to 1024, 8192 in all
- forks: int32 [16], replicated, may hold values from 1 to 2048
- holder: int32 [16], replicated, may hold values from 0 to 1023, as said below
- prompt_dy: bfloat16 [2048, 16, 4, 128], P('prefix', 'branch', 'tensor'), may hold values from -6 to 6
- branch_dy: bfloat16 [16, 1024, 16, 4, 128], P('branch', 'prefix', None, 'tensor'), may hold values from -6 to 6
Outputs:
- prompt_y: bfloat16 [2048, 16, 4, 128], P('prefix', 'branch', 'tensor')
- branch_y: bfloat16 [16, 1024, 16, 4, 128], P('branch', 'prefix', None, 'tensor')
- prompt_gx: bfloat16 [2048, 16, 4, 128], P('prefix', 'branch', 'tensor')
- branch_gx: bfloat16 [16, 1024, 16, 4, 128], P('branch', 'prefix', None, 'tensor')
- prompt_gbc: bfloat16 [2048, 4, 256], P(('prefix', 'branch'), 'tensor')
The draws below stay inside these ranges and needn't reach their ends.
Inputs may be any that keep to these rules, and one draw needn't show every extreme that they name: `holder`: the keys are distinct.
All inputs are finite; a program needn't handle non-finite values.
Results may differ from the reference program's by a relative error of at most 0.002.
Values sent between devices are 32-bit elements; how exact they have to be, the bound alone decides.
No kernel may reach another device: no remote copies, remote signals or barrier semaphores. Data moves between devices by JAX's collectives and lax.ppermute only.
A program may use at most 192 MiB of HBM per device.

```python
import math
import jax
import jax.numpy as jnp
import numpy as np
from jax import lax

HEAD_DIM = 64
STATE = 128
BLOCK = 64
HPD = 2
PROMPT = 2048
BMAX = 1024
BRANCHES = 16
N_BRANCH = 16
N_TENSOR = 4


def draw_holder(key, part):
    key = jax.random.fold_in(key, 7)
    rank_key, offset_key = jax.random.split(key)
    ranks = jax.random.permutation(rank_key, BRANCHES).astype(jnp.int32)
    offsets = jax.random.randint(offset_key, (BRANCHES,), 0, 64).astype(jnp.int32)
    offsets = jnp.where(ranks == 0, 0, jnp.where(ranks == BRANCHES - 1, 63, offsets))
    return (ranks * 64 + offsets).astype(jnp.int32)


def with_ends(entries, rng, smallest, largest):
    longest = entries.shape.index(max(entries.shape))
    spots = []
    for shift in (0, 1):
        where = [jax.random.randint(jax.random.fold_in(rng, axis), (), 0, length) for axis, length in enumerate(entries.shape)]
        where[longest] = (where[longest] + shift) % entries.shape[longest]
        spots.append(tuple(where))
    return entries.at[spots[0]].set(smallest).at[spots[1]].set(largest)


def shard_levels(key, extent, cuts, low, largest):
    gain, own = 1.0, jax.random.fold_in(key, 6)
    for dim, shards_of in cuts:
        steps = jnp.exp(jax.random.uniform(jax.random.fold_in(own, dim), (shards_of,), jnp.float32, low / len(cuts), largest / len(cuts)))
        gain = gain * jnp.repeat(steps, extent[dim] // shards_of).reshape([-1 if axis == dim else 1 for axis in range(len(extent))])
    return gain


def profile(amount, total, reach, slope):
    portions = [(1 << 20) // math.isqrt(standing ** slope) + 1 for standing in range(2, amount + 1)]
    rest, given = total - reach - (amount - 1), [1] * (amount - 1)
    while rest > 0:
        candidates = [i for i in range(amount - 1) if given[i] < reach]
        pool, budget = sum([portions[i] for i in candidates]), rest
        for i in candidates:
            extra = min(reach - given[i], max(1, budget * portions[i] // pool), rest)
            given[i] = given[i] + extra
            rest = rest - extra
    return np.array([reach] + given)


def uneven(key, count, total, limit, lean):
    if count == 2:
        one = jax.random.randint(key, (), max(1, total - limit), min(limit, total - 1) + 1)
        return jnp.stack([one, total - one])
    tallies = jnp.asarray(profile(count, total, limit, lean), jnp.int32)
    twos = (count - 1) // 2
    source_of, taker = tallies[1:1 + 2 * twos:2], tallies[2:2 + 2 * twos:2]
    slack = jnp.minimum(source_of - 1, limit - taker)
    moved = jax.random.randint(jax.random.fold_in(key, 1), (twos,), 0, 1 << 20) % (slack + 1)
    tallies = tallies.at[1:1 + 2 * twos:2].set(source_of - moved).at[2:2 + 2 * twos:2].set(taker + moved)
    return tallies[jax.random.permutation(jax.random.fold_in(key, 2), count)]


def centred(own_key, extent, deviation, most, cuts=(), held_as=jnp.bfloat16):
    array = jax.random.normal(own_key, extent, jnp.float32) * deviation
    if len(cuts) > 0:
        array = shard_levels(own_key, extent, cuts, -0.22, 0.18) * array
    return jnp.clip(array, min=-most, max=most).astype(held_as)


def setup_inputs(seed: int = 0) -> dict:
    seeds = jax.random.split(jax.random.key(seed), 17)
    return {
        "prompt_x": centred(seeds[0], (PROMPT, N_BRANCH, N_TENSOR, HPD * HEAD_DIM), 1.0, 6.0, ((0, 8), (1, 16), (2, 4))),
        "prompt_bc": centred(seeds[1], (PROMPT, N_TENSOR, 2 * STATE), 1.0, 6.0, ((0, 8), (1, 4))),
        "prompt_dt": centred(seeds[2], (N_BRANCH, N_TENSOR, HPD, PROMPT), 1.0, 4.0, ((0, 16), (1, 4), (3, 8)), jnp.float32),
        "branch_x": centred(seeds[3], (BRANCHES, BMAX, N_BRANCH, N_TENSOR, HPD * HEAD_DIM), 1.0, 6.0, ((0, 16), (1, 8), (3, 4))),
        "branch_bc": centred(seeds[4], (BRANCHES, BMAX, N_TENSOR, 2 * STATE), 1.0, 6.0, ((0, 16), (1, 8), (2, 4))),
        "branch_dt": centred(seeds[5], (BRANCHES, N_BRANCH, N_TENSOR, HPD, BMAX), 1.0, 4.0, ((0, 16), (2, 4), (4, 8)), jnp.float32),
        "conv_x": centred(seeds[6], (4, N_BRANCH, N_TENSOR, HPD * HEAD_DIM), 0.5, 3.0, ((2, 4),), jnp.float32),
        "conv_bc": centred(seeds[7], (4, N_TENSOR, 2 * STATE), 0.5, 3.0, ((1, 4),), jnp.float32),
        "a_log": jnp.clip(-4.0 + 5.5 * jax.random.uniform(seeds[8], (N_BRANCH, N_TENSOR, HPD), jnp.float32) ** shard_levels(seeds[8], (N_BRANCH, N_TENSOR, HPD), ((1, 4),), -0.2, 0.2), -4.0, 1.5),
        "dt_bias": jnp.clip(-6.0 + 4.0 * jax.random.uniform(seeds[9], (N_BRANCH, N_TENSOR, HPD), jnp.float32) ** shard_levels(seeds[9], (N_BRANCH, N_TENSOR, HPD), ((1, 4),), -0.2, 0.2), -6.0, -2.0),
        "d_skip": jnp.clip(0.5 + 1.0 * jax.random.uniform(seeds[10], (N_BRANCH, N_TENSOR, HPD), jnp.float32) ** shard_levels(seeds[10], (N_BRANCH, N_TENSOR, HPD), ((1, 4),), -0.2, 0.2), 0.5, 1.5),
        "lengths": uneven(seeds[11], BRANCHES, BRANCHES * BMAX // 2, BMAX, 2).astype(jnp.int32),
        "forks": with_ends(jax.random.randint(seeds[12], (BRANCHES,), 1, PROMPT + 1), jax.random.fold_in(seeds[12], 1), 1, PROMPT).astype(jnp.int32),
        "holder": draw_holder(jax.random.fold_in(seeds[16], 71), 0),
        "prompt_dy": centred(seeds[14], (PROMPT, N_BRANCH, N_TENSOR, HPD * HEAD_DIM), 1.0, 6.0, ((0, 8), (1, 16), (2, 4))),
        "branch_dy": centred(seeds[15], (BRANCHES, BMAX, N_BRANCH, N_TENSOR, HPD * HEAD_DIM), 1.0, 6.0, ((0, 16), (1, 8), (3, 4))),
    }


highest = lax.Precision.HIGHEST

def silu_conv(raw, tail_rows, kernel):
    length_t = raw.shape[0]
    padded = jnp.concatenate([tail_rows, raw], axis=0)
    summed = kernel[0] * padded[0:length_t]
    for offset in range(1, 4):
        summed = summed + kernel[offset] * padded[offset:offset + length_t]
    return jax.nn.silu(summed)

def to_blocks(values, block):
    return values.reshape((values.shape[0] // block, block) + values.shape[1:])

def block_pass(x_conv, b_conv, c_conv, step_size, log_decay, block):
    lower_mask = jnp.arange(block)[:, None] >= jnp.arange(block)[None, :]
    causal = lower_mask[:, :, None, None, None]

    def advance(state, pieces):
        x_blk, b_blk, c_blk, dt_blk, ld_blk = pieces
        within = jnp.cumsum(ld_blk, axis=0)
        gaps = within[:, None] - within[None, :]
        decays = jnp.where(causal, jnp.exp(jnp.where(causal, gaps, 0.0)), 0.0)
        scores = jnp.einsum('tgn,sgn->tsg', c_blk, b_blk, precision=highest)
        mixing = decays * scores[:, :, None, :, None] * dt_blk[None]
        inner = jnp.einsum('tsjgk,sjgkp->tjgkp', mixing, x_blk, precision=highest)
        carried = jnp.einsum('jgkpn,tgn->tjgkp', state, c_blk, precision=highest) * jnp.exp(within)[..., None]
        weights = jnp.exp(within[-1][None] - within) * dt_blk
        fresh = jnp.einsum('sjgk,sjgkp,sgn->jgkpn', weights, x_blk, b_blk, precision=highest)
        updated = jnp.exp(within[-1])[..., None, None] * state + fresh
        return (updated, (inner + carried, state))
    initial = jnp.zeros(x_conv.shape[1:] + (b_conv.shape[-1],), jnp.float32)
    final, (outputs, starts) = lax.scan(advance, initial, (to_blocks(x_conv, block), to_blocks(b_conv, block), to_blocks(c_conv, block), to_blocks(step_size, block), to_blocks(log_decay, block)))
    return (outputs.reshape(x_conv.shape), final, starts)

def states_at(x_conv, b_conv, step_size, log_decay, starts, position, valid, block):
    which = position // block
    inside = position - which * block
    x_rows = to_blocks(x_conv, block)[which]
    b_rows = to_blocks(b_conv, block)[which]
    dt_rows = to_blocks(step_size, block)[which]
    ld_rows = to_blocks(log_decay, block)[which]
    within = jnp.cumsum(ld_rows, axis=1)
    picker = (jnp.arange(block, dtype=jnp.int32)[None, :] == inside[:, None]).astype(jnp.float32)
    at_pos = jnp.einsum('ns,nsjgk->njgk', picker, within, precision=highest)
    upto = (jnp.arange(block, dtype=jnp.int32)[None, :] <= inside[:, None])[:, :, None, None, None]
    weights = jnp.where(upto, jnp.exp(jnp.where(upto, at_pos[:, None] - within, 0.0)), 0.0) * dt_rows
    partial_state = jnp.einsum('nsjgk,nsjgkp,nsgq->njgkpq', weights, x_rows, b_rows, precision=highest)
    carried = jnp.exp(at_pos)[..., None, None] * starts[which]
    return (partial_state + carried) * valid[:, None, None, None, None, None]

def start_terms(state_in, c_conv, running):
    return jnp.einsum('jgkpn,tgn->tjgkp', state_in, c_conv, precision=highest) * jnp.exp(running)[..., None]

def reference(prompt_x, prompt_bc, prompt_dt, branch_x, branch_bc, branch_dt, conv_x, conv_bc, a_log, dt_bias, d_skip, lengths, forks, holder, prompt_dy, branch_dy):
    heads = (N_BRANCH, N_TENSOR, HPD)
    kernel_x = conv_x.reshape((4,) + heads + (HEAD_DIM,))
    rate = jnp.exp(a_log)
    skip_gain = d_skip[..., None]
    prompt_step = jax.nn.softplus(jnp.transpose(prompt_dt, (3, 0, 1, 2)) + dt_bias)
    prompt_logs = -rate * prompt_step
    branch_step = jax.nn.softplus(jnp.transpose(branch_dt, (0, 4, 1, 2, 3)) + dt_bias)
    branch_logs = -rate * branch_step
    placed = lax.optimization_barrier(jnp.sum((holder[None, :] < holder[:, None]).astype(jnp.int32), axis=1)).astype(jnp.int32)
    owners = (placed[None, :] == jnp.arange(BRANCHES, dtype=jnp.int32)[:, None]).astype(jnp.int32)
    group_length = lax.optimization_barrier(jnp.sum(owners * lengths[None, :], axis=1))
    group_fork = lax.optimization_barrier(jnp.sum(owners * forks[None, :], axis=1))
    live = (jnp.arange(BMAX, dtype=jnp.int32)[None, :] < group_length[:, None]).astype(jnp.float32)
    live_full = live[:, :, None, None, None, None]
    tail_index = group_fork[:, None] - 3 + jnp.arange(3, dtype=jnp.int32)[None, :]
    tail_valid = (tail_index >= 0).astype(jnp.float32)
    tail_safe = jnp.maximum(tail_index, 0).astype(jnp.int32)

    def forward(prompt_in, bc_in, branch_in):
        prompt_raw = prompt_in.astype(jnp.float32).reshape((PROMPT,) + heads + (HEAD_DIM,))
        bc_raw = bc_in.astype(jnp.float32)
        empty_x = jnp.zeros((3,) + prompt_raw.shape[1:], jnp.float32)
        empty_bc = jnp.zeros((3,) + bc_raw.shape[1:], jnp.float32)
        x_conv = silu_conv(prompt_raw, empty_x, kernel_x)
        bc_conv = silu_conv(bc_raw, empty_bc, conv_bc)
        outputs, final, starts = block_pass(x_conv, bc_conv[..., :STATE], bc_conv[..., STATE:], prompt_step, prompt_logs, BLOCK)
        prompt_out = outputs + skip_gain * x_conv
        fork_state = states_at(x_conv, bc_conv[..., :STATE], prompt_step, prompt_logs, starts, (group_fork - 1).astype(jnp.int32), jnp.ones((BRANCHES,), jnp.float32), BLOCK)
        tail_x = prompt_raw[tail_safe] * tail_valid[:, :, None, None, None, None]
        tail_bc = bc_raw[tail_safe] * tail_valid[:, :, None, None]

        def one_branch(pieces):
            branch_row, bc_row, step_row, logs_row, start_row, tx_row, tbc_row = pieces
            raw_x = branch_row.astype(jnp.float32).reshape((BMAX,) + heads + (HEAD_DIM,))
            xb_conv = silu_conv(raw_x, tx_row, kernel_x)
            bcb_conv = silu_conv(bc_row.astype(jnp.float32), tbc_row, conv_bc)
            branch_out, final_b, starts_b = block_pass(xb_conv, bcb_conv[..., :STATE], bcb_conv[..., STATE:], step_row, logs_row, BLOCK)
            running = jnp.cumsum(logs_row, axis=0)
            return branch_out + start_terms(start_row, bcb_conv[..., STATE:], running) + skip_gain * xb_conv
        branch_out_all = lax.map(one_branch, (branch_in, branch_bc, branch_step, branch_logs, fork_state, tail_x, tail_bc))
        return (prompt_out, branch_out_all)
    (prompt_out, branch_out), pullback = jax.vjp(forward, prompt_x, prompt_bc, branch_x)
    prompt_cot = prompt_dy.astype(jnp.float32).reshape(prompt_out.shape)
    branch_cot = branch_dy.astype(jnp.float32).reshape(branch_out.shape) * live_full
    grad_prompt, grad_bc, grad_branch = pullback((prompt_cot, branch_cot))
    prompt_y = prompt_out.reshape(prompt_x.shape).astype(jnp.bfloat16)
    branch_y = (branch_out * live_full).reshape(branch_x.shape).astype(jnp.bfloat16)
    return (prompt_y, branch_y, grad_prompt, grad_branch, grad_bc)
```

```python
import functools

import jax
import jax.numpy as jnp
from jax import lax
from jax.experimental import pallas as pl
from jax.experimental.pallas import tpu as pltpu
from jax.sharding import PartitionSpec as P

HEAD_DIM = 64
STATE = 128
LANES = 128

F32 = jnp.float32
BF16 = jnp.bfloat16

TAIL_X = 0
TAIL_BC = 48
ROW_X = 54
ROW_DY = 102
ROW_BC = 150
ROW_STEP = 160
ROW_LOG = 168
EARLY = 176

VMEM_LIMIT = 56 * 1024 * 1024


def split2(a):
    hi = a.astype(BF16)
    return hi, (a - hi.astype(F32)).astype(BF16)


def split3(a):
    hi = a.astype(BF16)
    rest = a - hi.astype(F32)
    mid = rest.astype(BF16)
    return hi, mid, (rest - mid.astype(F32)).astype(BF16)


def mm(a, b):
    return lax.dot_general(a, b, (((1,), (0,)), ((), ())), preferred_element_type=F32)


def mm_nt(a, b):
    return lax.dot_general(a, b, (((1,), (1,)), ((), ())), preferred_element_type=F32)


def left(a):
    hi, lo = split2(a)
    return jnp.concatenate([hi, hi, lo], axis=1)


def right(b):
    hi, lo = split2(b)
    return jnp.concatenate([hi, lo, hi], axis=0)


def right_nt(b):
    hi, lo = split2(b)
    return jnp.concatenate([hi, lo, hi], axis=1)


def exact(a):
    return jnp.concatenate(split3(a), axis=1)


def iota(shape, dim):
    return lax.broadcasted_iota(jnp.int32, shape, dim)


def picker(base, j):
    one = (iota((LANES, LANES), 0) == base + 2 * j + iota((LANES, LANES), 1) // HEAD_DIM).astype(
        F32
    ).astype(BF16)
    return jnp.concatenate([one, one, one], axis=0)


def running_sum(logs):
    size = logs.shape[1]
    upper = (iota((size, size), 0) <= iota((size, size), 1)).astype(F32).astype(BF16)
    return mm(exact(logs), jnp.concatenate([upper, upper, upper], axis=0))


def block(j):
    return pl.ds(pl.multiple_of(j * LANES, LANES), LANES)


def sigmoid(x):
    return 1.0 / (1.0 + jnp.exp(-x))


def conv_branch(bx, rim, convx, xs, xt, ds):
    js = bx.shape[1]
    for r in range(3):
        xs[(5 + r) * js : (6 + r) * js, :] = rim[r, 0:js, :]

    def fill(c, _):
        xs[pl.ds(pl.multiple_of(8 * js + c * 16 * js, 16 * js), 16 * js), :] = (
            bx[pl.ds(c * 16, 16)].astype(F32).reshape(16 * js, LANES)
        )
        return 0

    lax.fori_loop(0, bx.shape[0] // 16, fill, 0)

    def one(c, _):
        pre = jnp.zeros((16, js, LANES), F32)
        for i in range(4):
            start = pl.multiple_of((5 + i) * js + c * 16 * js, js)
            pre = pre + convx[i][None] * xs[pl.ds(start, 16 * js), :].reshape(16, js, LANES)
        sg = sigmoid(pre)
        at = pl.ds(pl.multiple_of(c * 16 * js, 16 * js), 16 * js)
        xt[at, :] = (pre * sg).reshape(16 * js, LANES)
        if ds is not None:
            ds[at, :] = (sg * (1.0 + pre * (1.0 - sg))).reshape(16 * js, LANES)
        return 0

    lax.fori_loop(0, bx.shape[0] // 16, one, 0)


def conv_rows(raw, halo_rows, taps, scratch):
    n = raw.shape[0]
    scratch[8 : 8 + n, :] = raw.astype(F32)
    for r in range(3):
        scratch[5 + r : 6 + r, :] = halo_rows[r]
    pre = jnp.zeros(raw.shape, F32)
    for i in range(4):
        pre = pre + taps[i] * scratch[5 + i : 5 + i + n, :]
    return pre


def bc_halo(rim, first):
    return [
        jnp.concatenate([rim[r, first : first + 1, :], rim[r, first + 1 : first + 2, :]], axis=1)
        for r in range(3)
    ]


def silu(x):
    return x * sigmoid(x)


def silu_slope(x):
    sg = sigmoid(x)
    return sg * (1.0 + x * (1.0 - sg))


def branch_table(step, run):
    return jnp.concatenate([step, run, jnp.zeros((64, LANES), F32)], axis=0).T


def prompt_table(step, run):
    n = step.shape[1]
    r = iota((LANES, n), 0)
    runs = jnp.where(r % 2 == 0, run[0:1], run[1:2])
    steps = jnp.where(r % 2 == 0, step[0:1], step[1:2])
    return jnp.where((r == 2) | (r == 3), steps, runs).T


def halves(first, second, shape):
    return jnp.where(iota(shape, 1) < HEAD_DIM, first, second)


def local_kernel(
    scal, px, pbc, pstep, plogs, pdy, bx, bbc, bstep, blogs, bdy, rim, convx, convbc,
    out, xs, xt, dys, bcs, pxs, pbcs, wexp, tab,
):
    row, col, length = scal[17], scal[18], scal[16]
    n, js = bx.shape[0], bx.shape[1]
    span = px.shape[0]
    conv_branch(bx, rim, convx, xs, xt, None)

    def fill(c, _):
        pos = row * n + c * 16 + iota((16, js, LANES), 0)
        dead = (pos >= length) | (pos < 3)
        dys[pl.ds(pl.multiple_of(c * 16 * js, 16 * js), 16 * js), :] = jnp.where(
            dead, 0.0, bdy[pl.ds(c * 16, 16)].astype(F32)
        ).reshape(16 * js, LANES)
        return 0

    lax.fori_loop(0, n // 16, fill, 0)
    taps = [convbc[i : i + 1, :] for i in range(4)]
    bc = silu(conv_rows(bbc[...], bc_halo(rim, 19), taps, bcs))
    b_t = left(bc[:, :STATE].T)
    c_t = left(bc[:, STATE:].T)
    table = branch_table(bstep[...], running_sum(blogs[...]))
    parts = exact(table)

    def head_pair(j, _):
        at = pl.ds(j, n, stride=js)
        steps = mm(parts, picker(0, j))
        runs = mm(parts, picker(32, j))
        x_w = xt[at, :] * steps * jnp.exp(runs[n - 1 : n, :] - runs)
        out[:, block(j)] = mm(b_t, right(x_w))
        out[:, block(js + j)] = mm(c_t, right(dys[at, :] * jnp.exp(runs)))
        return 0

    lax.fori_loop(0, js, head_pair, 0)

    own = [convx[i, pl.ds(col, 1), :] for i in range(4)]
    x_p = silu(conv_rows(px[...], [rim[r, 16:17, :] for r in range(3)], own, pxs))
    bc_p = silu(conv_rows(pbc[...], bc_halo(rim, 17), taps, pbcs))
    b_pt = left(bc_p[:, :STATE].T)
    c_pt = left(bc_p[:, STATE:].T)
    ptable = prompt_table(pstep[...], running_sum(plogs[...]))
    tab[...] = ptable
    runs = halves(ptable[:, 0:1], ptable[:, 1:2], (span, LANES))
    steps = halves(ptable[:, 2:3], ptable[:, 3:4], (span, LANES))
    wexp[...] = runs
    x_hat = x_p * steps
    base = 3 * js * LANES
    out[:, base : base + LANES] = mm(b_pt, right(x_hat * jnp.exp(runs[span - 1 : span, :] - runs)))
    out[:, base + LANES : base + 2 * LANES] = mm(
        c_pt, right(pdy[...].astype(F32) * jnp.exp(runs))
    )
    lane = iota((1, LANES), 1)
    pxs[0:span, :] = x_hat

    def fork(g, acc):
        where = scal[g] - 1 - row * span
        inside = (where >= 0) & (where < span)

        @pl.when(inside)
        def _():
            w = wexp[...]
            gap = wexp[pl.ds(where, 1), :] - w
            upto = iota((span, LANES), 0) <= where
            u = jnp.exp(jnp.where(upto, gap, -1e30)) * pxs[0:span, :]
            out[:, block(2 * js + g)] = mm(b_pt, right(u))

        @pl.when(jnp.logical_not(inside))
        def _():
            out[:, block(2 * js + g)] = jnp.zeros((STATE, LANES), F32)

        safe = jnp.clip(where, 0, span - 1)
        return jnp.where(lane // 2 == 32 + g, tab[pl.ds(safe, 1), :], acc)

    marks = lax.fori_loop(0, js, fork, jnp.zeros((1, LANES), F32))
    misc = jnp.where(lane < 2, ptable[span - 1 : span, :], marks)
    misc = jnp.where((lane >= 32) & (lane < 64), table[n - 1 : n, :], misc)
    out[:, base + 2 * LANES : base + 3 * LANES] = jnp.broadcast_to(misc, (STATE, LANES))


def slice_kernel(scal, got, early, convbc, msg, aft, adj, pst, cols, mat, turned):
    row = scal[17]
    count, ns = got.shape[0], got.shape[1]
    js = msg.shape[0]
    span = scal[19]
    for half in range(2):
        seq = [
            jnp.sum(early[:, TAIL_BC + 2 * r + half, :], axis=0, keepdims=True) for r in range(3)
        ] + [early[0, ROW_BC + 2 * s + half : ROW_BC + 2 * s + half + 1, :] for s in range(3)]
        taps = [convbc[i : i + 1, half * STATE : (half + 1) * STATE] for i in range(4)]
        mat[...] = jnp.zeros((LANES, LANES), F32)
        for s in range(3):
            mat[s : s + 1, :] = sum(taps[i] * seq[s + i] for i in range(4))
        for i in range(4):
            mat[8 + i : 9 + i, :] = taps[i]
        turned[half * STATE : (half + 1) * STATE, :] = mat[...].T
    start = pl.multiple_of(row * ns, 16)
    b_col = turned[pl.ds(start, ns), :]
    c_col = turned[pl.ds(STATE + start, ns), :]
    cols[0:ns, :] = b_col
    cols[ns : 2 * ns, :] = c_col
    c_all = silu(c_col)
    misc = got[:, 0, (3 * js + 2) * LANES : (3 * js + 3) * LANES]
    misc_parts = exact(misc)
    log_parts = exact(early[0, ROW_LOG : ROW_LOG + 8, :])
    for j in range(js):
        at = slice(j * LANES, (j + 1) * LANES)
        lead = slice((js + j) * LANES, (js + j + 1) * LANES)
        fall = jnp.exp(mm(misc_parts, picker(32, j)))
        falls = jnp.exp(mm(log_parts, picker(0, j)))
        a = jnp.zeros((ns, LANES), F32)
        for p in reversed(range(count)):
            aft[p, :, at] = a
            a = fall[p : p + 1] * a + got[p, :, lead]
        for s in (2, 1, 0):
            dy = early[0, ROW_DY + s * js + j : ROW_DY + s * js + j + 1, :]
            a = a + dy * c_all[:, s : s + 1]
            adj[s, :, at] = a
            a = falls[s : s + 1] * a
        msg[j, 0:ns, LANES : 2 * LANES] = a
    pfall = jnp.exp(halves(misc[:, 0:1], misc[:, 1:2], (count, LANES)))
    base = 3 * js * LANES
    state = jnp.zeros((ns, LANES), F32)
    for p in range(count):
        pst[p] = state
        state = pfall[p : p + 1] * state + got[p, :, base : base + LANES]
    for g in range(js):
        holder = lax.div(scal[g] - 1, span)
        mark = got[holder, 0:1, base + 2 * LANES : base + 3 * LANES]
        reach = jnp.exp(
            halves(mark[:, 64 + 2 * g : 65 + 2 * g], mark[:, 65 + 2 * g : 66 + 2 * g], (1, LANES))
        )
        at = slice((2 * js + g) * LANES, (2 * js + g + 1) * LANES)
        msg[g, 0:ns, 0:LANES] = got[holder, :, at] + reach * pst[holder]
        msg[g, ns : ns + 8, :] = jnp.zeros((8, 2 * LANES), F32)
        for r in range(3):
            msg[g, ns + r : ns + r + 1, 0:LANES] = jnp.sum(
                early[:, TAIL_X + 3 * g + r, :], axis=0, keepdims=True
            )


def chain_kernel(
    scal, got, early, moved, aft, adj, pst, cols, convx, skip, msg, rows, injected
):
    row = scal[17]
    first = (row == 0).astype(F32)
    count, ns = got.shape[0], got.shape[1]
    js = moved.shape[0]
    span = scal[19]
    b_col, c_col = cols[0:ns, :], cols[ns : 2 * ns, :]
    b_all, c_all = silu(b_col), silu(c_col)
    base = 3 * js * LANES
    misc = got[:, 0, base + 2 * LANES : base + 3 * LANES]
    misc_parts = exact(misc)
    log_parts = exact(early[0, ROW_LOG : ROW_LOG + 8, :])
    step_parts = exact(early[0, ROW_STEP : ROW_STEP + 8, :])
    sum_b = [jnp.zeros((ns, LANES), F32) for _ in range(3)]
    sum_c = [jnp.zeros((ns, LANES), F32) for _ in range(3)]
    for j in range(js):
        at = slice(j * LANES, (j + 1) * LANES)
        fall = jnp.exp(mm(misc_parts, picker(32, j)))
        falls = jnp.exp(mm(log_parts, picker(0, j)))
        steps = mm(step_parts, picker(0, j))
        seq = [moved[j, ns + r : ns + r + 1, 0:LANES] for r in range(3)] + [
            early[0, ROW_X + s * js + j : ROW_X + s * js + j + 1, :] for s in range(3)
        ]
        gain = skip[j : j + 1, :] * first
        state = moved[j, 0:ns, 0:LANES]
        for s in range(3):
            dy = early[0, ROW_DY + s * js + j : ROW_DY + s * js + j + 1, :]
            pre = sum(convx[i, j : j + 1, :] * seq[s + i] for i in range(4))
            sg = sigmoid(pre)
            x_conv = pre * sg
            x_hat = steps[s : s + 1] * x_conv
            state = falls[s : s + 1] * state + x_hat * b_all[:, s : s + 1]
            a = adj[s, :, at]
            rows[j : j + 1, s * LANES : (s + 1) * LANES] = (
                jnp.sum(state * c_all[:, s : s + 1], axis=0, keepdims=True) + gain * x_conv
            )
            grad = steps[s : s + 1] * jnp.sum(a * b_all[:, s : s + 1], axis=0, keepdims=True)
            rows[j : j + 1, (3 + s) * LANES : (4 + s) * LANES] = (
                sg * (1.0 + pre * (1.0 - sg)) * (grad + gain * dy)
            )
            sum_c[s] = sum_c[s] + dy * state
            sum_b[s] = sum_b[s] + x_hat * a
        for p in range(count):
            msg[p, :, at] = state
            state = fall[p : p + 1] * state + got[p, :, at]
            msg[p, :, (js + j) * LANES : (js + j + 1) * LANES] = aft[p, :, at]
    lane = iota((ns, LANES), 1)
    back = jnp.zeros((ns, LANES), F32)
    for which, (total, column) in enumerate(((sum_b, b_col), (sum_c, c_col))):
        grads = [
            jnp.sum(total[s], axis=1, keepdims=True) * silu_slope(column[:, s : s + 1])
            for s in range(3)
        ]
        for m in range(3):
            tail = sum(grads[s] * column[:, 8 + m - s : 9 + m - s] for s in range(m + 1))
            back = jnp.where(lane == 3 * which + m, tail, back)
    pfall = jnp.exp(halves(misc[:, 0:1], misc[:, 1:2], (count, LANES)))
    injected[...] = jnp.zeros(injected.shape, F32)
    for g in range(js):
        holder = lax.div(scal[g] - 1, span)
        mark = got[holder, 0:1, base + 2 * LANES : base + 3 * LANES]
        reach = jnp.exp(
            halves(mark[:, 64 + 2 * g : 65 + 2 * g], mark[:, 65 + 2 * g : 66 + 2 * g], (1, LANES))
        )
        grad = moved[g, 0:ns, LANES : 2 * LANES]
        injected[holder] = injected[holder] + reach * grad
        for p in range(count):
            msg[p, :, (2 * js + g) * LANES : (2 * js + g + 1) * LANES] = grad
    a = jnp.zeros((ns, LANES), F32)
    for p in reversed(range(count)):
        msg[p, :, base + LANES : base + 2 * LANES] = a
        a = pfall[p : p + 1] * a + got[p, :, base + LANES : base + 2 * LANES] + injected[p]
    for p in range(count):
        msg[p, :, base : base + LANES] = pst[p]
        msg[p, :, base + 2 * LANES : base + 8 * LANES] = rows[...]
        msg[p, :, base + 8 * LANES : base + 9 * LANES] = back


def tail_grads(lead, taps):
    return [sum(lead[s] * taps[m - s] for s in range(m + 1)) for m in range(3)]


def final_kernel(
    scal, px, pbc, pstep, plogs, pdy, bx, bbc, bstep, blogs, bdy, rim, convx, convbc, skip, got,
    by, bgx, last, py, pgx, gbc, rims, forks,
    xs, xt, ds, dys, bcs, pxs, pbcs, wexp, wrow, pwrow, ys, rows, dxh, dbs,
):
    row, col, length = scal[17], scal[18], scal[16]
    n, js = bx.shape[0], bx.shape[1]
    span = px.shape[0]
    conv_branch(bx, rim, convx, xs, xt, ds)
    is_first = row == 0

    def fill(c, _):
        pos = row * n + c * 16 + iota((16, js, LANES), 0)
        dead = (pos >= length) | (pos < 3)
        dys[pl.ds(pl.multiple_of(c * 16 * js, 16 * js), 16 * js), :] = jnp.where(
            dead, 0.0, bdy[pl.ds(c * 16, 16)].astype(F32)
        ).reshape(16 * js, LANES)
        return 0

    lax.fori_loop(0, n // 16, fill, 0)
    base = 3 * js * LANES
    sums = got[0:js, base + 2 * LANES : base + 8 * LANES]
    for p in range(1, STATE // js):
        sums = sums + got[p * js : (p + 1) * js, base + 2 * LANES : base + 8 * LANES]
    rows[...] = sums
    taps = [convbc[i : i + 1, :] for i in range(4)]
    bc = silu(conv_rows(bbc[...], bc_halo(rim, 19), taps, bcs))
    b, c = bc[:, :STATE], bc[:, STATE:]
    b_l, c_l = left(b), left(c)
    scores = mm_nt(c_l, right_nt(b))
    scores_t = mm_nt(b_l, right_nt(c))
    run = running_sum(blogs[...])
    wrow[...] = run
    parts = exact(branch_table(bstep[...], run))
    causal = iota((n, n), 0) >= iota((n, n), 1)
    causal_t = iota((n, n), 0) <= iota((n, n), 1)
    low = iota((n, LANES), 1) < HEAD_DIM
    xs[n * js : (n + 8) * js, :] = jnp.zeros((8 * js, LANES), F32)

    def head_pair(j, _):
        at = pl.ds(j, n, stride=js)
        steps = mm(parts, picker(0, j))
        runs = mm(parts, picker(32, j))
        x_conv = xt[at, :]
        dy = dys[at, :]
        gain = skip[pl.ds(j, 1), :]
        x_hat = x_conv * steps
        x_hi, x_lo = split2(x_hat)
        dy_b = dy.astype(BF16)
        zero = jnp.zeros_like(dy_b)
        mix, mix_t = [], []
        for k in range(2):
            down = jnp.broadcast_to(runs[:, k * HEAD_DIM : k * HEAD_DIM + 1], (n, n))
            along = wrow[pl.ds(2 * j + k, 1), :]
            mix.append(split2(jnp.exp(jnp.where(causal, down - along, -1e30)) * scores))
            mix_t.append(split2(jnp.exp(jnp.where(causal_t, along - down, -1e30)) * scores_t))
        x_blk = [jnp.where(low, x_hi, zero), jnp.where(low, zero, x_hi)]
        x_rest = [jnp.where(low, x_lo, zero), jnp.where(low, zero, x_lo)]
        d_blk = [jnp.where(low, dy_b, zero), jnp.where(low, zero, dy_b)]
        y = mm(
            jnp.concatenate([mix[0][0], mix[1][0], mix[0][0], mix[1][0], mix[0][1], mix[1][1]], 1),
            jnp.concatenate(x_blk + x_rest + x_blk, 0),
        )
        y = y + jnp.exp(runs) * mm(c_l, right(got[:, block(j)]))
        ys[at, :] = y + gain * x_conv
        g = mm(
            jnp.concatenate([mix_t[0][0], mix_t[1][0], mix_t[0][1], mix_t[1][1]], 1),
            jnp.concatenate(d_blk + d_blk, 0),
        )
        g = g + jnp.exp(runs[n - 1 : n, :] - runs) * mm(b_l, right(got[:, block(js + j)]))
        xs[at, :] = (steps * g + gain * dy) * ds[at, :]
        return 0

    lax.fori_loop(0, js, head_pair, 0)

    @pl.when(is_first)
    def _():
        for s in range(3):
            ys[s * js : (s + 1) * js, :] = rows[:, s * LANES : (s + 1) * LANES]
            xs[s * js : (s + 1) * js, :] = rows[:, (3 + s) * LANES : (4 + s) * LANES]

    def finish(c, _):
        at = pl.multiple_of(c * 16 * js, 16 * js)
        pos = row * n + c * 16 + iota((16, js, LANES), 0)
        y = ys[pl.ds(at, 16 * js), :].reshape(16, js, LANES)
        by[pl.ds(c * 16, 16)] = jnp.where(pos < length, y, 0.0).astype(BF16)
        g = jnp.zeros((16, js, LANES), F32)
        for i in range(4):
            g = g + convx[i][None] * xs[pl.ds(at + (3 - i) * js, 16 * js), :].reshape(
                16, js, LANES
            )
        bgx[pl.ds(c * 16, 16)] = g.astype(BF16)
        return 0

    lax.fori_loop(0, n // 16, finish, 0)
    for m in range(3):
        at = n - 3 + m
        last[m] = sum(
            convx[i] * xs[(at + 3 - i) * js : (at + 4 - i) * js, :] for i in range(4)
        )
    taps_x = [convx[i] for i in range(4)]
    for m, g in enumerate(tail_grads([xs[s * js : (s + 1) * js, :] for s in range(3)], taps_x)):
        rims[m, 0:js, :] = g
    fork_lead = [rows[:, (3 + s) * LANES : (4 + s) * LANES] for s in range(3)]
    for m, g in enumerate(tail_grads(fork_lead, taps_x)):
        forks[m] = g

    own = [convx[i, pl.ds(col, 1), :] for i in range(4)]
    gain = skip[pl.ds(col, 1), :]
    x_pre = conv_rows(px[...], [rim[r, 16:17, :] for r in range(3)], own, pxs)
    bc_pre = conv_rows(pbc[...], bc_halo(rim, 17), taps, pbcs)
    x_p = silu(x_pre)
    bc_p = silu(bc_pre)
    b_p, c_p = bc_p[:, :STATE], bc_p[:, STATE:]
    b_l, c_l = left(b_p), left(c_p)
    scores = mm_nt(c_l, right_nt(b_p))
    scores_t = mm_nt(b_l, right_nt(c_p))
    prun = running_sum(plogs[...])
    ptable = prompt_table(pstep[...], prun)
    runs = halves(ptable[:, 0:1], ptable[:, 1:2], (span, LANES))
    steps = halves(ptable[:, 2:3], ptable[:, 3:4], (span, LANES))
    wexp[...] = runs
    x_hat = x_p * steps
    x_hi, x_lo = split2(x_hat)
    dy_b = pdy[...]
    dy = dy_b.astype(F32)
    low = iota((span, LANES), 1) < HEAD_DIM
    zero = jnp.zeros_like(x_hi)
    causal = iota((span, span), 0) >= iota((span, span), 1)
    causal_t = iota((span, span), 0) <= iota((span, span), 1)
    y = jnp.exp(runs) * mm(c_l, right(got[:, base : base + LANES])) + gain * x_p
    after = right(got[:, base + LANES : base + 2 * LANES])
    g = jnp.exp(runs[span - 1 : span, :] - runs) * mm(b_l, after)
    d_s = jnp.zeros((span, span), F32)
    d_st = jnp.zeros((span, span), F32)
    for k in range(2):
        keep = low if k == 0 else jnp.logical_not(low)
        xk_hi, xk_lo = jnp.where(keep, x_hi, zero), jnp.where(keep, x_lo, zero)
        dk = jnp.where(keep, dy_b, zero)
        down = jnp.broadcast_to(ptable[:, k : k + 1], (span, span))
        along = prun[k : k + 1, :]
        decay = jnp.exp(jnp.where(causal, down - along, -1e30))
        decay_t = jnp.exp(jnp.where(causal_t, along - down, -1e30))
        m_hi, m_lo = split2(decay * scores)
        t_hi, t_lo = split2(decay_t * scores_t)
        y = y + mm(
            jnp.concatenate([m_hi, m_hi, m_lo], 1), jnp.concatenate([xk_hi, xk_lo, xk_hi], 0)
        )
        g = g + mm(jnp.concatenate([t_hi, t_lo], 1), jnp.concatenate([dk, dk], 0))
        d_two = jnp.concatenate([dk, dk], 1)
        x_two = jnp.concatenate([x_hi, x_lo], 1)
        d_s = d_s + decay * mm_nt(d_two, x_two)
        d_st = d_st + decay_t * mm_nt(x_two, d_two)
    py[...] = y.astype(BF16)
    d_c = mm(left(d_s), right(b_p)) + mm_nt(
        left(jnp.exp(runs) * dy), right_nt(got[:, base : base + LANES])
    )
    d_b = mm(left(d_st), right(c_p)) + mm_nt(
        left(jnp.exp(runs[span - 1 : span, :] - runs) * x_hat),
        right_nt(got[:, base + LANES : base + 2 * LANES]),
    )
    dxh[...] = g
    dbs[...] = d_b
    pxs[0:span, :] = x_hat

    def fork(q, _):
        where = scal[q] - 1 - row * span

        @pl.when((where >= 0) & (where < span))
        def _():
            gap = wexp[pl.ds(where, 1), :] - wexp[...]
            u = jnp.exp(jnp.where(iota((span, LANES), 0) <= where, gap, -1e30))
            grad = got[:, block(2 * js + q)]
            dxh[...] += u * mm(b_l, right(grad))
            dbs[...] += mm_nt(left(u * pxs[0:span, :]), right_nt(grad))

        return 0

    lax.fori_loop(0, js, fork, 0)
    pre_g = (steps * dxh[...] + gain * dy) * silu_slope(x_pre)
    pxs[0:span, :] = pre_g
    pxs[span : span + 8, :] = jnp.zeros((8, LANES), F32)
    pgx[...] = sum(own[i] * pxs[3 - i : 3 - i + span, :] for i in range(4))
    for m, v in enumerate(tail_grads([pxs[s : s + 1, :] for s in range(3)], own)):
        rims[m, 16:17, :] = v
    pbcs[0:span, :] = jnp.concatenate([dbs[...], d_c], axis=1) * silu_slope(bc_pre)
    pbcs[span : span + 8, :] = jnp.zeros((8, 2 * STATE), F32)
    grad = sum(taps[i] * pbcs[3 - i : 3 - i + span, :] for i in range(4))
    for m, v in enumerate(tail_grads([pbcs[s : s + 1, :] for s in range(3)], taps)):
        rims[m, 17:18, :] = v[:, :STATE]
        rims[m, 18:19, :] = v[:, STATE:]
    spot = iota((span, LANES), 0) - (scal[20] - 3 - row * span)
    lane = iota((span, LANES), 1)
    tails = exact(got[:, base + 8 * LANES : base + 9 * LANES])
    into = []
    for half in range(2):
        hit = ((spot >= 0) & (spot < 3) & (lane == spot + 3 * half)).astype(F32).astype(BF16)
        into.append(mm_nt(jnp.concatenate([hit, hit, hit], 1), tails))
    gbc[...] = grad + jnp.concatenate(into, axis=1)


def finish_kernel(scal, pgx, got, out_x, out_bc):
    row = scal[17]
    span = pgx.shape[0]
    peers = got.shape[0]
    width = got.shape[1] - 3
    total = got[0]
    for p in range(1, peers):
        total = total + got[p]
    rows = width // 2
    out_bc[...] = total[0:width].reshape(rows, 2 * STATE).astype(BF16)


def specs(n):
    return [pl.BlockSpec(memory_space=pltpu.SMEM)] + [pl.BlockSpec(memory_space=pltpu.VMEM)] * (
        n - 1
    )


def call(kernel, args, outs, scratch, flops=10**8):
    return pl.pallas_call(
        kernel,
        out_shape=[jax.ShapeDtypeStruct(s, d) for s, d in outs],
        in_specs=specs(len(args)),
        out_specs=[pl.BlockSpec(memory_space=pltpu.VMEM)] * len(outs),
        scratch_shapes=[pltpu.VMEM(s, F32) for s in scratch],
        compiler_params=pltpu.CompilerParams(vmem_limit_bytes=VMEM_LIMIT),
    )(*args)


def shards(
    prompt_x,
    prompt_bc,
    prompt_dt,
    branch_x,
    branch_bc,
    branch_dt,
    conv_x,
    conv_bc,
    a_log,
    dt_bias,
    d_skip,
    lengths,
    forks,
    holder,
    prompt_dy,
    branch_dy,
):
    row = lax.axis_index("prefix")
    col = lax.axis_index("branch")
    count = lax.axis_size("prefix")
    js = lax.axis_size("branch")
    span = prompt_x.shape[0]
    n = branch_x.shape[1]
    heads = 2 * js
    ns = STATE // count

    placed = jnp.sum((holder[None, :] < holder[:, None]).astype(jnp.int32), axis=1)
    owners = (placed[None, :] == jnp.arange(js, dtype=jnp.int32)[:, None]).astype(jnp.int32)
    group_fork = jnp.sum(owners * forks[None, :], axis=1)
    group_length = jnp.sum(owners * lengths[None, :], axis=1)
    mine = (jnp.arange(js, dtype=jnp.int32) == col).astype(jnp.int32)
    own_length = jnp.sum(mine * group_length)
    own_fork = jnp.sum(mine * group_fork)
    scal = jnp.concatenate(
        [
            group_fork,
            jnp.stack(
                [
                    own_length,
                    row.astype(jnp.int32),
                    col.astype(jnp.int32),
                    jnp.int32(span),
                    own_fork,
                ]
            ),
        ]
    )

    px = prompt_x.reshape(span, LANES)
    pbc = prompt_bc.reshape(span, 2 * STATE)
    pdy = prompt_dy.reshape(span, LANES)
    bx = branch_x.reshape(n, js, LANES)
    bbc = branch_bc.reshape(n, 2 * STATE)
    bdy = branch_dy.reshape(n, js, LANES)
    convx = conv_x.reshape(4, js, LANES)
    convbc = conv_bc.reshape(4, 2 * STATE)
    skip = jnp.repeat(d_skip.reshape(js, 2), HEAD_DIM, axis=1)

    rate = jnp.exp(a_log.reshape(heads, 1))
    step = jax.nn.softplus(branch_dt.reshape(heads, n) + dt_bias.reshape(heads, 1))
    logs = -rate * step
    null = (row == 0) & (jnp.arange(n) < 3)[None, :]
    bstep = jnp.where(null, 0.0, step)
    blogs = jnp.where(null, 0.0, logs)
    rate_own = jnp.exp(lax.dynamic_slice_in_dim(a_log.reshape(js, 2), col, 1, 0)).reshape(2, 1)
    bias_own = lax.dynamic_slice_in_dim(dt_bias.reshape(js, 2), col, 1, 0).reshape(2, 1)
    pstep = jax.nn.softplus(prompt_dt.reshape(2, span) + bias_own)
    plogs = -rate_own * pstep

    def wide(a):
        return a.astype(F32).reshape(3, -1, LANES)

    packed = jnp.concatenate(
        [wide(bx[-3:]), wide(px[-3:]), wide(pbc[-3:]), wide(bbc[-3:])], axis=1
    )
    rim = lax.ppermute(packed, "prefix", [(i, i + 1) for i in range(count - 1)])

    tail_pos = (
        group_fork[:, None] - 3 + jnp.arange(3, dtype=jnp.int32)[None, :] - row * span
    ).reshape(-1)
    pick = (tail_pos[:, None] == jnp.arange(span, dtype=jnp.int32)[None, :]).astype(BF16)
    own_pos = own_fork - 3 + jnp.arange(3, dtype=jnp.int32) - row * span
    own_pick = (own_pos[:, None] == jnp.arange(span, dtype=jnp.int32)[None, :]).astype(BF16)
    tail_x = jnp.dot(pick, px, preferred_element_type=F32)
    tail_bc = jnp.dot(own_pick, pbc, preferred_element_type=F32).reshape(6, LANES)
    live3 = (jnp.arange(3) < own_length).astype(F32)[:, None, None]
    early = jnp.concatenate(
        [
            tail_x,
            tail_bc,
            bx[:3].astype(F32).reshape(3 * js, LANES),
            (bdy[:3].astype(F32) * live3).reshape(3 * js, LANES),
            bbc[:3].astype(F32).reshape(6, LANES),
            jnp.zeros((4, LANES), F32),
            jnp.pad(step[:, :3].T, ((0, 5), (0, LANES - heads))),
            jnp.pad(logs[:, :3].T, ((0, 5), (0, LANES - heads))),
        ],
        axis=0,
    )
    early = lax.all_gather(early, "prefix")

    locals_in = [scal, px, pbc, pstep, plogs, pdy, bx, bbc, bstep, blogs, bdy, rim, convx, convbc]
    big = (n * js, LANES)
    with jax.named_scope("local"):
        (sent,) = call(
            local_kernel,
            locals_in,
            [((STATE, (3 * js + 3) * LANES), F32)],
            [
                ((n + 8) * js, LANES), big, big, (n + 8, 2 * STATE), (span + 8, LANES),
                (span + 8, 2 * STATE), (span, LANES), (span, LANES),
            ],
        )
    got = lax.all_to_all(sent.reshape(count, ns, -1), "prefix", 0, 0, tiled=True)
    with jax.named_scope("slices"):
        msg, aft, adj, pst, cols = call(
            slice_kernel,
            [scal, got, early, convbc],
            [
                ((js, ns + 8, 2 * LANES), F32),
                ((count, ns, js * LANES), F32),
                ((3, ns, js * LANES), F32),
                ((count, ns, LANES), F32),
                ((2 * ns, LANES), F32),
            ],
            [(LANES, LANES), (2 * STATE, LANES)],
        )
    moved = lax.all_to_all(msg, "branch", 0, 0, tiled=True)
    with jax.named_scope("chains"):
        (msg3,) = call(
            chain_kernel,
            [scal, got, early, moved, aft, adj, pst, cols, convx, skip],
            [((count, ns, (3 * js + 9) * LANES), F32)],
            [(js, 6 * LANES), (count, ns, LANES)],
        )
    got3 = lax.all_to_all(msg3, "prefix", 0, 0, tiled=True).reshape(STATE, -1)
    with jax.named_scope("final"):
        by, bgx, last, py, pgx, gbc, rims, fork_grads = call(
            final_kernel,
            locals_in + [skip, got3],
            [
                ((n, js, LANES), BF16),
                ((n, js, LANES), BF16),
                ((3, js, LANES), F32),
                ((span, LANES), BF16),
                ((span, LANES), F32),
                ((span, 2 * STATE), F32),
                ((3, js + 3, LANES), F32),
                ((3, js, LANES), F32),
            ],
            [
                ((n + 8) * js, LANES), big, big, big, (n + 8, 2 * STATE), (span + 8, LANES),
                (span + 8, 2 * STATE), (span, LANES), (heads, n), (8, LANES), big,
                (js, 6 * LANES), (span, LANES), (span, STATE),
            ],
        )
    back = lax.ppermute(rims, "prefix", [(i, i - 1) for i in range(1, count)])
    bgx = bgx.at[-3:].set((last + back[:, :js]).astype(BF16))
    pgx = pgx.at[-3:].add(back[:, js])
    gbc = gbc.at[-3:].add(back[:, js + 1 : js + 3].reshape(3, 2 * STATE))
    rows = span // js
    out_msg = jnp.concatenate(
        [gbc.reshape(js, 2 * rows, LANES), jnp.moveaxis(fork_grads, 1, 0)], axis=1
    )
    end = lax.all_to_all(out_msg, "branch", 0, 0, tiled=True)
    prompt_gbc = jnp.sum(end[:, : 2 * rows], axis=0).reshape(rows, 1, 2 * STATE).astype(BF16)
    tails = end[:, 2 * rows :].reshape(3 * js, LANES)
    into = jnp.dot(pick.T.astype(F32), tails, precision=lax.Precision.HIGHEST)
    prompt_gx = (pgx + into).astype(BF16)
    return (
        py.reshape(prompt_x.shape),
        by.reshape(branch_x.shape),
        prompt_gx.reshape(prompt_x.shape),
        bgx.reshape(branch_x.shape),
        prompt_gbc,
    )


def solution(mesh):
    return jax.shard_map(
        shards,
        mesh=mesh,
        in_specs=(
            P("prefix", "branch", "tensor", None),
            P("prefix", "tensor", None),
            P("branch", "tensor", None, "prefix"),
            P("branch", "prefix", None, "tensor", None),
            P("branch", "prefix", "tensor", None),
            P("branch", None, "tensor", None, "prefix"),
            P(None, None, "tensor", None),
            P(None, "tensor", None),
            P(None, "tensor", None),
            P(None, "tensor", None),
            P(None, "tensor", None),
            P(),
            P(),
            P(),
            P("prefix", "branch", "tensor", None),
            P("branch", "prefix", None, "tensor", None),
        ),
        out_specs=(
            P("prefix", "branch", "tensor", None),
            P("branch", "prefix", None, "tensor", None),
            P("prefix", "branch", "tensor", None),
            P("branch", "prefix", None, "tensor", None),
            P(("prefix", "branch"), "tensor", None),
        ),
        check_vma=False,
    )
```

```python
import functools

import jax
import jax.numpy as jnp
from jax import lax
from jax.experimental import pallas as pl
from jax.experimental.pallas import tpu as pltpu
from jax.sharding import PartitionSpec as P

HEAD_DIM = 64
STATE = 128
LANES = 128

F32 = jnp.float32
BF16 = jnp.bfloat16

TAIL_X = 0
ROW_X = 3
ROW_DY = 6
ROW_BC = 9
ROW_STEP = 10
EARLY = 11

VMEM_LIMIT = 56 * 1024 * 1024


def split2(a):
    hi = a.astype(BF16)
    return hi, (a - hi.astype(F32)).astype(BF16)


def split3(a):
    hi = a.astype(BF16)
    rest = a - hi.astype(F32)
    mid = rest.astype(BF16)
    return hi, mid, (rest - mid.astype(F32)).astype(BF16)


def mm(a, b):
    return lax.dot_general(a, b, (((1,), (0,)), ((), ())), preferred_element_type=F32)


def mm_nt(a, b):
    return lax.dot_general(a, b, (((1,), (1,)), ((), ())), preferred_element_type=F32)


def left(a):
    hi, lo = split2(a)
    return jnp.concatenate([hi, hi, lo], axis=1)


def right(b):
    hi, lo = split2(b)
    return jnp.concatenate([hi, lo, hi], axis=0)


def right_nt(b):
    hi, lo = split2(b)
    return jnp.concatenate([hi, lo, hi], axis=1)


def exact(a):
    return jnp.concatenate(split3(a), axis=1)


def iota(shape, dim):
    return lax.broadcasted_iota(jnp.int32, shape, dim)


def picker(base, j):
    one = (iota((LANES, LANES), 0) == base + 2 * j + iota((LANES, LANES), 1) // HEAD_DIM).astype(
        F32
    ).astype(BF16)
    return jnp.concatenate([one, one, one], axis=0)


def running_sum(logs):
    size = logs.shape[1]
    upper = (iota((size, size), 0) <= iota((size, size), 1)).astype(F32).astype(BF16)
    return mm(exact(logs), jnp.concatenate([upper, upper, upper], axis=0))


def block(j):
    return pl.ds(pl.multiple_of(j * LANES, LANES), LANES)


def sigmoid(x):
    return 1.0 / (1.0 + jnp.exp(-x))


def head_column(pair, heads):
    shape = (heads, heads // 2)
    r = iota(shape, 0)
    both = jnp.where(r % 2 == 0, pair[0:1], pair[1:2])
    return jnp.sum(jnp.where(iota(shape, 1) == r // 2, both, 0.0), axis=1, keepdims=True)


def softplus(x):
    return jnp.maximum(x, 0.0) + jnp.log1p(jnp.exp(-jnp.abs(x)))


def setup_kernel(
    forks, lengths, holder, bx, px, pbc, bbc, alog, bias, gain, bdt, pdt,
    scal, rim, step, logs, pstep, plogs, skip,
):
    row, col = lax.axis_index("prefix"), lax.axis_index("branch")
    js = bx.shape[1]

    def place(b, _):
        group = lax.fori_loop(
            0, js, lambda c, t: t + (holder[c] < holder[b]).astype(jnp.int32), jnp.int32(0),
            unroll=16,
        )
        scal[group] = forks[b]

        @pl.when(group == col)
        def _():
            scal[16] = lengths[b]
            scal[20] = forks[b]

        return 0

    lax.fori_loop(0, js, place, 0)
    scal[17] = row
    scal[18] = col
    scal[19] = pdt.shape[1]
    last = bx.shape[0] - 3
    xl = px[...].astype(F32)
    bcl = pbc[...].astype(F32)
    bbl = bbc[...].astype(F32)
    for r in range(3):
        rim[r, 0:js, :] = bx[last + r].astype(F32)
        at = slice(last + r, last + r + 1)
        rim[r, js : js + 1, :] = xl[at]
        rim[r, js + 1 : js + 2, :] = bcl[at, :STATE]
        rim[r, js + 2 : js + 3, :] = bcl[at, STATE:]
        rim[r, js + 3 : js + 4, :] = bbl[at, :STATE]
        rim[r, js + 4 : js + 5, :] = bbl[at, STATE:]
    heads = bdt.shape[0]
    s = softplus(bdt[...] + head_column(bias[...], heads))
    step[...] = s
    logs[...] = -jnp.exp(head_column(alog[...], heads)) * s
    own = iota((2, js), 1) == col
    own_bias = jnp.sum(jnp.where(own, bias[...], 0.0), axis=1, keepdims=True)
    own_rate = jnp.exp(jnp.sum(jnp.where(own, alog[...], 0.0), axis=1, keepdims=True))
    s = softplus(pdt[...] + own_bias)
    pstep[...] = s
    plogs[...] = -own_rate * s
    diag = iota((js, js), 0) == iota((js, js), 1)
    first = jnp.sum(jnp.where(diag, gain[0:1], 0.0), axis=1, keepdims=True)
    second = jnp.sum(jnp.where(diag, gain[1:2], 0.0), axis=1, keepdims=True)
    skip[...] = halves(first, second, (js, LANES))


def conv_branch(bx, rim, convx, xs, xt, ds):
    js = bx.shape[1]
    for r in range(3):
        xs[(5 + r) * js : (6 + r) * js, :] = rim[r, 0:js, :]

    def fill(c, _):
        xs[pl.ds(pl.multiple_of(8 * js + c * 16 * js, 16 * js), 16 * js), :] = (
            bx[pl.ds(c * 16, 16)].astype(F32).reshape(16 * js, LANES)
        )
        return 0

    lax.fori_loop(0, bx.shape[0] // 16, fill, 0)

    def one(c, _):
        pre = jnp.zeros((16, js, LANES), F32)
        for i in range(4):
            start = pl.multiple_of((5 + i) * js + c * 16 * js, js)
            pre = pre + convx[i][None] * xs[pl.ds(start, 16 * js), :].reshape(16, js, LANES)
        sg = sigmoid(pre)
        at = pl.ds(pl.multiple_of(c * 16 * js, 16 * js), 16 * js)
        xt[at, :] = (pre * sg).reshape(16 * js, LANES)
        if ds is not None:
            ds[at, :] = (sg * (1.0 + pre * (1.0 - sg))).reshape(16 * js, LANES)
        return 0

    lax.fori_loop(0, bx.shape[0] // 16, one, 0)


def conv_rows(raw, halo_rows, taps, scratch):
    n = raw.shape[0]
    scratch[8 : 8 + n, :] = raw.astype(F32)
    for r in range(3):
        scratch[5 + r : 6 + r, :] = halo_rows[r]
    pre = jnp.zeros(raw.shape, F32)
    for i in range(4):
        pre = pre + taps[i] * scratch[5 + i : 5 + i + n, :]
    return pre


def bc_halo(rim, first):
    return [
        jnp.concatenate([rim[r, first : first + 1, :], rim[r, first + 1 : first + 2, :]], axis=1)
        for r in range(3)
    ]


def silu(x):
    return x * sigmoid(x)


def silu_slope(x):
    sg = sigmoid(x)
    return sg * (1.0 + x * (1.0 - sg))


def without_first(row, values):
    return jnp.where((row == 0) & (iota(values.shape, 1) < 3), 0.0, values)


def branch_table(step, run):
    return jnp.concatenate([step, run, jnp.zeros((64, LANES), F32)], axis=0).T


def prompt_table(step, run):
    n = step.shape[1]
    r = iota((LANES, n), 0)
    runs = jnp.where(r % 2 == 0, run[0:1], run[1:2])
    steps = jnp.where(r % 2 == 0, step[0:1], step[1:2])
    return jnp.where((r == 2) | (r == 3), steps, runs).T


def halves(first, second, shape):
    return jnp.where(iota(shape, 1) < HEAD_DIM, first, second)


def part(h, row):
    half = STATE // 2
    core = lax.rem(row, 2)
    return pl.ds(pl.multiple_of((core if h == 0 else 1 - core) * half, half), half)


def live_dy(row, length, bdy, dys):
    n, js = bdy.shape[0], bdy.shape[1]

    def fill(c, _):
        pos = row * n + c * 16 + iota((16, js, LANES), 0)
        dead = (pos >= length) | (pos < 3)
        dys[pl.ds(pl.multiple_of(c * 16 * js, 16 * js), 16 * js), :] = jnp.where(
            dead, 0.0, bdy[pl.ds(c * 16, 16)].astype(F32)
        ).reshape(16 * js, LANES)
        return 0

    lax.fori_loop(0, n // 16, fill, 0)


def lead_kernel(
    scal, px, pbc, pstep, plogs, pdy, bx, bbc, bstep, blogs, bdy, rim, convx, convbc,
    mine, other, dys, bcs, pxs, pbcs, wexp, tab, early, out,
):
    row, col, length = scal[17], scal[18], scal[16]
    n, js = bdy.shape[0], bdy.shape[1]
    span = px.shape[0]
    live_dy(row, length, bdy, dys)
    taps = [convbc[i : i + 1, :] for i in range(4)]
    bc = silu(conv_rows(bbc[...], bc_halo(rim, 19), taps, bcs))
    c_t = left(bc[:, STATE:].T)
    step, log = without_first(row, bstep[...]), without_first(row, blogs[...])
    table = branch_table(step, running_sum(log))
    parts = exact(table)

    def head_pair(j, _):
        at = pl.ds(j, n, stride=js)
        runs = mm(parts, picker(32, j))
        out[:, block(j)] = mm(c_t, right(dys[at, :] * jnp.exp(runs)))
        return 0

    lax.fori_loop(0, js, head_pair, 0, unroll=4)

    own = [convx[i, pl.ds(col, 1), :] for i in range(4)]
    x_p = silu(conv_rows(px[...], [rim[r, 16:17, :] for r in range(3)], own, pxs))
    bc_p = silu(conv_rows(pbc[...], bc_halo(rim, 17), taps, pbcs))
    b_pt = left(bc_p[:, :STATE].T)
    c_pt = left(bc_p[:, STATE:].T)
    ptable = prompt_table(pstep[...], running_sum(plogs[...]))
    tab[...] = ptable
    runs = halves(ptable[:, 0:1], ptable[:, 1:2], (span, LANES))
    steps = halves(ptable[:, 2:3], ptable[:, 3:4], (span, LANES))
    wexp[...] = runs
    x_hat = x_p * steps
    base = 2 * js * LANES
    out[:, base : base + LANES] = mm(b_pt, right(x_hat * jnp.exp(runs[span - 1 : span, :] - runs)))
    out[:, base + LANES : base + 2 * LANES] = mm(
        c_pt, right(pdy[...].astype(F32) * jnp.exp(runs))
    )
    lane = iota((1, LANES), 1)
    pxs[0:span, :] = x_hat

    def fork(g, acc):
        where = scal[g] - 1 - row * span
        inside = (where >= 0) & (where < span)

        @pl.when(inside)
        def _():
            w = wexp[...]
            gap = wexp[pl.ds(where, 1), :] - w
            upto = iota((span, LANES), 0) <= where
            u = jnp.exp(jnp.where(upto, gap, -1e30)) * pxs[0:span, :]
            out[:, block(js + g)] = mm(b_pt, right(u))

        @pl.when(jnp.logical_not(inside))
        def _():
            out[:, block(js + g)] = jnp.zeros((STATE, LANES), F32)

        safe = jnp.clip(where, 0, span - 1)
        return jnp.where(lane // 2 == 32 + g, tab[pl.ds(safe, 1), :], acc)

    marks = lax.fori_loop(0, js, fork, jnp.zeros((1, LANES), F32))
    misc = jnp.where(lane < 2, ptable[span - 1 : span, :], marks)
    misc = jnp.where((lane >= 32) & (lane < 64), table[n - 1 : n, :], misc)
    out[:, base + 2 * LANES : base + 3 * LANES] = jnp.broadcast_to(misc, (STATE, LANES))

    first = (row == 0).astype(F32)
    lane2 = iota((js, span), 1)
    spot = jnp.zeros((js, span), jnp.int32)
    for g in range(js):
        spot = jnp.where(iota((js, span), 0) == g, scal[g] - 3 - row * span, spot)
    hits = jnp.concatenate([(lane2 == spot + r).astype(F32).astype(BF16) for r in range(3)], 0)
    tails = mm(hits, px[...])
    own_spot = scal[20] - 3 - row * span + iota((js, span), 0)
    hit = ((lane2 == own_spot) & (iota((js, span), 0) < 3)).astype(F32).astype(BF16)
    tail_bc = mm(hit, pbc[...])
    raw_bc = bbc[0:16].astype(F32) * first
    raw = jnp.concatenate([bstep[...], blogs[...], jnp.zeros((64, LANES), F32)], axis=0).T
    early[...] = jnp.zeros(early.shape, F32)
    for r in range(3):
        early[:, (TAIL_X + r) * LANES : (TAIL_X + r + 1) * LANES] = tails[r * js : (r + 1) * js]
        early[:, (ROW_X + r) * LANES : (ROW_X + r + 1) * LANES] = bx[r].astype(F32) * first
        early[:, (ROW_DY + r) * LANES : (ROW_DY + r + 1) * LANES] = bdy[r].astype(F32) * (
            first * (r < length).astype(F32)
        )
        for half in range(2):
            at = slice(half * STATE, (half + 1) * STATE)
            early[2 * r + half : 2 * r + half + 1, ROW_BC * LANES : (ROW_BC + 1) * LANES] = (
                tail_bc[r : r + 1, at]
            )
            early[6 + 2 * r + half : 7 + 2 * r + half, ROW_BC * LANES : (ROW_BC + 1) * LANES] = (
                raw_bc[r : r + 1, at]
            )
    early[0:8, ROW_STEP * LANES : (ROW_STEP + 1) * LANES] = raw[0:8] * first
    for h, half_out in enumerate((mine, other)):
        half_out[:, : base + 3 * LANES] = out[part(h, row), :]
        for q in range(half_out.shape[0] // js):
            half_out[q * js : (q + 1) * js, base + 3 * LANES :] = early[...]


def pair_falls(even, odd, column):
    both = jnp.concatenate([even[0:1, column], odd[0:1, column], jnp.zeros((6, LANES), F32)], 0)
    return both, exact(both)


def in_odd(scal, g, span):
    where = scal[g] - 1 - lax.div(scal[17], 2) * (2 * span)
    return (where >= span) & (where < 2 * span)


def reach_of(mark, g):
    return jnp.exp(
        halves(mark[:, 64 + 2 * g : 65 + 2 * g], mark[:, 65 + 2 * g : 66 + 2 * g], (1, LANES))
    )


def by_core(row, run):
    core = lax.rem(row, 2)
    pl.when(core == 0)(functools.partial(run, True))
    pl.when(core == 1)(functools.partial(run, False))


def chip_kernel(scal, mine, theirs, out):
    row, span = scal[17], scal[19]
    half = theirs.shape[0]
    js = 16
    base = 2 * js * LANES
    column = slice(base + 2 * LANES, base + 3 * LANES)

    def join(is_even):
        even, odd = (mine, theirs) if is_even else (theirs, mine)
        both, parts = pair_falls(even, odd, column)
        for j in range(js):
            fall = jnp.exp(mm(parts, picker(32, j)))
            at = slice(j * LANES, (j + 1) * LANES)
            out[:, at] = even[:, at] + fall[0:1] * odd[:, at]
        fall = jnp.exp(halves(both[:, 0:1], both[:, 1:2], (8, LANES)))
        state = even[:, base : base + LANES]
        at = slice(base, base + LANES)
        out[:, at] = fall[1:2] * state + odd[:, at]
        at = slice(base + LANES, base + 2 * LANES)
        out[:, at] = even[:, at] + fall[0:1] * odd[:, at]
        lane = iota((1, LANES), 1)
        late = lane < 0
        for g in range(js):
            at = slice((js + g) * LANES, (js + g + 1) * LANES)
            is_odd = in_odd(scal, g, span)
            gain = is_odd.astype(F32) * reach_of(both[1:2], g)
            out[:, at] = even[:, at] + odd[:, at] + gain * state
            late = late | ((lane // 2 == 32 + g) & is_odd)
        before = jnp.where(lane % 2 == 0, both[0:1, 0:1], both[0:1, 1:2])
        marks = jnp.where(late, before + both[1:2], both[0:1])
        misc = jnp.where(lane < 64, both[0:1] + both[1:2], marks)
        out[:, column] = jnp.broadcast_to(misc, (half, LANES))
        out[:, base + 3 * LANES :] = even[:, base + 3 * LANES :] + odd[:, base + 3 * LANES :]

    by_core(row, join)


def spread_prompt_kernel(scal, got, mine, theirs, to_mine, to_other):
    row, span = scal[17], scal[19]
    js = 16
    base = 2 * js * LANES
    at0 = js * LANES
    column = slice(base + 2 * LANES, base + 3 * LANES)

    def split(is_even):
        even, odd = (mine, theirs) if is_even else (theirs, mine)
        to_even, to_odd = (to_mine, to_other) if is_even else (to_other, to_mine)
        both, _ = pair_falls(even, odd, column)
        fall = jnp.exp(halves(both[:, 0:1], both[:, 1:2], (8, LANES)))
        start = got[:, at0 : at0 + LANES]
        to_even[:, at0 : at0 + LANES] = start
        to_odd[:, at0 : at0 + LANES] = even[:, base : base + LANES] + fall[0:1] * start
        after = got[:, at0 + LANES : at0 + 2 * LANES]
        end = odd[:, base + LANES : base + 2 * LANES] + fall[1:2] * after
        for g in range(js):
            gain = in_odd(scal, g, span).astype(F32) * reach_of(both[1:2], g)
            grad = got[:, g * LANES : (g + 1) * LANES]
            end = end + gain * grad
        to_even[:, at0 + LANES : at0 + 2 * LANES] = end
        to_odd[:, at0 + LANES : at0 + 2 * LANES] = after
        for dst in (to_even, to_odd):
            dst[:, :at0] = got[:, :at0]
            dst[:, at0 + 2 * LANES :] = got[:, at0 + 2 * LANES : at0 + 9 * LANES]

    by_core(row, split)


def by_chip(row, pieces):
    chips = len(pieces)
    chip = lax.div(row, 2)
    for d, piece in enumerate(pieces):
        ns = piece.shape[0]
        yield piece, pl.multiple_of(lax.rem(chip - d + chips, chips) * ns, ns)


def spread_branch_kernel(
    scal, got, p0, p1, p2, p3, mine, theirs, smine, stheirs, to_mine, to_other, after
):
    row = scal[17]
    js = 16
    column = slice((2 * js + 2) * LANES, (2 * js + 3) * LANES)
    for piece, first in by_chip(row, (p0, p1, p2, p3)):
        after[pl.ds(first, piece.shape[0]), :] = piece[:, : js * LANES]

    def split(is_even):
        even, odd = (mine, theirs) if is_even else (theirs, mine)
        state = smine if is_even else stheirs
        to_even, to_odd = (to_mine, to_other) if is_even else (to_other, to_mine)
        _, parts = pair_falls(even, odd, column)
        for j in range(js):
            fall = jnp.exp(mm(parts, picker(32, j)))
            at = slice(j * LANES, (j + 1) * LANES)
            start = got[:, (js + 9 + j) * LANES : (js + 10 + j) * LANES]
            to_even[:, at] = start
            to_odd[:, at] = state[:, at] + fall[0:1] * start
            end = after[:, at]
            at2 = slice((js + j) * LANES, (js + j + 1) * LANES)
            to_even[:, at2] = odd[:, at] + fall[1:2] * end
            to_odd[:, at2] = end

    by_core(row, split)


def join_states_kernel(scal, mine, theirs, smine, stheirs, out):
    row = scal[17]
    js = 16
    column = slice((2 * js + 2) * LANES, (2 * js + 3) * LANES)

    def join(is_even):
        even, odd = (mine, theirs) if is_even else (theirs, mine)
        first, second = (smine, stheirs) if is_even else (stheirs, smine)
        _, parts = pair_falls(even, odd, column)
        for j in range(js):
            fall = jnp.exp(mm(parts, picker(32, j)))
            at = slice(j * LANES, (j + 1) * LANES)
            out[:, at] = fall[1:2] * first[:, at] + second[:, at]

    by_core(row, join)


def slice_kernel(
    scal, got, convbc, joined, msg, adj, pst, cols, early, q0, q1, q2, q3, mat, turned, aft
):
    row = scal[17]
    count, ns = got.shape[0], got.shape[1]
    js = msg.shape[0]
    span = 2 * scal[19]
    base = 2 * js * LANES
    total = got[0, :, base + 3 * LANES :]
    for p in range(1, count):
        total = total + got[p, :, base + 3 * LANES :]
    early[...] = total
    for half in range(2):
        seq = [
            early[2 * r + half : 2 * r + half + 1, ROW_BC * LANES : (ROW_BC + 1) * LANES]
            for r in range(6)
        ]
        taps = [convbc[i : i + 1, half * STATE : (half + 1) * STATE] for i in range(4)]
        mat[...] = jnp.zeros((LANES, LANES), F32)
        for s in range(3):
            mat[s : s + 1, :] = sum(taps[i] * seq[s + i] for i in range(4))
        for i in range(4):
            mat[8 + i : 9 + i, :] = taps[i]
        turned[half * STATE : (half + 1) * STATE, :] = mat[...].T
    start = pl.multiple_of((lax.rem(row, 2) * count + lax.div(row, 2)) * ns, 16)
    b_col = turned[pl.ds(start, ns), :]
    c_col = turned[pl.ds(STATE + start, ns), :]
    cols[0:ns, :] = b_col
    cols[ns : 2 * ns, :] = c_col
    c_all = silu(c_col)
    misc = got[:, 0, base + 2 * LANES : base + 3 * LANES]
    misc_parts = exact(misc)
    log_parts = exact(early[0:8, ROW_STEP * LANES : (ROW_STEP + 1) * LANES])
    for j in range(js):
        at = slice(j * LANES, (j + 1) * LANES)
        fall = jnp.exp(mm(misc_parts, picker(32, j)))
        falls = jnp.exp(mm(log_parts, picker(32, j)))
        a = jnp.zeros((ns, LANES), F32)
        for p in reversed(range(count)):
            aft[p, :, at] = a
            a = fall[p : p + 1] * a + got[p, :, at]
        for s in (2, 1, 0):
            dy = early[j : j + 1, (ROW_DY + s) * LANES : (ROW_DY + s + 1) * LANES]
            a = a + dy * c_all[:, s : s + 1]
            adj[s, :, at] = a
            a = falls[s : s + 1] * a
        msg[j, ns : 2 * ns, :] = a
    pfall = jnp.exp(halves(misc[:, 0:1], misc[:, 1:2], (count, LANES)))
    state = jnp.zeros((ns, LANES), F32)
    for p in range(count):
        pst[p] = state
        state = pfall[p : p + 1] * state + got[p, :, base : base + LANES]
    for g in range(js):
        holder = lax.div(scal[g] - 1, span)
        mark = got[holder, 0:1, base + 2 * LANES : base + 3 * LANES]
        reach = reach_of(mark, g)
        at = slice((js + g) * LANES, (js + g + 1) * LANES)
        msg[g, 0:ns, :] = got[holder, :, at] + reach * pst[holder]
        for r in range(3):
            msg[g, 2 * ns + r : 2 * ns + r + 1, :] = early[
                g : g + 1, (TAIL_X + r) * LANES : (TAIL_X + r + 1) * LANES
            ]
        msg[g, 2 * ns + 3 : 2 * ns + 8, :] = jnp.zeros((5, LANES), F32)
    chip = lax.div(row, 2)
    for d, q in enumerate((q0, q1, q2, q3)):
        to = lax.rem(chip + d, count)
        q[:, : js * LANES] = aft[to]
        q[:, js * LANES :] = joined[pl.ds(pl.multiple_of(to * ns, ns), ns), :]


def chain_kernel(
    scal, got, moved, s0, s1, s2, s3, adj, pst, cols, early, convx, skip,
    msg, rows, injected, states,
):
    row = scal[17]
    first = (row == 0).astype(F32)
    count, ns = got.shape[0], got.shape[1]
    js = moved.shape[0]
    span = 2 * scal[19]
    b_col, c_col = cols[0:ns, :], cols[ns : 2 * ns, :]
    b_all, c_all = silu(b_col), silu(c_col)
    base = 2 * js * LANES
    wide = js * LANES
    for piece, first_row in by_chip(row, (s0, s1, s2, s3)):
        states[pl.ds(first_row, ns), :] = piece[:, js * LANES :]
    misc = got[:, 0, base + 2 * LANES : base + 3 * LANES]
    misc_parts = exact(misc)
    log_parts = exact(early[0:8, ROW_STEP * LANES : (ROW_STEP + 1) * LANES])
    sum_b = [jnp.zeros((ns, LANES), F32) for _ in range(3)]
    sum_c = [jnp.zeros((ns, LANES), F32) for _ in range(3)]
    for j in range(js):
        at = slice(j * LANES, (j + 1) * LANES)
        fall = jnp.exp(mm(misc_parts, picker(32, j)))
        falls = jnp.exp(mm(log_parts, picker(32, j)))
        steps = mm(log_parts, picker(0, j))
        seq = [moved[j, 2 * ns + r : 2 * ns + r + 1, :] for r in range(3)] + [
            early[j : j + 1, (ROW_X + s) * LANES : (ROW_X + s + 1) * LANES] for s in range(3)
        ]
        gain = skip[j : j + 1, :] * first
        state = moved[j, 0:ns, :]
        for s in range(3):
            dy = early[j : j + 1, (ROW_DY + s) * LANES : (ROW_DY + s + 1) * LANES]
            pre = sum(convx[i, j : j + 1, :] * seq[s + i] for i in range(4))
            sg = sigmoid(pre)
            x_conv = pre * sg
            x_hat = steps[s : s + 1] * x_conv
            state = falls[s : s + 1] * state + x_hat * b_all[:, s : s + 1]
            a = adj[s, :, at]
            rows[j : j + 1, s * LANES : (s + 1) * LANES] = (
                jnp.sum(state * c_all[:, s : s + 1], axis=0, keepdims=True) + gain * x_conv
            )
            grad = steps[s : s + 1] * jnp.sum(a * b_all[:, s : s + 1], axis=0, keepdims=True)
            rows[j : j + 1, (3 + s) * LANES : (4 + s) * LANES] = (
                sg * (1.0 + pre * (1.0 - sg)) * (grad + gain * dy)
            )
            sum_c[s] = sum_c[s] + dy * state
            sum_b[s] = sum_b[s] + x_hat * a
        for p in range(count):
            msg[p, :, (js + 9 + j) * LANES : (js + 10 + j) * LANES] = state
            state = fall[p : p + 1] * state + states[p * ns : (p + 1) * ns, at]
    lane = iota((ns, LANES), 1)
    back = jnp.zeros((ns, LANES), F32)
    for which, (total, column) in enumerate(((sum_b, b_col), (sum_c, c_col))):
        grads = [
            jnp.sum(total[s], axis=1, keepdims=True) * silu_slope(column[:, s : s + 1])
            for s in range(3)
        ]
        for m in range(3):
            tail = sum(grads[s] * column[:, 8 + m - s : 9 + m - s] for s in range(m + 1))
            back = jnp.where(lane == 3 * which + m, tail, back)
    pfall = jnp.exp(halves(misc[:, 0:1], misc[:, 1:2], (count, LANES)))
    injected[...] = jnp.zeros(injected.shape, F32)
    for g in range(js):
        holder = lax.div(scal[g] - 1, span)
        mark = got[holder, 0:1, base + 2 * LANES : base + 3 * LANES]
        reach = reach_of(mark, g)
        grad = moved[g, ns : 2 * ns, :]
        injected[holder] = injected[holder] + reach * grad
        for p in range(count):
            msg[p, :, g * LANES : (g + 1) * LANES] = grad
    a = jnp.zeros((ns, LANES), F32)
    for p in reversed(range(count)):
        msg[p, :, wide + LANES : wide + 2 * LANES] = a
        a = pfall[p : p + 1] * a + got[p, :, base + LANES : base + 2 * LANES] + injected[p]
    for p in range(count):
        msg[p, :, wide : wide + LANES] = pst[p]
        msg[p, :, wide + 2 * LANES : wide + 8 * LANES] = rows[...]
        msg[p, :, wide + 8 * LANES : wide + 9 * LANES] = back


def tail_grads(lead, taps):
    return [sum(lead[s] * taps[m - s] for s in range(m + 1)) for m in range(3)]


def assemble(core, mine, theirs, lanes, full):
    half = mine.shape[0]
    full[pl.ds(pl.multiple_of(core * half, half), half), :] = mine[:, lanes]
    full[pl.ds(pl.multiple_of((1 - core) * half, half), half), :] = theirs[:, lanes]


def first_rows(mine, theirs, js, rows):
    at = slice((js + 2) * LANES, (js + 8) * LANES)
    total = mine[0:js, at] + theirs[0:js, at]
    for p in range(1, mine.shape[0] // js):
        total = total + mine[p * js : (p + 1) * js, at] + theirs[p * js : (p + 1) * js, at]
    rows[...] = total


def inner_kernel(
    scal, bx, bbc, bstep, blogs, bdy, rim, convx, convbc, skip,
    smine, sother, yi, gi, rise,
    xs, xt, ds, dys, bcs, wrow, out,
):
    row, length = scal[17], scal[16]
    n, js = bx.shape[0], bx.shape[1]
    conv_branch(bx, rim, convx, xs, xt, ds)
    live_dy(row, length, bdy, dys)
    taps = [convbc[i : i + 1, :] for i in range(4)]
    bc = silu(conv_rows(bbc[...], bc_halo(rim, 19), taps, bcs))
    b, c = bc[:, :STATE], bc[:, STATE:]
    b_t = left(b.T)
    scores = mm_nt(left(c), right_nt(b))
    scores_t = mm_nt(left(b), right_nt(c))
    run = running_sum(without_first(row, blogs[...]))
    wrow[...] = run
    parts = exact(branch_table(without_first(row, bstep[...]), run))
    causal = iota((n, n), 0) >= iota((n, n), 1)
    causal_t = iota((n, n), 0) <= iota((n, n), 1)
    low = iota((n, LANES), 1) < HEAD_DIM

    def head_pair(j, _):
        at = pl.ds(j, n, stride=js)
        steps = mm(parts, picker(0, j))
        runs = mm(parts, picker(32, j))
        x_conv = xt[at, :]
        dy = dys[at, :]
        gain = skip[pl.ds(j, 1), :]
        x_hat = x_conv * steps
        x_hi, x_lo = split2(x_hat)
        dy_b = dy.astype(BF16)
        zero = jnp.zeros_like(dy_b)
        out[:, block(j)] = mm(b_t, right(x_hat * jnp.exp(runs[n - 1 : n, :] - runs)))
        mix, mix_t = [], []
        for k in range(2):
            down = jnp.broadcast_to(runs[:, k * HEAD_DIM : k * HEAD_DIM + 1], (n, n))
            along = wrow[pl.ds(2 * j + k, 1), :]
            mix.append(split2(jnp.exp(jnp.where(causal, down - along, -1e30)) * scores))
            mix_t.append(split2(jnp.exp(jnp.where(causal_t, along - down, -1e30)) * scores_t))
        x_blk = [jnp.where(low, x_hi, zero), jnp.where(low, zero, x_hi)]
        x_rest = [jnp.where(low, x_lo, zero), jnp.where(low, zero, x_lo)]
        d_blk = [jnp.where(low, dy_b, zero), jnp.where(low, zero, dy_b)]
        y = mm(
            jnp.concatenate([mix[0][0], mix[1][0], mix[0][0], mix[1][0], mix[0][1], mix[1][1]], 1),
            jnp.concatenate(x_blk + x_rest + x_blk, 0),
        )
        yi[at, :] = y + gain * x_conv
        g = mm(
            jnp.concatenate([mix_t[0][0], mix_t[1][0], mix_t[0][1], mix_t[1][1]], 1),
            jnp.concatenate(d_blk + d_blk, 0),
        )
        slope = ds[at, :]
        gi[at, :] = (steps * g + gain * dy) * slope
        rise[at, :] = steps * slope
        return 0

    lax.fori_loop(0, js, head_pair, 0, unroll=2)
    for h, half_out in enumerate((smine, sother)):
        half_out[...] = out[part(h, row), :]


def carry_kernel(
    scal, bbc, bstep, blogs, rim, convx, convbc, yi, gi, rise,
    rmine, rtheirs, fmine, ftheirs,
    by, bgx, last, rims,
    xs, ys, bcs, rows, start, after,
):
    row, length = scal[17], scal[16]
    n, js = by.shape[0], by.shape[1]
    core = lax.rem(row, 2)
    assemble(core, fmine, ftheirs, slice(0, js * LANES), start)
    assemble(core, fmine, ftheirs, slice(js * LANES, 2 * js * LANES), after)
    first_rows(rmine, rtheirs, js, rows)
    taps = [convbc[i : i + 1, :] for i in range(4)]
    bc = silu(conv_rows(bbc[...], bc_halo(rim, 19), taps, bcs))
    b_l, c_l = left(bc[:, :STATE]), left(bc[:, STATE:])
    run = running_sum(without_first(row, blogs[...]))
    parts = exact(branch_table(without_first(row, bstep[...]), run))
    xs[n * js : (n + 8) * js, :] = jnp.zeros((8 * js, LANES), F32)

    def head_pair(j, _):
        at = pl.ds(j, n, stride=js)
        runs = mm(parts, picker(32, j))
        ys[at, :] = yi[at, :] + jnp.exp(runs) * mm(c_l, right(start[:, block(j)]))
        fall = jnp.exp(runs[n - 1 : n, :] - runs)
        xs[at, :] = gi[at, :] + rise[at, :] * fall * mm(b_l, right(after[:, block(j)]))
        return 0

    lax.fori_loop(0, js, head_pair, 0, unroll=4)

    @pl.when(row == 0)
    def _():
        for s in range(3):
            ys[s * js : (s + 1) * js, :] = rows[:, s * LANES : (s + 1) * LANES]
            xs[s * js : (s + 1) * js, :] = rows[:, (3 + s) * LANES : (4 + s) * LANES]

    def finish(c, _):
        at = pl.multiple_of(c * 16 * js, 16 * js)
        pos = row * n + c * 16 + iota((16, js, LANES), 0)
        y = ys[pl.ds(at, 16 * js), :].reshape(16, js, LANES)
        by[pl.ds(c * 16, 16)] = jnp.where(pos < length, y, 0.0).astype(BF16)
        g = jnp.zeros((16, js, LANES), F32)
        for i in range(4):
            g = g + convx[i][None] * xs[pl.ds(at + (3 - i) * js, 16 * js), :].reshape(
                16, js, LANES
            )
        bgx[pl.ds(c * 16, 16)] = g.astype(BF16)
        return 0

    lax.fori_loop(0, n // 16, finish, 0)
    for m in range(3):
        at = n - 3 + m
        last[m] = sum(
            convx[i] * xs[(at + 3 - i) * js : (at + 4 - i) * js, :] for i in range(4)
        )
    taps_x = [convx[i] for i in range(4)]
    for m, g in enumerate(tail_grads([xs[s * js : (s + 1) * js, :] for s in range(3)], taps_x)):
        rims[m, 0:js, :] = g


def prompt_kernel(
    scal, px, pbc, pstep, plogs, pdy, rim, convx, convbc, skip, mine, theirs,
    py, pgx, gbc, rims, forks,
    pxs, pbcs, wexp, rows, dxh, dbs, got, tail,
):
    row, col = scal[17], scal[18]
    span, js = px.shape[0], convx.shape[1]
    base = js * LANES
    core = lax.rem(row, 2)
    assemble(core, mine, theirs, slice(0, base + 2 * LANES), got)
    assemble(core, mine, theirs, slice(base + 8 * LANES, base + 9 * LANES), tail)
    first_rows(mine, theirs, js, rows)
    taps = [convbc[i : i + 1, :] for i in range(4)]
    fork_lead = [rows[:, (3 + s) * LANES : (4 + s) * LANES] for s in range(3)]
    for m, g in enumerate(tail_grads(fork_lead, [convx[i] for i in range(4)])):
        forks[m] = g
    own = [convx[i, pl.ds(col, 1), :] for i in range(4)]
    gain = skip[pl.ds(col, 1), :]
    x_pre = conv_rows(px[...], [rim[r, 16:17, :] for r in range(3)], own, pxs)
    bc_pre = conv_rows(pbc[...], bc_halo(rim, 17), taps, pbcs)
    x_p = silu(x_pre)
    bc_p = silu(bc_pre)
    b_p, c_p = bc_p[:, :STATE], bc_p[:, STATE:]
    b_l, c_l = left(b_p), left(c_p)
    scores = mm_nt(c_l, right_nt(b_p))
    scores_t = mm_nt(b_l, right_nt(c_p))
    prun = running_sum(plogs[...])
    ptable = prompt_table(pstep[...], prun)
    runs = halves(ptable[:, 0:1], ptable[:, 1:2], (span, LANES))
    steps = halves(ptable[:, 2:3], ptable[:, 3:4], (span, LANES))
    wexp[...] = runs
    x_hat = x_p * steps
    x_hi, x_lo = split2(x_hat)
    dy_b = pdy[...]
    dy = dy_b.astype(F32)
    low = iota((span, LANES), 1) < HEAD_DIM
    zero = jnp.zeros_like(x_hi)
    causal = iota((span, span), 0) >= iota((span, span), 1)
    causal_t = iota((span, span), 0) <= iota((span, span), 1)
    y = jnp.exp(runs) * mm(c_l, right(got[:, base : base + LANES])) + gain * x_p
    after = right(got[:, base + LANES : base + 2 * LANES])
    g = jnp.exp(runs[span - 1 : span, :] - runs) * mm(b_l, after)
    d_s = jnp.zeros((span, span), F32)
    d_st = jnp.zeros((span, span), F32)
    for k in range(2):
        keep = low if k == 0 else jnp.logical_not(low)
        xk_hi, xk_lo = jnp.where(keep, x_hi, zero), jnp.where(keep, x_lo, zero)
        dk = jnp.where(keep, dy_b, zero)
        down = jnp.broadcast_to(ptable[:, k : k + 1], (span, span))
        along = prun[k : k + 1, :]
        decay = jnp.exp(jnp.where(causal, down - along, -1e30))
        decay_t = jnp.exp(jnp.where(causal_t, along - down, -1e30))
        m_hi, m_lo = split2(decay * scores)
        t_hi, t_lo = split2(decay_t * scores_t)
        y = y + mm(
            jnp.concatenate([m_hi, m_hi, m_lo], 1), jnp.concatenate([xk_hi, xk_lo, xk_hi], 0)
        )
        g = g + mm(jnp.concatenate([t_hi, t_lo], 1), jnp.concatenate([dk, dk], 0))
        d_two = jnp.concatenate([dk, dk], 1)
        x_two = jnp.concatenate([x_hi, x_lo], 1)
        d_s = d_s + decay * mm_nt(d_two, x_two)
        d_st = d_st + decay_t * mm_nt(x_two, d_two)
    py[...] = y.astype(BF16)
    d_c = mm(left(d_s), right(b_p)) + mm_nt(
        left(jnp.exp(runs) * dy), right_nt(got[:, base : base + LANES])
    )
    d_b = mm(left(d_st), right(c_p)) + mm_nt(
        left(jnp.exp(runs[span - 1 : span, :] - runs) * x_hat),
        right_nt(got[:, base + LANES : base + 2 * LANES]),
    )
    dxh[...] = g
    dbs[...] = d_b
    pxs[0:span, :] = x_hat

    def fork(q, _):
        where = scal[q] - 1 - row * span

        @pl.when((where >= 0) & (where < span))
        def _():
            gap = wexp[pl.ds(where, 1), :] - wexp[...]
            u = jnp.exp(jnp.where(iota((span, LANES), 0) <= where, gap, -1e30))
            grad = got[:, block(q)]
            dxh[...] += u * mm(b_l, right(grad))
            dbs[...] += mm_nt(left(u * pxs[0:span, :]), right_nt(grad))

        return 0

    lax.fori_loop(0, js, fork, 0)
    pre_g = (steps * dxh[...] + gain * dy) * silu_slope(x_pre)
    pxs[0:span, :] = pre_g
    pxs[span : span + 8, :] = jnp.zeros((8, LANES), F32)
    pgx[...] = sum(own[i] * pxs[3 - i : 3 - i + span, :] for i in range(4))
    for m, v in enumerate(tail_grads([pxs[s : s + 1, :] for s in range(3)], own)):
        rims[m, 0:1, :] = v
    pbcs[0:span, :] = jnp.concatenate([dbs[...], d_c], axis=1) * silu_slope(bc_pre)
    pbcs[span : span + 8, :] = jnp.zeros((8, 2 * STATE), F32)
    grad = sum(taps[i] * pbcs[3 - i : 3 - i + span, :] for i in range(4))
    for m, v in enumerate(tail_grads([pbcs[s : s + 1, :] for s in range(3)], taps)):
        rims[m, 1:2, :] = v[:, :STATE]
        rims[m, 2:3, :] = v[:, STATE:]
    spot = iota((span, LANES), 0) - (scal[20] - 3 - row * span)
    lane = iota((span, LANES), 1)
    tails = exact(tail[...])
    into = []
    for half in range(2):
        hit = ((spot >= 0) & (spot < 3) & (lane == spot + 3 * half)).astype(F32).astype(BF16)
        into.append(mm_nt(jnp.concatenate([hit, hit, hit], 1), tails))
    gbc[...] = grad + jnp.concatenate(into, axis=1)


def packing_kernel(pgx, gbc, back, forks, msg, out):
    span, peers = pgx.shape[0], msg.shape[0]
    rows = span // peers
    out[...] = pgx[...]
    for m in range(3):
        at = slice(span - 3 + m, span - 2 + m)
        out[at, :] = pgx[at, :] + back[m, 0:1, :]
    for q in range(peers):
        msg[q, 0:rows, :] = gbc[q * rows : (q + 1) * rows, :STATE]
        msg[q, rows : 2 * rows, :] = gbc[q * rows : (q + 1) * rows, STATE:]
        for m in range(3):
            msg[q, 2 * rows + m : 2 * rows + m + 1, :] = forks[m, q : q + 1, :]
        msg[q, 2 * rows + 3 : 2 * rows + 8, :] = jnp.zeros((5, LANES), F32)
    for m in range(3):
        at = rows - 3 + m
        msg[peers - 1, at : at + 1, :] += back[m, 1:2, :]
        msg[peers - 1, rows + at : rows + at + 1, :] += back[m, 2:3, :]


def finish_kernel(scal, pgx, got, out_x, out_bc, tails):
    row = scal[17]
    span, peers = pgx.shape[0], got.shape[0]
    rows = span // peers
    total = got[0, 0 : 2 * rows, :]
    for p in range(1, peers):
        total = total + got[p, 0 : 2 * rows, :]
    out_bc[:, :STATE] = total[0:rows].astype(BF16)
    out_bc[:, STATE:] = total[rows : 2 * rows].astype(BF16)
    lane = iota((1, LANES), 1)
    spot = jnp.full((1, LANES), -1, jnp.int32)
    tails[...] = jnp.zeros((LANES, LANES), F32)
    for g in range(peers):
        tails[8 * g : 8 * g + 8, :] = got[g, 2 * rows : 2 * rows + 8, :]
        where = scal[g] - 3 - row * span + lane - 8 * g
        spot = jnp.where((lane >= 8 * g) & (lane < 8 * g + 3), where, spot)
    hit = (iota((span, LANES), 0) == spot).astype(F32).astype(BF16)
    into = mm(jnp.concatenate([hit, hit, hit], 1), jnp.concatenate(split3(tails[...]), 0))
    out_x[...] = (pgx[...] + into).astype(BF16)


def call(kernel, args, outs, scratch, scalars=1, flops=10**9, blocks=None, out_smem=0):
    vmem = pl.BlockSpec(memory_space=pltpu.VMEM)
    smem = pl.BlockSpec(memory_space=pltpu.SMEM)
    given = [smem] * scalars + [vmem] * (len(args) - scalars)
    for at, spec in (blocks or {}).items():
        given[at] = spec
    return pl.pallas_call(
        kernel,
        grid=(1,) if blocks else (),
        out_shape=[jax.ShapeDtypeStruct(s, d) for s, d in outs],
        in_specs=given,
        out_specs=[smem] * out_smem + [vmem] * (len(outs) - out_smem),
        scratch_shapes=[pltpu.VMEM(s, F32) for s in scratch],
        compiler_params=pltpu.CompilerParams(vmem_limit_bytes=VMEM_LIMIT),
        cost_estimate=pl.CostEstimate(flops=flops, bytes_accessed=10**6, transcendentals=0),
    )(*args)


def shards(
    prompt_x,
    prompt_bc,
    prompt_dt,
    branch_x,
    branch_bc,
    branch_dt,
    conv_x,
    conv_bc,
    a_log,
    dt_bias,
    d_skip,
    lengths,
    forks,
    holder,
    prompt_dy,
    branch_dy,
):
    count = lax.axis_size("prefix")
    js = lax.axis_size("branch")
    span = prompt_x.shape[0]
    n = branch_x.shape[1]
    heads = 2 * js
    ns = STATE // count
    chips = count // 2
    half = STATE // 2
    px = prompt_x.reshape(span, LANES)
    pbc = prompt_bc.reshape(span, 2 * STATE)
    pdt = prompt_dt.reshape(2, span)
    pdy = prompt_dy.reshape(span, LANES)
    bx = branch_x.reshape(n, js, LANES)
    bbc = branch_bc.reshape(n, 2 * STATE)
    bdt = branch_dt.reshape(heads, n)
    bdy = branch_dy.reshape(n, js, LANES)
    convx = conv_x.reshape(4, js, LANES)
    convbc = conv_bc.reshape(4, 2 * STATE)
    a_pair, bias_pair, skip_pair = (
        jnp.transpose(v.reshape(js, 2)) for v in (a_log, dt_bias, d_skip)
    )
    cores = [(i, i ^ 1) for i in range(count)]
    columns = [[i for i in range(count) if i % 2 == c] for c in range(2)]

    with jax.named_scope("setup"):
        scal, rim, step, logs, pstep, plogs, skip = call(
            setup_kernel,
            [forks, lengths, holder, bx, px, pbc, bbc, a_pair, bias_pair, skip_pair, bdt, pdt],
            [
                ((24,), jnp.int32),
                ((3, js + 5, LANES), F32),
                ((heads, n), F32),
                ((heads, n), F32),
                ((2, span), F32),
                ((2, span), F32),
                ((js, LANES), F32),
            ],
            [],
            scalars=3,
            out_smem=1,
            blocks={
                3: pl.BlockSpec((16, js, LANES), lambda i: (n // 16 - 1, 0, 0)),
                4: pl.BlockSpec((16, LANES), lambda i: (span // 16 - 1, 0)),
                5: pl.BlockSpec((16, 2 * STATE), lambda i: (span // 16 - 1, 0)),
                6: pl.BlockSpec((16, 2 * STATE), lambda i: (n // 16 - 1, 0)),
            },
        )
    rim = lax.ppermute(rim, "prefix", [(i, i + 1) for i in range(count - 1)])
    big = (n * js, LANES)
    tall = ((n + 8) * js, LANES)
    each = (half, js * LANES)
    piece = (ns, 2 * js * LANES)

    def across(v):
        return lax.ppermute(v, "prefix", cores)

    def round_chips(blocks):
        moved_on = [blocks[0]]
        for d in range(1, chips):
            pairs = [(i, (i + 2 * d) % count) for i in range(count)]
            moved_on.append(lax.ppermute(blocks[d], "prefix", pairs))
        return moved_on

    def between_chips(v):
        return lax.all_to_all(v, "prefix", 0, 0, axis_index_groups=columns, tiled=True)

    width = (2 * js + 3 + EARLY) * LANES
    with jax.named_scope("lead"):
        mine, other = call(
            lead_kernel,
            [scal, px, pbc, pstep, plogs, pdy, bx, bbc, step, logs, bdy, rim, convx, convbc],
            [((half, width), F32)] * 2,
            [
                big, (n + 8, 2 * STATE), (span + 8, LANES), (span + 8, 2 * STATE),
                (span, LANES), (span, LANES), (js, EARLY * LANES), (STATE, (2 * js + 3) * LANES),
            ],
        )
    theirs = across(other)
    with jax.named_scope("chip"):
        (joined,) = call(chip_kernel, [scal, mine, theirs], [((half, width), F32)], [])
    got = between_chips(joined.reshape(chips, ns, width))
    with jax.named_scope("inner"):
        smine, sother, yi, gi, rise = call(
            inner_kernel,
            [scal, bx, bbc, step, logs, bdy, rim, convx, convbc, skip],
            [(each, F32)] * 2 + [(big, F32)] * 3,
            [tall, big, big, big, (n + 8, 2 * STATE), (heads, n), (STATE, js * LANES)],
            flops=10**10,
        )
    stheirs = across(sother)
    with jax.named_scope("join_states"):
        (sjoined,) = call(
            join_states_kernel, [scal, mine, theirs, smine, stheirs], [(each, F32)], []
        )
    with jax.named_scope("slices"):
        msg, adj, pst, cols, early, *ablocks = call(
            slice_kernel,
            [scal, got, convbc, sjoined],
            [
                ((js, 2 * ns + 8, LANES), F32),
                ((3, ns, js * LANES), F32),
                ((chips, ns, LANES), F32),
                ((2 * ns, LANES), F32),
                ((ns, EARLY * LANES), F32),
            ]
            + [(piece, F32)] * 4,
            [(LANES, LANES), (2 * STATE, LANES), (chips, ns, js * LANES)],
        )
    moved = lax.all_to_all(msg, "branch", 0, 0, tiled=True)
    agot = round_chips(ablocks)
    moved, *agot = lax.optimization_barrier((moved, *agot))
    width3 = (js + 9) * LANES
    with jax.named_scope("chains"):
        (msg3,) = call(
            chain_kernel,
            [scal, got, moved, *agot, adj, pst, cols, early, convx, skip],
            [((chips, ns, width3 + js * LANES), F32)],
            [(js, 6 * LANES), (chips, ns, LANES), each],
        )
    got3 = between_chips(msg3).reshape(half, width3 + js * LANES)
    with jax.named_scope("spread_prompt"):
        rmine, rother = call(
            spread_prompt_kernel,
            [scal, got3, mine, theirs],
            [((half, width3), F32)] * 2,
            [],
        )
    both = (half, 2 * js * LANES)
    with jax.named_scope("spread_branch"):
        fmine, fother = call(
            spread_branch_kernel,
            [scal, got3, *agot, mine, theirs, smine, stheirs],
            [(both, F32)] * 2,
            [each],
        )
    rtheirs = across(rother)
    rtheirs, fother = lax.optimization_barrier((rtheirs, fother))
    ftheirs = across(fother)
    with jax.named_scope("prompt"):
        py, pgx, gbc, prims, fork_grads = call(
            prompt_kernel,
            [scal, px, pbc, pstep, plogs, pdy, rim, convx, convbc, skip, rmine, rtheirs],
            [
                ((span, LANES), BF16),
                ((span, LANES), F32),
                ((span, 2 * STATE), F32),
                ((3, 3, LANES), F32),
                ((3, js, LANES), F32),
            ],
            [
                (span + 8, LANES), (span + 8, 2 * STATE), (span, LANES), (js, 6 * LANES),
                (span, LANES), (span, STATE), (STATE, (js + 2) * LANES), (STATE, LANES),
            ],
        )
    backward = [(i, i - 1) for i in range(1, count)]
    pback = lax.ppermute(prims, "prefix", backward)
    with jax.named_scope("packing"):
        out_msg, pgx = call(
            packing_kernel,
            [pgx, gbc, pback, fork_grads],
            [((js, 2 * span // js + 8, LANES), F32), ((span, LANES), F32)],
            [],
            scalars=0,
        )
    end = lax.all_to_all(out_msg, "branch", 0, 0, tiled=True)
    with jax.named_scope("carry"):
        by, bgx, last, brims = call(
            carry_kernel,
            [
                scal, bbc, step, logs, rim, convx, convbc, yi, gi, rise,
                rmine, rtheirs, fmine, ftheirs,
            ],
            [
                ((n, js, LANES), BF16),
                ((n, js, LANES), BF16),
                ((3, js, LANES), F32),
                ((3, js, LANES), F32),
            ],
            [
                tall, big, (n + 8, 2 * STATE), (js, 6 * LANES),
                (STATE, js * LANES), (STATE, js * LANES),
            ],
            flops=10**10,
        )
    bback = lax.ppermute(brims, "prefix", backward)
    bgx = bgx.at[-3:].set((last + bback).astype(BF16))
    with jax.named_scope("finish"):
        prompt_gx, prompt_gbc = call(
            finish_kernel,
            [scal, pgx, end],
            [((span, LANES), BF16), ((span // js, 2 * STATE), BF16)],
            [(LANES, LANES)],
        )
    return (
        py.reshape(prompt_x.shape),
        by.reshape(branch_x.shape),
        prompt_gx.reshape(prompt_x.shape),
        bgx.reshape(branch_x.shape),
        prompt_gbc.reshape(span // js, 1, 2 * STATE),
    )


def solution(mesh):
    return jax.shard_map(
        shards,
        mesh=mesh,
        in_specs=(
            P("prefix", "branch", "tensor", None),
            P("prefix", "tensor", None),
            P("branch", "tensor", None, "prefix"),
            P("branch", "prefix", None, "tensor", None),
            P("branch", "prefix", "tensor", None),
            P("branch", None, "tensor", None, "prefix"),
            P(None, None, "tensor", None),
            P(None, "tensor", None),
            P(None, "tensor", None),
            P(None, "tensor", None),
            P(None, "tensor", None),
            P(),
            P(),
            P(),
            P("prefix", "branch", "tensor", None),
            P("branch", "prefix", None, "tensor", None),
        ),
        out_specs=(
            P("prefix", "branch", "tensor", None),
            P("branch", "prefix", None, "tensor", None),
            P("prefix", "branch", "tensor", None),
            P("branch", "prefix", None, "tensor", None),
            P(("prefix", "branch"), "tensor", None),
        ),
        check_vma=False,
    )
```

```python
import functools

import jax
import jax.numpy as jnp
from jax import lax
from jax.experimental import pallas as pl
from jax.experimental.pallas import tpu as pltpu
from jax.sharding import PartitionSpec as P

HEAD_DIM = 64
STATE = 128
LANES = 128

F32 = jnp.float32
BF16 = jnp.bfloat16

TAIL_X = 0
ROW_X = 3
ROW_DY = 6
ROW_BC = 9
ROW_STEP = 10
EARLY = 11

VMEM_LIMIT = 56 * 1024 * 1024


def split2(a):
    hi = a.astype(BF16)
    return hi, (a - hi.astype(F32)).astype(BF16)


def split3(a):
    hi = a.astype(BF16)
    rest = a - hi.astype(F32)
    mid = rest.astype(BF16)
    return hi, mid, (rest - mid.astype(F32)).astype(BF16)


def mm(a, b):
    return lax.dot_general(a, b, (((1,), (0,)), ((), ())), preferred_element_type=F32)


def mm_nt(a, b):
    return lax.dot_general(a, b, (((1,), (1,)), ((), ())), preferred_element_type=F32)


def left(a):
    hi, lo = split2(a)
    return jnp.concatenate([hi, hi, lo], axis=1)


def right(b):
    hi, lo = split2(b)
    return jnp.concatenate([hi, lo, hi], axis=0)


def right_nt(b):
    hi, lo = split2(b)
    return jnp.concatenate([hi, lo, hi], axis=1)


def exact(a):
    return jnp.concatenate(split3(a), axis=1)


def iota(shape, dim):
    return lax.broadcasted_iota(jnp.int32, shape, dim)


def picker(base, j):
    one = (iota((LANES, LANES), 0) == base + 2 * j + iota((LANES, LANES), 1) // HEAD_DIM).astype(
        F32
    ).astype(BF16)
    return jnp.concatenate([one, one, one], axis=0)


def running_sum(logs):
    size = logs.shape[1]
    upper = (iota((size, size), 0) <= iota((size, size), 1)).astype(F32).astype(BF16)
    return mm(exact(logs), jnp.concatenate([upper, upper, upper], axis=0))


def block(j):
    return pl.ds(pl.multiple_of(j * LANES, LANES), LANES)


def sigmoid(x):
    return 1.0 / (1.0 + jnp.exp(-x))


def head_column(pair, heads):
    shape = (heads, heads // 2)
    r = iota(shape, 0)
    both = jnp.where(r % 2 == 0, pair[0:1], pair[1:2])
    return jnp.sum(jnp.where(iota(shape, 1) == r // 2, both, 0.0), axis=1, keepdims=True)


def softplus(x):
    return jnp.maximum(x, 0.0) + jnp.log1p(jnp.exp(-jnp.abs(x)))


def setup_kernel(
    forks, lengths, holder, bx, px, pbc, bbc, alog, bias, gain, bdt, pdt,
    scal, rim, step, logs, pstep, plogs, skip,
):
    row, col = lax.axis_index("prefix"), lax.axis_index("branch")
    js = bx.shape[1]

    def place(b, _):
        group = lax.fori_loop(
            0, js, lambda c, t: t + (holder[c] < holder[b]).astype(jnp.int32), jnp.int32(0),
            unroll=16,
        )
        scal[group] = forks[b]

        @pl.when(group == col)
        def _():
            scal[16] = lengths[b]
            scal[20] = forks[b]

        return 0

    lax.fori_loop(0, js, place, 0)
    scal[17] = row
    scal[18] = col
    scal[19] = pdt.shape[1]
    last = bx.shape[0] - 3
    xl = px[...].astype(F32)
    bcl = pbc[...].astype(F32)
    bbl = bbc[...].astype(F32)
    for r in range(3):
        rim[r, 0:js, :] = bx[last + r].astype(F32)
        at = slice(last + r, last + r + 1)
        rim[r, js : js + 1, :] = xl[at]
        rim[r, js + 1 : js + 2, :] = bcl[at, :STATE]
        rim[r, js + 2 : js + 3, :] = bcl[at, STATE:]
        rim[r, js + 3 : js + 4, :] = bbl[at, :STATE]
        rim[r, js + 4 : js + 5, :] = bbl[at, STATE:]
    heads = bdt.shape[0]
    s = softplus(bdt[...] + head_column(bias[...], heads))
    step[...] = s
    logs[...] = -jnp.exp(head_column(alog[...], heads)) * s
    own = iota((2, js), 1) == col
    own_bias = jnp.sum(jnp.where(own, bias[...], 0.0), axis=1, keepdims=True)
    own_rate = jnp.exp(jnp.sum(jnp.where(own, alog[...], 0.0), axis=1, keepdims=True))
    s = softplus(pdt[...] + own_bias)
    pstep[...] = s
    plogs[...] = -own_rate * s
    diag = iota((js, js), 0) == iota((js, js), 1)
    first = jnp.sum(jnp.where(diag, gain[0:1], 0.0), axis=1, keepdims=True)
    second = jnp.sum(jnp.where(diag, gain[1:2], 0.0), axis=1, keepdims=True)
    skip[...] = halves(first, second, (js, LANES))


def conv_branch(bx, rim, convx, xs, xt, ds):
    js = bx.shape[1]
    for r in range(3):
        xs[(5 + r) * js : (6 + r) * js, :] = rim[r, 0:js, :]

    def fill(c, _):
        xs[pl.ds(pl.multiple_of(8 * js + c * 16 * js, 16 * js), 16 * js), :] = (
            bx[pl.ds(c * 16, 16)].astype(F32).reshape(16 * js, LANES)
        )
        return 0

    lax.fori_loop(0, bx.shape[0] // 16, fill, 0)

    def one(c, _):
        pre = jnp.zeros((16, js, LANES), F32)
        for i in range(4):
            start = pl.multiple_of((5 + i) * js + c * 16 * js, js)
            pre = pre + convx[i][None] * xs[pl.ds(start, 16 * js), :].reshape(16, js, LANES)
        sg = sigmoid(pre)
        at = pl.ds(pl.multiple_of(c * 16 * js, 16 * js), 16 * js)
        xt[at, :] = (pre * sg).reshape(16 * js, LANES)
        if ds is not None:
            ds[at, :] = (sg * (1.0 + pre * (1.0 - sg))).reshape(16 * js, LANES)
        return 0

    lax.fori_loop(0, bx.shape[0] // 16, one, 0)


def conv_rows(raw, halo_rows, taps, scratch):
    n = raw.shape[0]
    scratch[8 : 8 + n, :] = raw.astype(F32)
    for r in range(3):
        scratch[5 + r : 6 + r, :] = halo_rows[r]
    pre = jnp.zeros(raw.shape, F32)
    for i in range(4):
        pre = pre + taps[i] * scratch[5 + i : 5 + i + n, :]
    return pre


def bc_halo(rim, first):
    return [
        jnp.concatenate([rim[r, first : first + 1, :], rim[r, first + 1 : first + 2, :]], axis=1)
        for r in range(3)
    ]


def silu(x):
    return x * sigmoid(x)


def silu_slope(x):
    sg = sigmoid(x)
    return sg * (1.0 + x * (1.0 - sg))


def without_first(row, values):
    return jnp.where((row == 0) & (iota(values.shape, 1) < 3), 0.0, values)


def branch_table(step, run):
    return jnp.concatenate([step, run, jnp.zeros((64, LANES), F32)], axis=0).T


def prompt_table(step, run):
    n = step.shape[1]
    r = iota((LANES, n), 0)
    runs = jnp.where(r % 2 == 0, run[0:1], run[1:2])
    steps = jnp.where(r % 2 == 0, step[0:1], step[1:2])
    return jnp.where((r == 2) | (r == 3), steps, runs).T


def halves(first, second, shape):
    return jnp.where(iota(shape, 1) < HEAD_DIM, first, second)


def part(h, row):
    half = STATE // 2
    core = lax.rem(row, 2)
    return pl.ds(pl.multiple_of((core if h == 0 else 1 - core) * half, half), half)


def live_dy(row, length, bdy, dys):
    n, js = bdy.shape[0], bdy.shape[1]

    def fill(c, _):
        pos = row * n + c * 16 + iota((16, js, LANES), 0)
        dead = (pos >= length) | (pos < 3)
        dys[pl.ds(pl.multiple_of(c * 16 * js, 16 * js), 16 * js), :] = jnp.where(
            dead, 0.0, bdy[pl.ds(c * 16, 16)].astype(F32)
        ).reshape(16 * js, LANES)
        return 0

    lax.fori_loop(0, n // 16, fill, 0)


def early_kernel(
    scal, px, pbc, pstep, plogs, bx, bbc, bstep, blogs, bdy,
    early, dys, table, run, ptable, prun,
):
    row, length = scal[17], scal[16]
    js = bdy.shape[1]
    span = px.shape[0]
    live_dy(row, length, bdy, dys)
    step, logs = bstep[...], blogs[...]
    sums = running_sum(without_first(row, logs))
    run[...] = sums
    table[...] = branch_table(without_first(row, step), sums)
    sums = running_sum(plogs[...])
    prun[...] = sums
    ptable[...] = prompt_table(pstep[...], sums)
    first = (row == 0).astype(F32)
    lane2 = iota((js, span), 1)
    spot = jnp.zeros((js, span), jnp.int32)
    for g in range(js):
        spot = jnp.where(iota((js, span), 0) == g, scal[g] - 3 - row * span, spot)
    hits = jnp.concatenate([(lane2 == spot + r).astype(F32).astype(BF16) for r in range(3)], 0)
    tails = mm(hits, px[...])
    own_spot = scal[20] - 3 - row * span + iota((js, span), 0)
    hit = ((lane2 == own_spot) & (iota((js, span), 0) < 3)).astype(F32).astype(BF16)
    tail_bc = mm(hit, pbc[...])
    raw_bc = bbc[...].astype(F32) * first
    raw = jnp.concatenate([step, logs, jnp.zeros((64, LANES), F32)], axis=0).T
    early[...] = jnp.zeros(early.shape, F32)
    for r in range(3):
        early[:, (TAIL_X + r) * LANES : (TAIL_X + r + 1) * LANES] = tails[r * js : (r + 1) * js]
        early[:, (ROW_X + r) * LANES : (ROW_X + r + 1) * LANES] = bx[r].astype(F32) * first
        early[:, (ROW_DY + r) * LANES : (ROW_DY + r + 1) * LANES] = bdy[r].astype(F32) * (
            first * (r < length).astype(F32)
        )
        for half in range(2):
            at = slice(half * STATE, (half + 1) * STATE)
            early[2 * r + half : 2 * r + half + 1, ROW_BC * LANES : (ROW_BC + 1) * LANES] = (
                tail_bc[r : r + 1, at]
            )
            early[6 + 2 * r + half : 7 + 2 * r + half, ROW_BC * LANES : (ROW_BC + 1) * LANES] = (
                raw_bc[r : r + 1, at]
            )
    early[0:8, ROW_STEP * LANES : (ROW_STEP + 1) * LANES] = raw[0:8] * first


def lead_kernel(
    scal, px, pbc, pdy, bbc, rim, convx, convbc, early, dys, table, tab,
    mine, other, bcs, pxs, pbcs, wexp, out,
):
    row, col = scal[17], scal[18]
    js = convx.shape[1]
    n = bbc.shape[0]
    span = px.shape[0]
    taps = [convbc[i : i + 1, :] for i in range(4)]
    bc = silu(conv_rows(bbc[...], bc_halo(rim, 19), taps, bcs))
    c_t = left(bc[:, STATE:].T)

    runs = table[...]
    grown = jnp.exp(runs)
    for j in range(0, js, 2):
        dy = [
            dys[pl.ds(q, n, stride=js), :] * head_lanes(grown, 32, q) for q in (j, j + 1)
        ]
        out[:, j * LANES : (j + 2) * LANES] = mm(c_t, right(jnp.concatenate(dy, axis=1)))

    own = [convx[i, pl.ds(col, 1), :] for i in range(4)]
    x_p = silu(conv_rows(px[...], [rim[r, 16:17, :] for r in range(3)], own, pxs))
    bc_p = silu(conv_rows(pbc[...], bc_halo(rim, 17), taps, pbcs))
    b_pt = left(bc_p[:, :STATE].T)
    c_pt = left(bc_p[:, STATE:].T)
    ptable = tab[...]
    runs = halves(ptable[:, 0:1], ptable[:, 1:2], (span, LANES))
    steps = halves(ptable[:, 2:3], ptable[:, 3:4], (span, LANES))
    wexp[...] = runs
    x_hat = x_p * steps
    base = 2 * js * LANES
    out[:, base : base + LANES] = mm(b_pt, right(x_hat * jnp.exp(runs[span - 1 : span, :] - runs)))
    out[:, base + LANES : base + 2 * LANES] = mm(
        c_pt, right(pdy[...].astype(F32) * jnp.exp(runs))
    )
    lane = iota((1, LANES), 1)
    pxs[0:span, :] = x_hat

    def fork(g, acc):
        where = scal[g] - 1 - row * span
        inside = (where >= 0) & (where < span)

        @pl.when(inside)
        def _():
            w = wexp[...]
            gap = wexp[pl.ds(where, 1), :] - w
            upto = iota((span, LANES), 0) <= where
            u = jnp.exp(jnp.where(upto, gap, -1e30)) * pxs[0:span, :]
            out[:, block(js + g)] = mm(b_pt, right(u))

        @pl.when(jnp.logical_not(inside))
        def _():
            out[:, block(js + g)] = jnp.zeros((STATE, LANES), F32)

        safe = jnp.clip(where, 0, span - 1)
        return jnp.where(lane // 2 == 32 + g, tab[pl.ds(safe, 1), :], acc)

    marks = lax.fori_loop(0, js, fork, jnp.zeros((1, LANES), F32))
    misc = jnp.where(lane < 2, ptable[span - 1 : span, :], marks)
    misc = jnp.where((lane >= 32) & (lane < 64), table[n - 1 : n, :], misc)
    out[:, base + 2 * LANES : base + 3 * LANES] = jnp.broadcast_to(misc, (STATE, LANES))

    for h, half_out in enumerate((mine, other)):
        half_out[:, : base + 3 * LANES] = out[part(h, row), :]
        for q in range(half_out.shape[0] // js):
            half_out[q * js : (q + 1) * js, base + 3 * LANES :] = early[...]


def pair_falls(even, odd, column):
    both = jnp.concatenate([even[0:1, column], odd[0:1, column], jnp.zeros((6, LANES), F32)], 0)
    return both, jnp.exp(both)


def head_lanes(values, base, j):
    at = base + 2 * j
    return halves(values[:, at : at + 1], values[:, at + 1 : at + 2], values.shape)


def in_odd(scal, g, span):
    where = scal[g] - 1 - lax.div(scal[17], 2) * (2 * span)
    return (where >= span) & (where < 2 * span)


def reach_of(mark, g):
    return jnp.exp(
        halves(mark[:, 64 + 2 * g : 65 + 2 * g], mark[:, 65 + 2 * g : 66 + 2 * g], (1, LANES))
    )


def by_core(row, run):
    core = lax.rem(row, 2)
    pl.when(core == 0)(functools.partial(run, True))
    pl.when(core == 1)(functools.partial(run, False))


def chip_kernel(scal, mine, theirs, out, keep_mine, keep_theirs):
    row, span = scal[17], scal[19]
    half = theirs.shape[0]
    js = 16
    base = 2 * js * LANES
    column = slice(base + 2 * LANES, base + 3 * LANES)
    keep_mine[...] = mine[:, base : base + 3 * LANES]
    keep_theirs[...] = theirs[:, base : base + 3 * LANES]

    def join(is_even):
        even, odd = (mine, theirs) if is_even else (theirs, mine)
        both, parts = pair_falls(even, odd, column)
        for j in range(js):
            fall = head_lanes(parts, 32, j)
            at = slice(j * LANES, (j + 1) * LANES)
            out[:, at] = even[:, at] + fall[0:1] * odd[:, at]
        fall = jnp.exp(halves(both[:, 0:1], both[:, 1:2], (8, LANES)))
        state = even[:, base : base + LANES]
        at = slice(base, base + LANES)
        out[:, at] = fall[1:2] * state + odd[:, at]
        at = slice(base + LANES, base + 2 * LANES)
        out[:, at] = even[:, at] + fall[0:1] * odd[:, at]
        lane = iota((1, LANES), 1)
        late = lane < 0
        for g in range(js):
            at = slice((js + g) * LANES, (js + g + 1) * LANES)
            is_odd = in_odd(scal, g, span)
            gain = is_odd.astype(F32) * reach_of(both[1:2], g)
            out[:, at] = even[:, at] + odd[:, at] + gain * state
            late = late | ((lane // 2 == 32 + g) & is_odd)
        before = jnp.where(lane % 2 == 0, both[0:1, 0:1], both[0:1, 1:2])
        marks = jnp.where(late, before + both[1:2], both[0:1])
        misc = jnp.where(lane < 64, both[0:1] + both[1:2], marks)
        out[:, column] = jnp.broadcast_to(misc, (half, LANES))
        out[:, base + 3 * LANES :] = even[:, base + 3 * LANES :] + odd[:, base + 3 * LANES :]

    by_core(row, join)


def by_chip(row, pieces):
    chips = len(pieces)
    chip = lax.div(row, 2)
    for d, piece in enumerate(pieces):
        ns = piece.shape[0]
        yield piece, pl.multiple_of(lax.rem(chip - d + chips, chips) * ns, ns)


def spread_branch_kernel(
    scal, got, p0, p1, p2, p3, mine, theirs, smine, stheirs, to_mine, to_other, after
):
    row = scal[17]
    js = 16
    column = slice((2 * js + 2) * LANES, (2 * js + 3) * LANES)
    for piece, first in by_chip(row, (p0, p1, p2, p3)):
        after[pl.ds(first, piece.shape[0]), :] = piece[:, : js * LANES]

    def split(is_even):
        even, odd = (mine, theirs) if is_even else (theirs, mine)
        state = smine if is_even else stheirs
        to_even, to_odd = (to_mine, to_other) if is_even else (to_other, to_mine)
        _, parts = pair_falls(even, odd, column)
        for j in range(js):
            fall = head_lanes(parts, 32, j)
            at = slice(j * LANES, (j + 1) * LANES)
            start = got[:, (js + 9 + j) * LANES : (js + 10 + j) * LANES]
            to_even[:, at] = start
            to_odd[:, at] = state[:, at] + fall[0:1] * start
            end = after[:, at]
            at2 = slice((js + j) * LANES, (js + j + 1) * LANES)
            to_even[:, at2] = odd[:, at] + fall[1:2] * end
            to_odd[:, at2] = end

    by_core(row, split)


def join_states_kernel(scal, mine, theirs, smine, stheirs, out):
    row = scal[17]
    js = 16
    column = slice(2 * LANES, 3 * LANES)

    def join(is_even):
        even, odd = (mine, theirs) if is_even else (theirs, mine)
        first, second = (smine, stheirs) if is_even else (stheirs, smine)
        _, parts = pair_falls(even, odd, column)
        for j in range(js):
            fall = head_lanes(parts, 32, j)
            at = slice(j * LANES, (j + 1) * LANES)
            out[:, at] = fall[1:2] * first[:, at] + second[:, at]

    by_core(row, join)


def slice_kernel(
    scal, got, convbc, joined, msg, adj, pst, cols, early, q0, q1, q2, q3, mat, turned, aft
):
    row = scal[17]
    count, ns = got.shape[0], got.shape[1]
    js = msg.shape[0]
    span = 2 * scal[19]
    base = 2 * js * LANES
    total = got[0, :, base + 3 * LANES :]
    for p in range(1, count):
        total = total + got[p, :, base + 3 * LANES :]
    early[...] = total
    for half in range(2):
        seq = [
            early[2 * r + half : 2 * r + half + 1, ROW_BC * LANES : (ROW_BC + 1) * LANES]
            for r in range(6)
        ]
        taps = [convbc[i : i + 1, half * STATE : (half + 1) * STATE] for i in range(4)]
        mat[...] = jnp.zeros((LANES, LANES), F32)
        for s in range(3):
            mat[s : s + 1, :] = sum(taps[i] * seq[s + i] for i in range(4))
        for i in range(4):
            mat[8 + i : 9 + i, :] = taps[i]
        turned[half * STATE : (half + 1) * STATE, :] = mat[...].T
    start = pl.multiple_of((lax.rem(row, 2) * count + lax.div(row, 2)) * ns, 16)
    b_col = turned[pl.ds(start, ns), :]
    c_col = turned[pl.ds(STATE + start, ns), :]
    cols[0:ns, :] = b_col
    cols[ns : 2 * ns, :] = c_col
    c_all = silu(c_col)
    misc = got[:, 0, base + 2 * LANES : base + 3 * LANES]
    falls_all = jnp.exp(misc)
    token = early[0:8, ROW_STEP * LANES : (ROW_STEP + 1) * LANES]
    token_falls = jnp.exp(token)
    for j in range(js):
        at = slice(j * LANES, (j + 1) * LANES)
        fall = head_lanes(falls_all, 32, j)
        falls = head_lanes(token_falls, 32, j)
        a = jnp.zeros((ns, LANES), F32)
        for p in reversed(range(count)):
            aft[p, :, at] = a
            a = fall[p : p + 1] * a + got[p, :, at]
        for s in (2, 1, 0):
            dy = early[j : j + 1, (ROW_DY + s) * LANES : (ROW_DY + s + 1) * LANES]
            a = a + dy * c_all[:, s : s + 1]
            adj[s, :, at] = a
            a = falls[s : s + 1] * a
        msg[j, ns : 2 * ns, :] = a
    pfall = jnp.exp(halves(misc[:, 0:1], misc[:, 1:2], (count, LANES)))
    state = jnp.zeros((ns, LANES), F32)
    for p in range(count):
        pst[p] = state
        state = pfall[p : p + 1] * state + got[p, :, base : base + LANES]
    for g in range(js):
        holder = lax.div(scal[g] - 1, span)
        mark = got[holder, 0:1, base + 2 * LANES : base + 3 * LANES]
        reach = reach_of(mark, g)
        at = slice((js + g) * LANES, (js + g + 1) * LANES)
        msg[g, 0:ns, :] = got[holder, :, at] + reach * pst[holder]
        for r in range(3):
            msg[g, 2 * ns + r : 2 * ns + r + 1, :] = early[
                g : g + 1, (TAIL_X + r) * LANES : (TAIL_X + r + 1) * LANES
            ]
        msg[g, 2 * ns + 3 : 2 * ns + 8, :] = jnp.zeros((5, LANES), F32)
    chip = lax.div(row, 2)
    for d, q in enumerate((q0, q1, q2, q3)):
        to = lax.rem(chip + d, count)
        q[:, : js * LANES] = aft[to]
        q[:, js * LANES :] = joined[pl.ds(pl.multiple_of(to * ns, ns), ns), :]


def chain_kernel(
    scal, got, moved, s0, s1, s2, s3, adj, pst, cols, early, convx, skip,
    msg, rows, injected, states,
):
    row = scal[17]
    first = (row == 0).astype(F32)
    count, ns = got.shape[0], got.shape[1]
    js = moved.shape[0]
    span = 2 * scal[19]
    b_col, c_col = cols[0:ns, :], cols[ns : 2 * ns, :]
    b_all, c_all = silu(b_col), silu(c_col)
    base = 2 * js * LANES
    wide = js * LANES
    for piece, first_row in by_chip(row, (s0, s1, s2, s3)):
        states[pl.ds(first_row, ns), :] = piece[:, js * LANES :]
    misc = got[:, 0, base + 2 * LANES : base + 3 * LANES]
    falls_all = jnp.exp(misc)
    token = early[0:8, ROW_STEP * LANES : (ROW_STEP + 1) * LANES]
    token_falls = jnp.exp(token)
    sum_b = [jnp.zeros((ns, LANES), F32) for _ in range(3)]
    sum_c = [jnp.zeros((ns, LANES), F32) for _ in range(3)]
    for j in range(js):
        at = slice(j * LANES, (j + 1) * LANES)
        fall = head_lanes(falls_all, 32, j)
        falls = head_lanes(token_falls, 32, j)
        steps = head_lanes(token, 0, j)
        seq = [moved[j, 2 * ns + r : 2 * ns + r + 1, :] for r in range(3)] + [
            early[j : j + 1, (ROW_X + s) * LANES : (ROW_X + s + 1) * LANES] for s in range(3)
        ]
        gain = skip[j : j + 1, :] * first
        state = moved[j, 0:ns, :]
        for s in range(3):
            dy = early[j : j + 1, (ROW_DY + s) * LANES : (ROW_DY + s + 1) * LANES]
            pre = sum(convx[i, j : j + 1, :] * seq[s + i] for i in range(4))
            sg = sigmoid(pre)
            x_conv = pre * sg
            x_hat = steps[s : s + 1] * x_conv
            state = falls[s : s + 1] * state + x_hat * b_all[:, s : s + 1]
            a = adj[s, :, at]
            rows[j : j + 1, s * LANES : (s + 1) * LANES] = (
                jnp.sum(state * c_all[:, s : s + 1], axis=0, keepdims=True) + gain * x_conv
            )
            grad = steps[s : s + 1] * jnp.sum(a * b_all[:, s : s + 1], axis=0, keepdims=True)
            rows[j : j + 1, (3 + s) * LANES : (4 + s) * LANES] = (
                sg * (1.0 + pre * (1.0 - sg)) * (grad + gain * dy)
            )
            sum_c[s] = sum_c[s] + dy * state
            sum_b[s] = sum_b[s] + x_hat * a
        for p in range(count):
            msg[p, :, (js + 9 + j) * LANES : (js + 10 + j) * LANES] = state
            state = fall[p : p + 1] * state + states[p * ns : (p + 1) * ns, at]
    lane = iota((ns, LANES), 1)
    back = jnp.zeros((ns, LANES), F32)
    for which, (total, column) in enumerate(((sum_b, b_col), (sum_c, c_col))):
        grads = [
            jnp.sum(total[s], axis=1, keepdims=True) * silu_slope(column[:, s : s + 1])
            for s in range(3)
        ]
        for m in range(3):
            tail = sum(grads[s] * column[:, 8 + m - s : 9 + m - s] for s in range(m + 1))
            back = jnp.where(lane == 3 * which + m, tail, back)
    pfall = jnp.exp(halves(misc[:, 0:1], misc[:, 1:2], (count, LANES)))
    injected[...] = jnp.zeros(injected.shape, F32)
    for g in range(js):
        holder = lax.div(scal[g] - 1, span)
        mark = got[holder, 0:1, base + 2 * LANES : base + 3 * LANES]
        reach = reach_of(mark, g)
        grad = moved[g, ns : 2 * ns, :]
        injected[holder] = injected[holder] + reach * grad
        for p in range(count):
            msg[p, :, g * LANES : (g + 1) * LANES] = grad
    a = jnp.zeros((ns, LANES), F32)
    for p in reversed(range(count)):
        msg[p, :, wide + LANES : wide + 2 * LANES] = a
        a = pfall[p : p + 1] * a + got[p, :, base + LANES : base + 2 * LANES] + injected[p]
    for p in range(count):
        msg[p, :, wide : wide + LANES] = pst[p]
        msg[p, :, wide + 2 * LANES : wide + 8 * LANES] = rows[...]
        msg[p, :, wide + 8 * LANES : wide + 9 * LANES] = back


def tail_grads(lead, taps):
    return [sum(lead[s] * taps[m - s] for s in range(m + 1)) for m in range(3)]


def assemble(core, mine, theirs, lanes, full):
    half = mine.shape[0]
    full[pl.ds(pl.multiple_of(core * half, half), half), :] = mine[:, lanes]
    full[pl.ds(pl.multiple_of((1 - core) * half, half), half), :] = theirs[:, lanes]


def first_rows(mine, theirs, js, rows):
    at = slice((js + 2) * LANES, (js + 8) * LANES)
    total = mine[0:js, at] + theirs[0:js, at]
    for p in range(1, mine.shape[0] // js):
        total = total + mine[p * js : (p + 1) * js, at] + theirs[p * js : (p + 1) * js, at]
    rows[...] = total


def inner_kernel(
    scal, bx, bbc, rim, convx, convbc, skip, dys, table, wrow,
    smine, sother, yi, gi, rise,
    xs, xt, ds, bcs, out,
):
    row = scal[17]
    n, js = bx.shape[0], bx.shape[1]
    conv_branch(bx, rim, convx, xs, xt, ds)
    taps = [convbc[i : i + 1, :] for i in range(4)]
    bc = silu(conv_rows(bbc[...], bc_halo(rim, 19), taps, bcs))
    b, c = bc[:, :STATE], bc[:, STATE:]
    b_t = left(b.T)
    scores = mm_nt(left(c), right_nt(b))
    scores_t = mm_nt(left(b), right_nt(c))
    causal = iota((n, n), 0) >= iota((n, n), 1)
    causal_t = iota((n, n), 0) <= iota((n, n), 1)
    low = iota((n, LANES), 1) < HEAD_DIM

    runs = table[...]
    fall = jnp.exp(runs[n - 1 : n, :] - runs)
    faded = []
    for j in range(js):
        at = pl.ds(j, n, stride=js)
        steps = head_lanes(runs, 0, j)
        x_conv = xt[at, :]
        dy = dys[at, :]
        gain = skip[j : j + 1, :]
        x_hat = x_conv * steps
        x_hi, x_lo = split2(x_hat)
        dy_b = dy.astype(BF16)
        zero = jnp.zeros_like(dy_b)
        faded.append(x_hat * head_lanes(fall, 32, j))
        if j % 2 == 1:
            out[:, (j - 1) * LANES : (j + 1) * LANES] = mm(
                b_t, right(jnp.concatenate(faded[-2:], axis=1))
            )
        mix, mix_t = [], []
        for k in range(2):
            down = jnp.broadcast_to(runs[:, 32 + 2 * j + k : 33 + 2 * j + k], (n, n))
            along = wrow[2 * j + k : 2 * j + k + 1, :]
            mix.append(split2(jnp.exp(jnp.where(causal, down - along, -1e30)) * scores))
            mix_t.append(split2(jnp.exp(jnp.where(causal_t, along - down, -1e30)) * scores_t))
        x_blk = [jnp.where(low, x_hi, zero), jnp.where(low, zero, x_hi)]
        x_rest = [jnp.where(low, x_lo, zero), jnp.where(low, zero, x_lo)]
        d_blk = [jnp.where(low, dy_b, zero), jnp.where(low, zero, dy_b)]
        y = mm(
            jnp.concatenate([mix[0][0], mix[1][0], mix[0][0], mix[1][0], mix[0][1], mix[1][1]], 1),
            jnp.concatenate(x_blk + x_rest + x_blk, 0),
        )
        yi[at, :] = y + gain * x_conv
        g = mm(
            jnp.concatenate([mix_t[0][0], mix_t[1][0], mix_t[0][1], mix_t[1][1]], 1),
            jnp.concatenate(d_blk + d_blk, 0),
        )
        slope = ds[at, :]
        gi[at, :] = (steps * g + gain * dy) * slope
        rise[at, :] = steps * slope * head_lanes(fall, 32, j)
    for h, half_out in enumerate((smine, sother)):
        half_out[...] = out[part(h, row), :]


def carry_kernel(
    scal, bbc, rim, convx, convbc, yi, gi, rise, table, rows, fmine, ftheirs,
    by, bgx, last, rims,
    xs, ys, bcs, start, after,
):
    row, length = scal[17], scal[16]
    n, js = by.shape[0], by.shape[1]
    core = lax.rem(row, 2)
    assemble(core, fmine, ftheirs, slice(0, js * LANES), start)
    assemble(core, fmine, ftheirs, slice(js * LANES, 2 * js * LANES), after)
    taps = [convbc[i : i + 1, :] for i in range(4)]
    bc = silu(conv_rows(bbc[...], bc_halo(rim, 19), taps, bcs))
    b_l, c_l = left(bc[:, :STATE]), left(bc[:, STATE:])
    xs[n * js : (n + 8) * js, :] = jnp.zeros((8 * js, LANES), F32)

    grown = jnp.exp(table[...])
    for j in range(0, js, 2):
        both = slice(j * LANES, (j + 2) * LANES)
        y = mm(c_l, right(start[:, both]))
        g = mm(b_l, right(after[:, both]))
        for q in range(2):
            at = pl.ds(j + q, n, stride=js)
            half = slice(q * LANES, (q + 1) * LANES)
            ys[at, :] = yi[at, :] + head_lanes(grown, 32, j + q) * y[:, half]
            xs[at, :] = gi[at, :] + rise[at, :] * g[:, half]

    @pl.when(row == 0)
    def _():
        for s in range(3):
            ys[s * js : (s + 1) * js, :] = rows[:, s * LANES : (s + 1) * LANES]
            xs[s * js : (s + 1) * js, :] = rows[:, (3 + s) * LANES : (4 + s) * LANES]

    def finish(c, _):
        at = pl.multiple_of(c * 16 * js, 16 * js)
        pos = row * n + c * 16 + iota((16, js, LANES), 0)
        y = ys[pl.ds(at, 16 * js), :].reshape(16, js, LANES)
        by[pl.ds(c * 16, 16)] = jnp.where(pos < length, y, 0.0).astype(BF16)
        g = jnp.zeros((16, js, LANES), F32)
        for i in range(4):
            g = g + convx[i][None] * xs[pl.ds(at + (3 - i) * js, 16 * js), :].reshape(
                16, js, LANES
            )
        bgx[pl.ds(c * 16, 16)] = g.astype(BF16)
        return 0

    lax.fori_loop(0, n // 16, finish, 0)
    for m in range(3):
        at = n - 3 + m
        last[m] = sum(
            convx[i] * xs[(at + 3 - i) * js : (at + 4 - i) * js, :] for i in range(4)
        )
    taps_x = [convx[i] for i in range(4)]
    for m, g in enumerate(tail_grads([xs[s * js : (s + 1) * js, :] for s in range(3)], taps_x)):
        rims[m, 0:js, :] = g


def prompt_inner_kernel(
    scal, px, pbc, pdy, rim, convx, convbc, skip, tab, prun,
    yp, gp, dbp, dcp, xh, xpre, bcpre, pxs, pbcs,
):
    col = scal[18]
    span = px.shape[0]
    taps = [convbc[i : i + 1, :] for i in range(4)]
    own = [convx[i, pl.ds(col, 1), :] for i in range(4)]
    gain = skip[pl.ds(col, 1), :]
    x_pre = conv_rows(px[...], [rim[r, 16:17, :] for r in range(3)], own, pxs)
    bc_pre = conv_rows(pbc[...], bc_halo(rim, 17), taps, pbcs)
    xpre[...] = x_pre
    bcpre[...] = bc_pre
    x_p = silu(x_pre)
    bc_p = silu(bc_pre)
    b_p, c_p = bc_p[:, :STATE], bc_p[:, STATE:]
    scores = mm_nt(left(c_p), right_nt(b_p))
    scores_t = mm_nt(left(b_p), right_nt(c_p))
    ptable = tab[...]
    steps = halves(ptable[:, 2:3], ptable[:, 3:4], (span, LANES))
    x_hat = x_p * steps
    xh[...] = x_hat
    x_hi, x_lo = split2(x_hat)
    dy_b = pdy[...]
    low = iota((span, LANES), 1) < HEAD_DIM
    zero = jnp.zeros_like(x_hi)
    causal = iota((span, span), 0) >= iota((span, span), 1)
    causal_t = iota((span, span), 0) <= iota((span, span), 1)
    y = gain * x_p
    g = jnp.zeros((span, LANES), F32)
    d_s = jnp.zeros((span, span), F32)
    d_st = jnp.zeros((span, span), F32)
    for k in range(2):
        keep = low if k == 0 else jnp.logical_not(low)
        xk_hi, xk_lo = jnp.where(keep, x_hi, zero), jnp.where(keep, x_lo, zero)
        dk = jnp.where(keep, dy_b, zero)
        down = jnp.broadcast_to(ptable[:, k : k + 1], (span, span))
        along = prun[k : k + 1, :]
        decay = jnp.exp(jnp.where(causal, down - along, -1e30))
        decay_t = jnp.exp(jnp.where(causal_t, along - down, -1e30))
        m_hi, m_lo = split2(decay * scores)
        t_hi, t_lo = split2(decay_t * scores_t)
        y = y + mm(
            jnp.concatenate([m_hi, m_hi, m_lo], 1), jnp.concatenate([xk_hi, xk_lo, xk_hi], 0)
        )
        g = g + mm(jnp.concatenate([t_hi, t_lo], 1), jnp.concatenate([dk, dk], 0))
        d_two = jnp.concatenate([dk, dk], 1)
        x_two = jnp.concatenate([x_hi, x_lo], 1)
        d_s = d_s + decay * mm_nt(d_two, x_two)
        d_st = d_st + decay_t * mm_nt(x_two, d_two)
    yp[...] = y
    gp[...] = g
    dcp[...] = mm(left(d_s), right(b_p))
    dbp[...] = mm(left(d_st), right(c_p))


def prompt_kernel(
    scal, pdy, convx, convbc, skip, tab, yp, gp, dbp, dcp, xh, xpre, bcpre,
    mine, theirs, keep_mine, keep_theirs, keep_far,
    py, pgx, msg, rims, rows,
    pxs, pbcs, wexp, dxh, dbs, got, tail, near,
):
    row, col = scal[17], scal[18]
    span, js = pdy.shape[0], convx.shape[1]
    base = js * LANES
    core = lax.rem(row, 2)
    assemble(core, mine, theirs, slice(0, base + 2 * LANES), got)
    assemble(core, mine, theirs, slice(base + 8 * LANES, base + 9 * LANES), tail)
    near[part(0, row), :] = keep_theirs[...]
    near[part(1, row), :] = keep_far[...]
    first_rows(mine, theirs, js, rows)
    mark = keep_theirs[0:1, 2 * LANES : 3 * LANES]
    fall = jnp.exp(halves(mark[:, 0:1], mark[:, 1:2], (1, LANES)))
    begin, end = slice(base, base + LANES), slice(base + LANES, base + 2 * LANES)

    @pl.when(core == 1)
    def _():
        got[:, begin] = near[:, :LANES] + fall * got[:, begin]

    @pl.when(core == 0)
    def _():
        got[:, end] = near[:, LANES : 2 * LANES] + fall * got[:, end]
        for g in range(js):

            @pl.when(in_odd(scal, g, span))
            def _():
                got[:, end] += reach_of(mark, g) * got[:, g * LANES : (g + 1) * LANES]

    taps_x = [convx[i] for i in range(4)]
    fork_lead = [rows[:, (3 + s) * LANES : (4 + s) * LANES] for s in range(3)]
    chunk = span // js
    for m, v in enumerate(tail_grads(fork_lead, taps_x)):
        for q in range(js):
            msg[q, 2 * chunk + m : 2 * chunk + m + 1, :] = v[q : q + 1]
    taps = [convbc[i : i + 1, :] for i in range(4)]
    own = [convx[i, pl.ds(col, 1), :] for i in range(4)]
    gain = skip[pl.ds(col, 1), :]
    x_hat = xh[...]
    bc_p = silu(bcpre[...])
    b_l, c_l = left(bc_p[:, :STATE]), left(bc_p[:, STATE:])
    ptable = tab[...]
    runs = halves(ptable[:, 0:1], ptable[:, 1:2], (span, LANES))
    steps = halves(ptable[:, 2:3], ptable[:, 3:4], (span, LANES))
    wexp[...] = runs
    dy = pdy[...].astype(F32)
    grown = jnp.exp(runs)
    rest = jnp.exp(runs[span - 1 : span, :] - runs)
    py[...] = (yp[...] + grown * mm(c_l, right(got[:, begin]))).astype(BF16)
    dxh[...] = gp[...] + rest * mm(b_l, right(got[:, end]))
    d_c = dcp[...] + mm_nt(left(grown * dy), right_nt(got[:, begin]))
    dbs[...] = dbp[...] + mm_nt(left(rest * x_hat), right_nt(got[:, end]))

    def fork(q, _):
        where = scal[q] - 1 - row * span

        @pl.when((where >= 0) & (where < span))
        def _():
            gap = wexp[pl.ds(where, 1), :] - wexp[...]
            u = jnp.exp(jnp.where(iota((span, LANES), 0) <= where, gap, -1e30))
            grad = got[:, block(q)]
            dxh[...] += u * mm(b_l, right(grad))
            dbs[...] += mm_nt(left(u * xh[...]), right_nt(grad))

        return 0

    lax.fori_loop(0, js, fork, 0)
    pxs[0:span, :] = (steps * dxh[...] + gain * dy) * silu_slope(xpre[...])
    pxs[span : span + 8, :] = jnp.zeros((8, LANES), F32)
    pgx[...] = sum(own[i] * pxs[3 - i : 3 - i + span, :] for i in range(4))
    for m, v in enumerate(tail_grads([pxs[s : s + 1, :] for s in range(3)], own)):
        rims[m, 0:1, :] = v
    pbcs[0:span, :] = jnp.concatenate([dbs[...], d_c], axis=1) * silu_slope(bcpre[...])
    pbcs[span : span + 8, :] = jnp.zeros((8, 2 * STATE), F32)
    grad = sum(taps[i] * pbcs[3 - i : 3 - i + span, :] for i in range(4))
    for m, v in enumerate(tail_grads([pbcs[s : s + 1, :] for s in range(3)], taps)):
        rims[m, 1:2, :] = v[:, :STATE]
        rims[m, 2:3, :] = v[:, STATE:]
    spot = iota((span, LANES), 0) - (scal[20] - 3 - row * span)
    lane = iota((span, LANES), 1)
    tails = exact(tail[...])
    for half in range(2):
        hit = ((spot >= 0) & (spot < 3) & (lane == spot + 3 * half)).astype(F32).astype(BF16)
        into = mm_nt(jnp.concatenate([hit, hit, hit], 1), tails)
        total = grad[:, half * STATE : (half + 1) * STATE] + into
        for q in range(js):
            msg[q, half * chunk : (half + 1) * chunk, :] = total[
                q * chunk : (q + 1) * chunk
            ]
    for q in range(js):
        msg[q, 2 * chunk + 3 : 2 * chunk + 8, :] = jnp.zeros((5, LANES), F32)


def rim_kernel(msg, back, out):
    rows = (msg.shape[1] - 8) // 2
    out[...] = msg[...]
    for m in range(3):
        for half in range(2):
            at = (half + 1) * rows - 3 + m
            out[0, at : at + 1, :] = msg[0, at : at + 1, :] + back[m, 1 + half : 2 + half, :]


def finish_kernel(scal, pgx, back, got, out_x, out_bc, tails):
    row = scal[17]
    span, peers = pgx.shape[0], got.shape[0]
    rows = span // peers
    total = got[0, 0 : 2 * rows, :]
    for p in range(1, peers):
        total = total + got[p, 0 : 2 * rows, :]
    out_bc[:, :STATE] = total[0:rows].astype(BF16)
    out_bc[:, STATE:] = total[rows : 2 * rows].astype(BF16)
    lane = iota((1, LANES), 1)
    spot = jnp.full((1, LANES), -1, jnp.int32)
    tails[...] = jnp.zeros((LANES, LANES), F32)
    for g in range(peers):
        tails[8 * g : 8 * g + 8, :] = got[g, 2 * rows : 2 * rows + 8, :]
        where = scal[g] - 3 - row * span + lane - 8 * g
        spot = jnp.where((lane >= 8 * g) & (lane < 8 * g + 3), where, spot)
    hit = (iota((span, LANES), 0) == spot).astype(F32).astype(BF16)
    into = mm(jnp.concatenate([hit, hit, hit], 1), jnp.concatenate(split3(tails[...]), 0))
    total = pgx[...] + into
    where = iota((span, LANES), 0)
    for m in range(3):
        total = total + jnp.where(where == span - 3 + m, back[m, 0:1, :], 0.0)
    out_x[...] = total.astype(BF16)


def call(
    kernel, args, outs, scratch, scalars=1, flops=10**9, blocks=None, out_smem=0,
    out_blocks=None, aliases=None,
):
    vmem = pl.BlockSpec(memory_space=pltpu.VMEM)
    smem = pl.BlockSpec(memory_space=pltpu.SMEM)
    given = [smem] * scalars + [vmem] * (len(args) - scalars)
    for at, spec in (blocks or {}).items():
        given[at] = spec
    taken = [smem] * out_smem + [vmem] * (len(outs) - out_smem)
    for at, spec in (out_blocks or {}).items():
        taken[at] = spec
    return pl.pallas_call(
        kernel,
        grid=(1,) if blocks else (),
        out_shape=[jax.ShapeDtypeStruct(s, d) for s, d in outs],
        in_specs=given,
        out_specs=taken,
        input_output_aliases=aliases or {},
        scratch_shapes=[pltpu.VMEM(s, F32) for s in scratch],
        compiler_params=pltpu.CompilerParams(vmem_limit_bytes=VMEM_LIMIT),
        cost_estimate=pl.CostEstimate(flops=flops, bytes_accessed=10**6, transcendentals=0),
    )(*args)


def shards(
    prompt_x,
    prompt_bc,
    prompt_dt,
    branch_x,
    branch_bc,
    branch_dt,
    conv_x,
    conv_bc,
    a_log,
    dt_bias,
    d_skip,
    lengths,
    forks,
    holder,
    prompt_dy,
    branch_dy,
):
    count = lax.axis_size("prefix")
    js = lax.axis_size("branch")
    span = prompt_x.shape[0]
    n = branch_x.shape[1]
    heads = 2 * js
    ns = STATE // count
    chips = count // 2
    half = STATE // 2
    px = prompt_x.reshape(span, LANES)
    pbc = prompt_bc.reshape(span, 2 * STATE)
    pdt = prompt_dt.reshape(2, span)
    pdy = prompt_dy.reshape(span, LANES)
    bx = branch_x.reshape(n, js, LANES)
    bbc = branch_bc.reshape(n, 2 * STATE)
    bdt = branch_dt.reshape(heads, n)
    bdy = branch_dy.reshape(n, js, LANES)
    convx = conv_x.reshape(4, js, LANES)
    convbc = conv_bc.reshape(4, 2 * STATE)
    a_pair, bias_pair, skip_pair = (
        jnp.transpose(v.reshape(js, 2)) for v in (a_log, dt_bias, d_skip)
    )
    cores = [(i, i ^ 1) for i in range(count)]
    columns = [[i for i in range(count) if i % 2 == c] for c in range(2)]

    with jax.named_scope("setup"):
        scal, rim, step, logs, pstep, plogs, skip = call(
            setup_kernel,
            [forks, lengths, holder, bx, px, pbc, bbc, a_pair, bias_pair, skip_pair, bdt, pdt],
            [
                ((24,), jnp.int32),
                ((3, js + 5, LANES), F32),
                ((heads, n), F32),
                ((heads, n), F32),
                ((2, span), F32),
                ((2, span), F32),
                ((js, LANES), F32),
            ],
            [],
            scalars=3,
            out_smem=1,
            blocks={
                3: pl.BlockSpec((16, js, LANES), lambda i: (n // 16 - 1, 0, 0)),
                4: pl.BlockSpec((16, LANES), lambda i: (span // 16 - 1, 0)),
                5: pl.BlockSpec((16, 2 * STATE), lambda i: (span // 16 - 1, 0)),
                6: pl.BlockSpec((16, 2 * STATE), lambda i: (n // 16 - 1, 0)),
            },
        )
    rim = lax.ppermute(rim, "prefix", [(i, i + 1) for i in range(count - 1)])
    big = (n * js, LANES)
    tall = ((n + 8) * js, LANES)
    each = (half, js * LANES)
    piece = (ns, 2 * js * LANES)

    def across(v):
        return lax.ppermute(v, "prefix", cores)

    def round_chips(blocks):
        moved_on = [blocks[0]]
        for d in range(1, chips):
            pairs = [(i, (i + 2 * d) % count) for i in range(count)]
            moved_on.append(lax.ppermute(blocks[d], "prefix", pairs))
        return moved_on

    def between_chips(v):
        return lax.all_to_all(v, "prefix", 0, 0, axis_index_groups=columns, tiled=True)

    with jax.named_scope("early"):
        early_part, dys, table, run, tab, prun = call(
            early_kernel,
            [scal, px, pbc, pstep, plogs, bx, bbc, step, logs, bdy],
            [
                ((js, EARLY * LANES), F32),
                (big, F32),
                ((n, LANES), F32),
                ((heads, n), F32),
                ((span, LANES), F32),
                ((2, span), F32),
            ],
            [],
            blocks={
                5: pl.BlockSpec((16, js, LANES), lambda i: (0, 0, 0)),
                6: pl.BlockSpec((16, 2 * STATE), lambda i: (0, 0)),
            },
        )
    width = (2 * js + 3 + EARLY) * LANES
    with jax.named_scope("lead"):
        mine, other = call(
            lead_kernel,
            [
                scal, px, pbc, pdy, bbc, rim, convx, convbc, early_part, dys, table, tab,
            ],
            [((half, width), F32)] * 2,
            [
                (n + 8, 2 * STATE), (span + 8, LANES), (span + 8, 2 * STATE),
                (span, LANES), (STATE, (2 * js + 3) * LANES),
            ],
        )
    theirs = across(other)
    with jax.named_scope("chip"):
        joined, keep_mine, keep_theirs = call(
            chip_kernel,
            [scal, mine, theirs],
            [((half, width), F32)] + [((half, 3 * LANES), F32)] * 2,
            [],
        )
    got = between_chips(joined.reshape(chips, ns, width))
    with jax.named_scope("inner"):
        smine, sother, yi, gi, rise = call(
            inner_kernel,
            [scal, bx, bbc, rim, convx, convbc, skip, dys, table, run],
            [(each, F32)] * 2 + [(big, F32)] * 3,
            [tall, big, big, (n + 8, 2 * STATE), (STATE, js * LANES)],
            flops=10**10,
        )
    stheirs = across(sother)
    keep_far = across(keep_mine)
    with jax.named_scope("join_states"):
        (sjoined,) = call(
            join_states_kernel, [scal, keep_mine, keep_theirs, smine, stheirs], [(each, F32)], []
        )
    got, keep_far = lax.optimization_barrier((got, keep_far))
    with jax.named_scope("slices"):
        msg, adj, pst, cols, early, *ablocks = call(
            slice_kernel,
            [scal, got, convbc, sjoined],
            [
                ((js, 2 * ns + 8, LANES), F32),
                ((3, ns, js * LANES), F32),
                ((chips, ns, LANES), F32),
                ((2 * ns, LANES), F32),
                ((ns, EARLY * LANES), F32),
            ]
            + [(piece, F32)] * 4,
            [(LANES, LANES), (2 * STATE, LANES), (chips, ns, js * LANES)],
        )
    moved = lax.all_to_all(msg, "branch", 0, 0, tiled=True)
    agot = round_chips(ablocks)
    moved, *agot = lax.optimization_barrier((moved, *agot))
    width3 = (js + 9) * LANES
    with jax.named_scope("chains"):
        (msg3,) = call(
            chain_kernel,
            [scal, got, moved, *agot, adj, pst, cols, early, convx, skip],
            [((chips, ns, width3 + js * LANES), F32)],
            [(js, 6 * LANES), (chips, ns, LANES), each],
        )
    msg3, tab3 = lax.optimization_barrier((msg3, tab))
    got3 = between_chips(msg3).reshape(half, width3 + js * LANES)
    narrow = ((span, LANES), F32)
    wide2 = ((span, 2 * STATE), F32)
    with jax.named_scope("prompt_inner"):
        inner_parts = call(
            prompt_inner_kernel,
            [scal, px, pbc, pdy, rim, convx, convbc, skip, tab3, prun],
            [narrow] * 6 + [wide2],
            [(span + 8, LANES), (span + 8, 2 * STATE)],
            flops=10**10,
        )
    got3, *inner_parts = lax.optimization_barrier((got3, *inner_parts))
    theirs3 = across(got3)
    both = (half, 2 * js * LANES)
    with jax.named_scope("spread_branch"):
        fmine, fother = call(
            spread_branch_kernel,
            [scal, got3, *agot, mine, theirs, smine, stheirs],
            [(both, F32)] * 2,
            [each],
        )
    theirs3, fother = lax.optimization_barrier((theirs3, fother))
    ftheirs = across(fother)
    peers = (js, 2 * span // js + 8, LANES)
    with jax.named_scope("prompt"):
        py, pgx, out_msg, prims, rows = call(
            prompt_kernel,
            [
                scal, pdy, convx, convbc, skip, tab, *inner_parts,
                got3, theirs3, keep_mine, keep_theirs, keep_far,
            ],
            [
                ((span, LANES), BF16),
                narrow,
                (peers, F32),
                ((3, 3, LANES), F32),
                ((js, 6 * LANES), F32),
            ],
            [
                (span + 8, LANES), (span + 8, 2 * STATE), (span, LANES),
                (span, LANES), (span, STATE), (STATE, (js + 2) * LANES), (STATE, LANES),
                (STATE, 3 * LANES),
            ],
        )
    backward = [(i, i - 1) for i in range(1, count)]
    pback = lax.ppermute(prims, "prefix", backward)
    final = pl.BlockSpec((1,) + peers[1:], lambda i: (js - 1, 0, 0))
    with jax.named_scope("rim"):
        (out_msg,) = call(
            rim_kernel,
            [out_msg, pback],
            [(peers, F32)],
            [],
            scalars=0,
            blocks={0: final},
            out_blocks={0: final},
            aliases={0: 0},
        )
    end = lax.all_to_all(out_msg, "branch", 0, 0, tiled=True)
    with jax.named_scope("carry"):
        by, bgx, last, brims = call(
            carry_kernel,
            [
                scal, bbc, rim, convx, convbc, yi, gi, rise, table, rows, fmine, ftheirs,
            ],
            [
                ((n, js, LANES), BF16),
                ((n, js, LANES), BF16),
                ((3, js, LANES), F32),
                ((3, js, LANES), F32),
            ],
            [
                tall, big, (n + 8, 2 * STATE), (STATE, js * LANES), (STATE, js * LANES),
            ],
            flops=10**10,
        )
    bback = lax.ppermute(brims, "prefix", backward)
    bgx = bgx.at[-3:].set((last + bback).astype(BF16))
    with jax.named_scope("finish"):
        prompt_gx, prompt_gbc = call(
            finish_kernel,
            [scal, pgx, pback, end],
            [((span, LANES), BF16), ((span // js, 2 * STATE), BF16)],
            [(LANES, LANES)],
        )
    return (
        py.reshape(prompt_x.shape),
        by.reshape(branch_x.shape),
        prompt_gx.reshape(prompt_x.shape),
        bgx.reshape(branch_x.shape),
        prompt_gbc.reshape(span // js, 1, 2 * STATE),
    )


def solution(mesh):
    return jax.shard_map(
        shards,
        mesh=mesh,
        in_specs=(
            P("prefix", "branch", "tensor", None),
            P("prefix", "tensor", None),
            P("branch", "tensor", None, "prefix"),
            P("branch", "prefix", None, "tensor", None),
            P("branch", "prefix", "tensor", None),
            P("branch", None, "tensor", None, "prefix"),
            P(None, None, "tensor", None),
            P(None, "tensor", None),
            P(None, "tensor", None),
            P(None, "tensor", None),
            P(None, "tensor", None),
            P(),
            P(),
            P(),
            P("prefix", "branch", "tensor", None),
            P("branch", "prefix", None, "tensor", None),
        ),
        out_specs=(
            P("prefix", "branch", "tensor", None),
            P("branch", "prefix", None, "tensor", None),
            P("prefix", "branch", "tensor", None),
            P("branch", "prefix", None, "tensor", None),
            P(("prefix", "branch"), "tensor", None),
        ),
        check_vma=False,
    )
```

```python
import functools

import jax
import jax.numpy as jnp
from jax import lax
from jax.experimental import pallas as pl
from jax.experimental.pallas import tpu as pltpu
from jax.sharding import PartitionSpec as P

HEAD_DIM = 64
STATE = 128
LANES = 128

F32 = jnp.float32
BF16 = jnp.bfloat16

TAIL_X = 0
ROW_X = 3
ROW_DY = 6
ROW_BC = 9
ROW_STEP = 10
EARLY = 11

VMEM_LIMIT = 56 * 1024 * 1024
VMEM_SMALL = 20 * 1024 * 1024


def split2(a):
    hi = a.astype(BF16)
    return hi, (a - hi.astype(F32)).astype(BF16)


def split3(a):
    hi = a.astype(BF16)
    rest = a - hi.astype(F32)
    mid = rest.astype(BF16)
    return hi, mid, (rest - mid.astype(F32)).astype(BF16)


def mm(a, b):
    return lax.dot_general(a, b, (((1,), (0,)), ((), ())), preferred_element_type=F32)


def mm_nt(a, b):
    return lax.dot_general(a, b, (((1,), (1,)), ((), ())), preferred_element_type=F32)


def left(a):
    hi, lo = split2(a)
    return jnp.concatenate([hi, hi, lo], axis=1)


def right(b):
    hi, lo = split2(b)
    return jnp.concatenate([hi, lo, hi], axis=0)


def right_nt(b):
    hi, lo = split2(b)
    return jnp.concatenate([hi, lo, hi], axis=1)


def exact(a):
    return jnp.concatenate(split3(a), axis=1)


def iota(shape, dim):
    return lax.broadcasted_iota(jnp.int32, shape, dim)


def picker(base, j):
    one = (iota((LANES, LANES), 0) == base + 2 * j + iota((LANES, LANES), 1) // HEAD_DIM).astype(
        F32
    ).astype(BF16)
    return jnp.concatenate([one, one, one], axis=0)


def running_sum(logs):
    size = logs.shape[1]
    upper = (iota((size, size), 0) <= iota((size, size), 1)).astype(F32).astype(BF16)
    return mm(exact(logs), jnp.concatenate([upper, upper, upper], axis=0))


def block(j):
    return pl.ds(pl.multiple_of(j * LANES, LANES), LANES)


def sigmoid(x):
    return 1.0 / (1.0 + jnp.exp(-x))


def head_column(pair, heads):
    shape = (heads, heads // 2)
    r = iota(shape, 0)
    both = jnp.where(r % 2 == 0, pair[0:1], pair[1:2])
    return jnp.sum(jnp.where(iota(shape, 1) == r // 2, both, 0.0), axis=1, keepdims=True)


def softplus(x):
    return jnp.maximum(x, 0.0) + jnp.log1p(jnp.exp(-jnp.abs(x)))


def setup_kernel(
    forks, lengths, holder, bx, px, pbc, bbc, alog, bias, gain, bdt, pdt,
    scal, rim, step, logs, pstep, plogs, skip,
):
    row, col = lax.axis_index("prefix"), lax.axis_index("branch")
    js = bx.shape[1]

    def place(b, _):
        group = lax.fori_loop(
            0, js, lambda c, t: t + (holder[c] < holder[b]).astype(jnp.int32), jnp.int32(0),
            unroll=16,
        )
        scal[group] = forks[b]

        @pl.when(group == col)
        def _():
            scal[16] = lengths[b]
            scal[20] = forks[b]

        return 0

    lax.fori_loop(0, js, place, 0)
    scal[17] = row
    scal[18] = col
    scal[19] = pdt.shape[1]
    last = bx.shape[0] - 3
    xl = px[...].astype(F32)
    bcl = pbc[...].astype(F32)
    bbl = bbc[...].astype(F32)
    for r in range(3):
        rim[r, 0:js, :] = bx[last + r].astype(F32)
        at = slice(last + r, last + r + 1)
        rim[r, js : js + 1, :] = xl[at]
        rim[r, js + 1 : js + 2, :] = bcl[at, :STATE]
        rim[r, js + 2 : js + 3, :] = bcl[at, STATE:]
        rim[r, js + 3 : js + 4, :] = bbl[at, :STATE]
        rim[r, js + 4 : js + 5, :] = bbl[at, STATE:]
    heads = bdt.shape[0]
    s = softplus(bdt[...] + head_column(bias[...], heads))
    step[...] = s
    logs[...] = -jnp.exp(head_column(alog[...], heads)) * s
    own = iota((2, js), 1) == col
    own_bias = jnp.sum(jnp.where(own, bias[...], 0.0), axis=1, keepdims=True)
    own_rate = jnp.exp(jnp.sum(jnp.where(own, alog[...], 0.0), axis=1, keepdims=True))
    s = softplus(pdt[...] + own_bias)
    pstep[...] = s
    plogs[...] = -own_rate * s
    diag = iota((js, js), 0) == iota((js, js), 1)
    first = jnp.sum(jnp.where(diag, gain[0:1], 0.0), axis=1, keepdims=True)
    second = jnp.sum(jnp.where(diag, gain[1:2], 0.0), axis=1, keepdims=True)
    skip[...] = halves(first, second, (js, LANES))


def conv_branch(bx, rim, convx, xs, xt, ds):
    js = bx.shape[1]
    for r in range(3):
        xs[(5 + r) * js : (6 + r) * js, :] = rim[r, 0:js, :]

    def fill(c, _):
        xs[pl.ds(pl.multiple_of(8 * js + c * 16 * js, 16 * js), 16 * js), :] = (
            bx[pl.ds(c * 16, 16)].astype(F32).reshape(16 * js, LANES)
        )
        return 0

    lax.fori_loop(0, bx.shape[0] // 16, fill, 0)

    def one(c, _):
        pre = jnp.zeros((16, js, LANES), F32)
        for i in range(4):
            start = pl.multiple_of((5 + i) * js + c * 16 * js, js)
            pre = pre + convx[i][None] * xs[pl.ds(start, 16 * js), :].reshape(16, js, LANES)
        sg = sigmoid(pre)
        at = pl.ds(pl.multiple_of(c * 16 * js, 16 * js), 16 * js)
        xt[at, :] = (pre * sg).reshape(16 * js, LANES)
        if ds is not None:
            ds[at, :] = (sg * (1.0 + pre * (1.0 - sg))).reshape(16 * js, LANES)
        return 0

    lax.fori_loop(0, bx.shape[0] // 16, one, 0)


def conv_rows(raw, halo_rows, taps, scratch):
    n = raw.shape[0]
    scratch[8 : 8 + n, :] = raw.astype(F32)
    for r in range(3):
        scratch[5 + r : 6 + r, :] = halo_rows[r]
    pre = jnp.zeros(raw.shape, F32)
    for i in range(4):
        pre = pre + taps[i] * scratch[5 + i : 5 + i + n, :]
    return pre


def bc_halo(rim, first):
    return [
        jnp.concatenate([rim[r, first : first + 1, :], rim[r, first + 1 : first + 2, :]], axis=1)
        for r in range(3)
    ]


def silu(x):
    return x * sigmoid(x)


def silu_slope(x):
    sg = sigmoid(x)
    return sg * (1.0 + x * (1.0 - sg))


def without_first(row, values):
    return jnp.where((row == 0) & (iota(values.shape, 1) < 3), 0.0, values)


def branch_table(step, run):
    return jnp.concatenate([step, run, jnp.zeros((64, LANES), F32)], axis=0).T


def prompt_table(step, run):
    n = step.shape[1]
    r = iota((LANES, n), 0)
    runs = jnp.where(r % 2 == 0, run[0:1], run[1:2])
    steps = jnp.where(r % 2 == 0, step[0:1], step[1:2])
    return jnp.where((r == 2) | (r == 3), steps, runs).T


def halves(first, second, shape):
    return jnp.where(iota(shape, 1) < HEAD_DIM, first, second)


def part(h, row):
    half = STATE // 2
    core = lax.rem(row, 2)
    return pl.ds(pl.multiple_of((core if h == 0 else 1 - core) * half, half), half)


def live_dy(row, length, bdy, dys):
    n, js = bdy.shape[0], bdy.shape[1]

    def fill(c, _):
        pos = row * n + c * 16 + iota((16, js, LANES), 0)
        dead = (pos >= length) | (pos < 3)
        dys[pl.ds(pl.multiple_of(c * 16 * js, 16 * js), 16 * js), :] = jnp.where(
            dead, 0.0, bdy[pl.ds(c * 16, 16)].astype(F32)
        ).reshape(16 * js, LANES)
        return 0

    lax.fori_loop(0, n // 16, fill, 0)


def early_kernel(
    scal, px, pbc, pstep, plogs, bx, bbc, bstep, blogs, bdy,
    early, dys, table, run, ptable, prun,
):
    row, length = scal[17], scal[16]
    js = bdy.shape[1]
    span = px.shape[0]
    live_dy(row, length, bdy, dys)
    step, logs = bstep[...], blogs[...]
    sums = running_sum(without_first(row, logs))
    run[...] = sums
    table[...] = branch_table(without_first(row, step), sums)
    sums = running_sum(plogs[...])
    prun[...] = sums
    ptable[...] = prompt_table(pstep[...], sums)
    first = (row == 0).astype(F32)
    lane2 = iota((js, span), 1)
    spot = jnp.zeros((js, span), jnp.int32)
    for g in range(js):
        spot = jnp.where(iota((js, span), 0) == g, scal[g] - 3 - row * span, spot)
    hits = jnp.concatenate([(lane2 == spot + r).astype(F32).astype(BF16) for r in range(3)], 0)
    tails = mm(hits, px[...])
    own_spot = scal[20] - 3 - row * span + iota((js, span), 0)
    hit = ((lane2 == own_spot) & (iota((js, span), 0) < 3)).astype(F32).astype(BF16)
    tail_bc = mm(hit, pbc[...])
    raw_bc = bbc[...].astype(F32) * first
    raw = jnp.concatenate([step, logs, jnp.zeros((64, LANES), F32)], axis=0).T
    early[...] = jnp.zeros(early.shape, F32)
    for r in range(3):
        early[:, (TAIL_X + r) * LANES : (TAIL_X + r + 1) * LANES] = tails[r * js : (r + 1) * js]
        early[:, (ROW_X + r) * LANES : (ROW_X + r + 1) * LANES] = bx[r].astype(F32) * first
        early[:, (ROW_DY + r) * LANES : (ROW_DY + r + 1) * LANES] = bdy[r].astype(F32) * (
            first * (r < length).astype(F32)
        )
        for half in range(2):
            at = slice(half * STATE, (half + 1) * STATE)
            early[2 * r + half : 2 * r + half + 1, ROW_BC * LANES : (ROW_BC + 1) * LANES] = (
                tail_bc[r : r + 1, at]
            )
            early[6 + 2 * r + half : 7 + 2 * r + half, ROW_BC * LANES : (ROW_BC + 1) * LANES] = (
                raw_bc[r : r + 1, at]
            )
    early[0:8, ROW_STEP * LANES : (ROW_STEP + 1) * LANES] = raw[0:8] * first


def lead_kernel(
    scal, px, pbc, pdy, bbc, rim, convx, convbc, early, dys, table, tab,
    mine, other, bcs, pxs, pbcs, wexp, out,
):
    row, col = scal[17], scal[18]
    js = convx.shape[1]
    n = bbc.shape[0]
    span = px.shape[0]
    taps = [convbc[i : i + 1, :] for i in range(4)]
    bc = silu(conv_rows(bbc[...], bc_halo(rim, 19), taps, bcs))
    c_t = left(bc[:, STATE:].T)

    runs = table[...]
    grown = jnp.exp(runs)
    for j in range(0, js, 2):
        dy = [
            dys[pl.ds(q, n, stride=js), :] * head_lanes(grown, 32, q) for q in (j, j + 1)
        ]
        out[:, j * LANES : (j + 2) * LANES] = mm(c_t, right(jnp.concatenate(dy, axis=1)))

    own = [convx[i, pl.ds(col, 1), :] for i in range(4)]
    x_p = silu(conv_rows(px[...], [rim[r, 16:17, :] for r in range(3)], own, pxs))
    bc_p = silu(conv_rows(pbc[...], bc_halo(rim, 17), taps, pbcs))
    b_pt = left(bc_p[:, :STATE].T)
    c_pt = left(bc_p[:, STATE:].T)
    ptable = tab[...]
    runs = halves(ptable[:, 0:1], ptable[:, 1:2], (span, LANES))
    steps = halves(ptable[:, 2:3], ptable[:, 3:4], (span, LANES))
    wexp[...] = runs
    x_hat = x_p * steps
    base = 2 * js * LANES
    out[:, base : base + LANES] = mm(b_pt, right(x_hat * jnp.exp(runs[span - 1 : span, :] - runs)))
    out[:, base + LANES : base + 2 * LANES] = mm(
        c_pt, right(pdy[...].astype(F32) * jnp.exp(runs))
    )
    lane = iota((1, LANES), 1)
    pxs[0:span, :] = x_hat

    def fork(g, acc):
        where = scal[g] - 1 - row * span
        inside = (where >= 0) & (where < span)

        @pl.when(inside)
        def _():
            w = wexp[...]
            gap = wexp[pl.ds(where, 1), :] - w
            upto = iota((span, LANES), 0) <= where
            u = jnp.exp(jnp.where(upto, gap, -1e30)) * pxs[0:span, :]
            out[:, block(js + g)] = mm(b_pt, right(u))

        @pl.when(jnp.logical_not(inside))
        def _():
            out[:, block(js + g)] = jnp.zeros((STATE, LANES), F32)

        safe = jnp.clip(where, 0, span - 1)
        return jnp.where(lane // 2 == 32 + g, tab[pl.ds(safe, 1), :], acc)

    marks = lax.fori_loop(0, js, fork, jnp.zeros((1, LANES), F32))
    misc = jnp.where(lane < 2, ptable[span - 1 : span, :], marks)
    misc = jnp.where((lane >= 32) & (lane < 64), table[n - 1 : n, :], misc)
    out[:, base + 2 * LANES : base + 3 * LANES] = jnp.broadcast_to(misc, (STATE, LANES))

    for h, half_out in enumerate((mine, other)):
        half_out[:, : base + 3 * LANES] = out[part(h, row), :]
        for q in range(half_out.shape[0] // js):
            half_out[q * js : (q + 1) * js, base + 3 * LANES :] = early[...]


def pair_falls(even, odd, column):
    both = jnp.concatenate([even[0:1, column], odd[0:1, column], jnp.zeros((6, LANES), F32)], 0)
    return both, jnp.exp(both)


def head_lanes(values, base, j):
    at = base + 2 * j
    return halves(values[:, at : at + 1], values[:, at + 1 : at + 2], values.shape)


def in_odd(scal, g, span):
    where = scal[g] - 1 - lax.div(scal[17], 2) * (2 * span)
    return (where >= span) & (where < 2 * span)


def reach_of(mark, g):
    return jnp.exp(
        halves(mark[:, 64 + 2 * g : 65 + 2 * g], mark[:, 65 + 2 * g : 66 + 2 * g], (1, LANES))
    )


def by_core(row, run):
    core = lax.rem(row, 2)
    pl.when(core == 0)(functools.partial(run, True))
    pl.when(core == 1)(functools.partial(run, False))


def chip_kernel(scal, mine, theirs, out, keep_mine, keep_theirs):
    row, span = scal[17], scal[19]
    half = theirs.shape[0]
    js = 16
    base = 2 * js * LANES
    column = slice(base + 2 * LANES, base + 3 * LANES)
    keep_mine[...] = mine[:, base : base + 3 * LANES]
    keep_theirs[...] = theirs[:, base : base + 3 * LANES]

    def join(is_even):
        even, odd = (mine, theirs) if is_even else (theirs, mine)
        both, parts = pair_falls(even, odd, column)
        for j in range(js):
            fall = head_lanes(parts, 32, j)
            at = slice(j * LANES, (j + 1) * LANES)
            out[:, at] = even[:, at] + fall[0:1] * odd[:, at]
        fall = jnp.exp(halves(both[:, 0:1], both[:, 1:2], (8, LANES)))
        state = even[:, base : base + LANES]
        at = slice(base, base + LANES)
        out[:, at] = fall[1:2] * state + odd[:, at]
        at = slice(base + LANES, base + 2 * LANES)
        out[:, at] = even[:, at] + fall[0:1] * odd[:, at]
        lane = iota((1, LANES), 1)
        late = lane < 0
        for g in range(js):
            at = slice((js + g) * LANES, (js + g + 1) * LANES)
            is_odd = in_odd(scal, g, span)
            gain = is_odd.astype(F32) * reach_of(both[1:2], g)
            out[:, at] = even[:, at] + odd[:, at] + gain * state
            late = late | ((lane // 2 == 32 + g) & is_odd)
        before = jnp.where(lane % 2 == 0, both[0:1, 0:1], both[0:1, 1:2])
        marks = jnp.where(late, before + both[1:2], both[0:1])
        misc = jnp.where(lane < 64, both[0:1] + both[1:2], marks)
        out[:, column] = jnp.broadcast_to(misc, (half, LANES))
        out[:, base + 3 * LANES :] = even[:, base + 3 * LANES :] + odd[:, base + 3 * LANES :]

    by_core(row, join)


def by_chip(row, pieces):
    chips = len(pieces)
    chip = lax.div(row, 2)
    for d, piece in enumerate(pieces):
        ns = piece.shape[0]
        yield piece, pl.multiple_of(lax.rem(chip - d + chips, chips) * ns, ns)


def spread_branch_kernel(
    scal, got, p0, p1, p2, p3, mine, theirs, smine, stheirs, to_mine, to_other, after
):
    row = scal[17]
    js = 16
    column = slice((2 * js + 2) * LANES, (2 * js + 3) * LANES)
    for piece, first in by_chip(row, (p0, p1, p2, p3)):
        after[pl.ds(first, piece.shape[0]), :] = piece[:, : js * LANES]

    def split(is_even):
        even, odd = (mine, theirs) if is_even else (theirs, mine)
        state = smine if is_even else stheirs
        to_even, to_odd = (to_mine, to_other) if is_even else (to_other, to_mine)
        _, parts = pair_falls(even, odd, column)
        for j in range(js):
            fall = head_lanes(parts, 32, j)
            at = slice(j * LANES, (j + 1) * LANES)
            start = got[:, (js + 9 + j) * LANES : (js + 10 + j) * LANES]
            to_even[:, at] = start
            to_odd[:, at] = state[:, at] + fall[0:1] * start
            end = after[:, at]
            at2 = slice((js + j) * LANES, (js + j + 1) * LANES)
            to_even[:, at2] = odd[:, at] + fall[1:2] * end
            to_odd[:, at2] = end

    by_core(row, split)


def join_states_kernel(scal, mine, theirs, smine, stheirs, out):
    row = scal[17]
    js = 16
    column = slice(2 * LANES, 3 * LANES)

    def join(is_even):
        even, odd = (mine, theirs) if is_even else (theirs, mine)
        first, second = (smine, stheirs) if is_even else (stheirs, smine)
        _, parts = pair_falls(even, odd, column)
        for j in range(js):
            fall = head_lanes(parts, 32, j)
            at = slice(j * LANES, (j + 1) * LANES)
            out[:, at] = fall[1:2] * first[:, at] + second[:, at]

    by_core(row, join)


def slice_kernel(
    scal, got, convbc, joined, msg, adj, pst, cols, early, q0, q1, q2, q3, mat, turned, aft
):
    row = scal[17]
    count, ns = got.shape[0], got.shape[1]
    js = msg.shape[0]
    span = 2 * scal[19]
    base = 2 * js * LANES
    total = got[0, :, base + 3 * LANES :]
    for p in range(1, count):
        total = total + got[p, :, base + 3 * LANES :]
    early[...] = total
    for half in range(2):
        seq = [
            early[2 * r + half : 2 * r + half + 1, ROW_BC * LANES : (ROW_BC + 1) * LANES]
            for r in range(6)
        ]
        taps = [convbc[i : i + 1, half * STATE : (half + 1) * STATE] for i in range(4)]
        mat[...] = jnp.zeros((LANES, LANES), F32)
        for s in range(3):
            mat[s : s + 1, :] = sum(taps[i] * seq[s + i] for i in range(4))
        for i in range(4):
            mat[8 + i : 9 + i, :] = taps[i]
        turned[half * STATE : (half + 1) * STATE, :] = mat[...].T
    start = pl.multiple_of((lax.rem(row, 2) * count + lax.div(row, 2)) * ns, 16)
    b_col = turned[pl.ds(start, ns), :]
    c_col = turned[pl.ds(STATE + start, ns), :]
    cols[0:ns, :] = b_col
    cols[ns : 2 * ns, :] = c_col
    c_all = silu(c_col)
    misc = got[:, 0, base + 2 * LANES : base + 3 * LANES]
    falls_all = jnp.exp(misc)
    token = early[0:8, ROW_STEP * LANES : (ROW_STEP + 1) * LANES]
    token_falls = jnp.exp(token)
    for j in range(js):
        at = slice(j * LANES, (j + 1) * LANES)
        fall = head_lanes(falls_all, 32, j)
        falls = head_lanes(token_falls, 32, j)
        a = jnp.zeros((ns, LANES), F32)
        for p in reversed(range(count)):
            aft[p, :, at] = a
            a = fall[p : p + 1] * a + got[p, :, at]
        for s in (2, 1, 0):
            dy = early[j : j + 1, (ROW_DY + s) * LANES : (ROW_DY + s + 1) * LANES]
            a = a + dy * c_all[:, s : s + 1]
            adj[s, :, at] = a
            a = falls[s : s + 1] * a
        msg[j, ns : 2 * ns, :] = a
    pfall = jnp.exp(halves(misc[:, 0:1], misc[:, 1:2], (count, LANES)))
    state = jnp.zeros((ns, LANES), F32)
    for p in range(count):
        pst[p] = state
        state = pfall[p : p + 1] * state + got[p, :, base : base + LANES]
    for g in range(js):
        holder = lax.div(scal[g] - 1, span)
        mark = got[holder, 0:1, base + 2 * LANES : base + 3 * LANES]
        reach = reach_of(mark, g)
        at = slice((js + g) * LANES, (js + g + 1) * LANES)
        msg[g, 0:ns, :] = got[holder, :, at] + reach * pst[holder]
        for r in range(3):
            msg[g, 2 * ns + r : 2 * ns + r + 1, :] = early[
                g : g + 1, (TAIL_X + r) * LANES : (TAIL_X + r + 1) * LANES
            ]
        msg[g, 2 * ns + 3 : 2 * ns + 8, :] = jnp.zeros((5, LANES), F32)
    chip = lax.div(row, 2)
    for d, q in enumerate((q0, q1, q2, q3)):
        to = lax.rem(chip + d, count)
        q[:, : js * LANES] = aft[to]
        q[:, js * LANES :] = joined[pl.ds(pl.multiple_of(to * ns, ns), ns), :]


def chain_kernel(
    scal, got, moved, s0, s1, s2, s3, adj, pst, cols, early, convx, skip,
    msg, rows, injected, states,
):
    row = scal[17]
    first = (row == 0).astype(F32)
    count, ns = got.shape[0], got.shape[1]
    js = moved.shape[0]
    span = 2 * scal[19]
    b_col, c_col = cols[0:ns, :], cols[ns : 2 * ns, :]
    b_all, c_all = silu(b_col), silu(c_col)
    base = 2 * js * LANES
    wide = js * LANES
    for piece, first_row in by_chip(row, (s0, s1, s2, s3)):
        states[pl.ds(first_row, ns), :] = piece[:, js * LANES :]
    misc = got[:, 0, base + 2 * LANES : base + 3 * LANES]
    falls_all = jnp.exp(misc)
    token = early[0:8, ROW_STEP * LANES : (ROW_STEP + 1) * LANES]
    token_falls = jnp.exp(token)
    sum_b = [jnp.zeros((ns, LANES), F32) for _ in range(3)]
    sum_c = [jnp.zeros((ns, LANES), F32) for _ in range(3)]
    for j in range(js):
        at = slice(j * LANES, (j + 1) * LANES)
        fall = head_lanes(falls_all, 32, j)
        falls = head_lanes(token_falls, 32, j)
        steps = head_lanes(token, 0, j)
        seq = [moved[j, 2 * ns + r : 2 * ns + r + 1, :] for r in range(3)] + [
            early[j : j + 1, (ROW_X + s) * LANES : (ROW_X + s + 1) * LANES] for s in range(3)
        ]
        gain = skip[j : j + 1, :] * first
        state = moved[j, 0:ns, :]
        for s in range(3):
            dy = early[j : j + 1, (ROW_DY + s) * LANES : (ROW_DY + s + 1) * LANES]
            pre = sum(convx[i, j : j + 1, :] * seq[s + i] for i in range(4))
            sg = sigmoid(pre)
            x_conv = pre * sg
            x_hat = steps[s : s + 1] * x_conv
            state = falls[s : s + 1] * state + x_hat * b_all[:, s : s + 1]
            a = adj[s, :, at]
            rows[j : j + 1, s * LANES : (s + 1) * LANES] = (
                jnp.sum(state * c_all[:, s : s + 1], axis=0, keepdims=True) + gain * x_conv
            )
            grad = steps[s : s + 1] * jnp.sum(a * b_all[:, s : s + 1], axis=0, keepdims=True)
            rows[j : j + 1, (3 + s) * LANES : (4 + s) * LANES] = (
                sg * (1.0 + pre * (1.0 - sg)) * (grad + gain * dy)
            )
            sum_c[s] = sum_c[s] + dy * state
            sum_b[s] = sum_b[s] + x_hat * a
        for p in range(count):
            msg[p, :, (js + 9 + j) * LANES : (js + 10 + j) * LANES] = state
            state = fall[p : p + 1] * state + states[p * ns : (p + 1) * ns, at]
    lane = iota((ns, LANES), 1)
    back = jnp.zeros((ns, LANES), F32)
    for which, (total, column) in enumerate(((sum_b, b_col), (sum_c, c_col))):
        grads = [
            jnp.sum(total[s], axis=1, keepdims=True) * silu_slope(column[:, s : s + 1])
            for s in range(3)
        ]
        for m in range(3):
            tail = sum(grads[s] * column[:, 8 + m - s : 9 + m - s] for s in range(m + 1))
            back = jnp.where(lane == 3 * which + m, tail, back)
    pfall = jnp.exp(halves(misc[:, 0:1], misc[:, 1:2], (count, LANES)))
    injected[...] = jnp.zeros(injected.shape, F32)
    for g in range(js):
        holder = lax.div(scal[g] - 1, span)
        mark = got[holder, 0:1, base + 2 * LANES : base + 3 * LANES]
        reach = reach_of(mark, g)
        grad = moved[g, ns : 2 * ns, :]
        injected[holder] = injected[holder] + reach * grad
        for p in range(count):
            msg[p, :, g * LANES : (g + 1) * LANES] = grad
    a = jnp.zeros((ns, LANES), F32)
    for p in reversed(range(count)):
        msg[p, :, wide + LANES : wide + 2 * LANES] = a
        a = pfall[p : p + 1] * a + got[p, :, base + LANES : base + 2 * LANES] + injected[p]
    for p in range(count):
        msg[p, :, wide : wide + LANES] = pst[p]
        msg[p, :, wide + 2 * LANES : wide + 8 * LANES] = rows[...]
        msg[p, :, wide + 8 * LANES : wide + 9 * LANES] = back


def tail_grads(lead, taps):
    return [sum(lead[s] * taps[m - s] for s in range(m + 1)) for m in range(3)]


def assemble(core, mine, theirs, lanes, full):
    half = mine.shape[0]
    full[pl.ds(pl.multiple_of(core * half, half), half), :] = mine[:, lanes]
    full[pl.ds(pl.multiple_of((1 - core) * half, half), half), :] = theirs[:, lanes]


def first_rows(mine, theirs, js, rows):
    at = slice((js + 2) * LANES, (js + 8) * LANES)
    total = mine[0:js, at] + theirs[0:js, at]
    for p in range(1, mine.shape[0] // js):
        total = total + mine[p * js : (p + 1) * js, at] + theirs[p * js : (p + 1) * js, at]
    rows[...] = total


def inner_kernel(
    scal, bx, bbc, rim, convx, convbc, skip, dys, table, wrow,
    smine, sother, yi, gi, rise,
    xs, xt, ds, bcs, out,
):
    row = scal[17]
    n, js = bx.shape[0], bx.shape[1]
    conv_branch(bx, rim, convx, xs, xt, ds)
    taps = [convbc[i : i + 1, :] for i in range(4)]
    bc = silu(conv_rows(bbc[...], bc_halo(rim, 19), taps, bcs))
    b, c = bc[:, :STATE], bc[:, STATE:]
    b_t = left(b.T)
    scores = mm_nt(left(c), right_nt(b))
    scores_t = mm_nt(left(b), right_nt(c))
    causal = iota((n, n), 0) >= iota((n, n), 1)
    causal_t = iota((n, n), 0) <= iota((n, n), 1)
    low = iota((n, LANES), 1) < HEAD_DIM

    runs = table[...]
    fall = jnp.exp(runs[n - 1 : n, :] - runs)
    faded = []
    for j in range(js):
        at = pl.ds(j, n, stride=js)
        steps = head_lanes(runs, 0, j)
        x_conv = xt[at, :]
        dy = dys[at, :]
        gain = skip[j : j + 1, :]
        x_hat = x_conv * steps
        x_hi, x_lo = split2(x_hat)
        dy_b = dy.astype(BF16)
        zero = jnp.zeros_like(dy_b)
        faded.append(x_hat * head_lanes(fall, 32, j))
        if j % 2 == 1:
            out[:, (j - 1) * LANES : (j + 1) * LANES] = mm(
                b_t, right(jnp.concatenate(faded[-2:], axis=1))
            )
        mix, mix_t = [], []
        for k in range(2):
            down = jnp.broadcast_to(runs[:, 32 + 2 * j + k : 33 + 2 * j + k], (n, n))
            along = wrow[2 * j + k : 2 * j + k + 1, :]
            mix.append(split2(jnp.exp(jnp.where(causal, down - along, -1e30)) * scores))
            mix_t.append(split2(jnp.exp(jnp.where(causal_t, along - down, -1e30)) * scores_t))
        x_blk = [jnp.where(low, x_hi, zero), jnp.where(low, zero, x_hi)]
        x_rest = [jnp.where(low, x_lo, zero), jnp.where(low, zero, x_lo)]
        d_blk = [jnp.where(low, dy_b, zero), jnp.where(low, zero, dy_b)]
        y = mm(
            jnp.concatenate([mix[0][0], mix[1][0], mix[0][0], mix[1][0], mix[0][1], mix[1][1]], 1),
            jnp.concatenate(x_blk + x_rest + x_blk, 0),
        )
        yi[at, :] = y + gain * x_conv
        g = mm(
            jnp.concatenate([mix_t[0][0], mix_t[1][0], mix_t[0][1], mix_t[1][1]], 1),
            jnp.concatenate(d_blk + d_blk, 0),
        )
        slope = ds[at, :]
        gi[at, :] = (steps * g + gain * dy) * slope
        rise[at, :] = steps * slope * head_lanes(fall, 32, j)
    for h, half_out in enumerate((smine, sother)):
        half_out[...] = out[part(h, row), :]


def carry_kernel(
    scal, bbc, rim, convx, convbc, yi, gi, rise, table, rows, fmine, ftheirs,
    by, bgx, last, rims,
    xs, ys, bcs, start, after,
):
    row, length = scal[17], scal[16]
    n, js = by.shape[0], by.shape[1]
    core = lax.rem(row, 2)
    assemble(core, fmine, ftheirs, slice(0, js * LANES), start)
    assemble(core, fmine, ftheirs, slice(js * LANES, 2 * js * LANES), after)
    taps = [convbc[i : i + 1, :] for i in range(4)]
    bc = silu(conv_rows(bbc[...], bc_halo(rim, 19), taps, bcs))
    b_l, c_l = left(bc[:, :STATE]), left(bc[:, STATE:])
    xs[n * js : (n + 8) * js, :] = jnp.zeros((8 * js, LANES), F32)

    grown = jnp.exp(table[...])
    for j in range(0, js, 2):
        both = slice(j * LANES, (j + 2) * LANES)
        y = mm(c_l, right(start[:, both]))
        g = mm(b_l, right(after[:, both]))
        for q in range(2):
            at = pl.ds(j + q, n, stride=js)
            half = slice(q * LANES, (q + 1) * LANES)
            ys[at, :] = yi[at, :] + head_lanes(grown, 32, j + q) * y[:, half]
            xs[at, :] = gi[at, :] + rise[at, :] * g[:, half]

    @pl.when(row == 0)
    def _():
        for s in range(3):
            ys[s * js : (s + 1) * js, :] = rows[:, s * LANES : (s + 1) * LANES]
            xs[s * js : (s + 1) * js, :] = rows[:, (3 + s) * LANES : (4 + s) * LANES]

    def finish(c, _):
        at = pl.multiple_of(c * 16 * js, 16 * js)
        pos = row * n + c * 16 + iota((16, js, LANES), 0)
        y = ys[pl.ds(at, 16 * js), :].reshape(16, js, LANES)
        by[pl.ds(c * 16, 16)] = jnp.where(pos < length, y, 0.0).astype(BF16)
        g = jnp.zeros((16, js, LANES), F32)
        for i in range(4):
            g = g + convx[i][None] * xs[pl.ds(at + (3 - i) * js, 16 * js), :].reshape(
                16, js, LANES
            )
        bgx[pl.ds(c * 16, 16)] = g.astype(BF16)
        return 0

    lax.fori_loop(0, n // 16, finish, 0)
    for m in range(3):
        at = n - 3 + m
        last[m] = sum(
            convx[i] * xs[(at + 3 - i) * js : (at + 4 - i) * js, :] for i in range(4)
        )
    taps_x = [convx[i] for i in range(4)]
    for m, g in enumerate(tail_grads([xs[s * js : (s + 1) * js, :] for s in range(3)], taps_x)):
        rims[m, 0:js, :] = g


def prompt_inner_kernel(
    scal, px, pbc, pdy, rim, convx, convbc, skip, tab, prun,
    yp, gp, dbp, dcp, xh, xpre, bcpre, pxs, pbcs,
):
    col = scal[18]
    span = px.shape[0]
    taps = [convbc[i : i + 1, :] for i in range(4)]
    own = [convx[i, pl.ds(col, 1), :] for i in range(4)]
    gain = skip[pl.ds(col, 1), :]
    x_pre = conv_rows(px[...], [rim[r, 16:17, :] for r in range(3)], own, pxs)
    bc_pre = conv_rows(pbc[...], bc_halo(rim, 17), taps, pbcs)
    xpre[...] = x_pre
    bcpre[...] = bc_pre
    x_p = silu(x_pre)
    bc_p = silu(bc_pre)
    b_p, c_p = bc_p[:, :STATE], bc_p[:, STATE:]
    scores = mm_nt(left(c_p), right_nt(b_p))
    scores_t = mm_nt(left(b_p), right_nt(c_p))
    ptable = tab[...]
    steps = halves(ptable[:, 2:3], ptable[:, 3:4], (span, LANES))
    x_hat = x_p * steps
    xh[...] = x_hat
    x_hi, x_lo = split2(x_hat)
    dy_b = pdy[...]
    low = iota((span, LANES), 1) < HEAD_DIM
    zero = jnp.zeros_like(x_hi)
    causal = iota((span, span), 0) >= iota((span, span), 1)
    causal_t = iota((span, span), 0) <= iota((span, span), 1)
    y = gain * x_p
    g = jnp.zeros((span, LANES), F32)
    d_s = jnp.zeros((span, span), F32)
    d_st = jnp.zeros((span, span), F32)
    for k in range(2):
        keep = low if k == 0 else jnp.logical_not(low)
        xk_hi, xk_lo = jnp.where(keep, x_hi, zero), jnp.where(keep, x_lo, zero)
        dk = jnp.where(keep, dy_b, zero)
        down = jnp.broadcast_to(ptable[:, k : k + 1], (span, span))
        along = prun[k : k + 1, :]
        decay = jnp.exp(jnp.where(causal, down - along, -1e30))
        decay_t = jnp.exp(jnp.where(causal_t, along - down, -1e30))
        m_hi, m_lo = split2(decay * scores)
        t_hi, t_lo = split2(decay_t * scores_t)
        y = y + mm(
            jnp.concatenate([m_hi, m_hi, m_lo], 1), jnp.concatenate([xk_hi, xk_lo, xk_hi], 0)
        )
        g = g + mm(jnp.concatenate([t_hi, t_lo], 1), jnp.concatenate([dk, dk], 0))
        d_two = jnp.concatenate([dk, dk], 1)
        x_two = jnp.concatenate([x_hi, x_lo], 1)
        d_s = d_s + decay * mm_nt(d_two, x_two)
        d_st = d_st + decay_t * mm_nt(x_two, d_two)
    yp[...] = y
    gp[...] = g
    dcp[...] = mm(left(d_s), right(b_p))
    dbp[...] = mm(left(d_st), right(c_p))


def prompt_kernel(
    scal, pdy, convx, convbc, skip, tab, yp, gp, dbp, dcp, xh, xpre, bcpre,
    mine, theirs, keep_mine, keep_theirs, keep_far,
    py, pgx, msg, rims, rows,
    pxs, pbcs, wexp, dxh, dbs, got, tail, near,
):
    row, col = scal[17], scal[18]
    span, js = pdy.shape[0], convx.shape[1]
    base = js * LANES
    core = lax.rem(row, 2)
    assemble(core, mine, theirs, slice(0, base + 2 * LANES), got)
    assemble(core, mine, theirs, slice(base + 8 * LANES, base + 9 * LANES), tail)
    near[part(0, row), :] = keep_theirs[...]
    near[part(1, row), :] = keep_far[...]
    first_rows(mine, theirs, js, rows)
    mark = keep_theirs[0:1, 2 * LANES : 3 * LANES]
    fall = jnp.exp(halves(mark[:, 0:1], mark[:, 1:2], (1, LANES)))
    begin, end = slice(base, base + LANES), slice(base + LANES, base + 2 * LANES)

    @pl.when(core == 1)
    def _():
        got[:, begin] = near[:, :LANES] + fall * got[:, begin]

    @pl.when(core == 0)
    def _():
        got[:, end] = near[:, LANES : 2 * LANES] + fall * got[:, end]
        for g in range(js):

            @pl.when(in_odd(scal, g, span))
            def _():
                got[:, end] += reach_of(mark, g) * got[:, g * LANES : (g + 1) * LANES]

    taps_x = [convx[i] for i in range(4)]
    fork_lead = [rows[:, (3 + s) * LANES : (4 + s) * LANES] for s in range(3)]
    chunk = span // js
    for m, v in enumerate(tail_grads(fork_lead, taps_x)):
        for q in range(js):
            msg[q, 2 * chunk + m : 2 * chunk + m + 1, :] = v[q : q + 1]
    taps = [convbc[i : i + 1, :] for i in range(4)]
    own = [convx[i, pl.ds(col, 1), :] for i in range(4)]
    gain = skip[pl.ds(col, 1), :]
    x_hat = xh[...]
    bc_p = silu(bcpre[...])
    b_l, c_l = left(bc_p[:, :STATE]), left(bc_p[:, STATE:])
    ptable = tab[...]
    runs = halves(ptable[:, 0:1], ptable[:, 1:2], (span, LANES))
    steps = halves(ptable[:, 2:3], ptable[:, 3:4], (span, LANES))
    wexp[...] = runs
    dy = pdy[...].astype(F32)
    grown = jnp.exp(runs)
    rest = jnp.exp(runs[span - 1 : span, :] - runs)
    py[...] = (yp[...] + grown * mm(c_l, right(got[:, begin]))).astype(BF16)
    dxh[...] = gp[...] + rest * mm(b_l, right(got[:, end]))
    d_c = dcp[...] + mm_nt(left(grown * dy), right_nt(got[:, begin]))
    dbs[...] = dbp[...] + mm_nt(left(rest * x_hat), right_nt(got[:, end]))

    def fork(q, _):
        where = scal[q] - 1 - row * span

        @pl.when((where >= 0) & (where < span))
        def _():
            gap = wexp[pl.ds(where, 1), :] - wexp[...]
            u = jnp.exp(jnp.where(iota((span, LANES), 0) <= where, gap, -1e30))
            grad = got[:, block(q)]
            dxh[...] += u * mm(b_l, right(grad))
            dbs[...] += mm_nt(left(u * xh[...]), right_nt(grad))

        return 0

    lax.fori_loop(0, js, fork, 0)
    pxs[0:span, :] = (steps * dxh[...] + gain * dy) * silu_slope(xpre[...])
    pxs[span : span + 8, :] = jnp.zeros((8, LANES), F32)
    pgx[...] = sum(own[i] * pxs[3 - i : 3 - i + span, :] for i in range(4))
    for m, v in enumerate(tail_grads([pxs[s : s + 1, :] for s in range(3)], own)):
        rims[m, 0:1, :] = v
    pbcs[0:span, :] = jnp.concatenate([dbs[...], d_c], axis=1) * silu_slope(bcpre[...])
    pbcs[span : span + 8, :] = jnp.zeros((8, 2 * STATE), F32)
    grad = sum(taps[i] * pbcs[3 - i : 3 - i + span, :] for i in range(4))
    for m, v in enumerate(tail_grads([pbcs[s : s + 1, :] for s in range(3)], taps)):
        rims[m, 1:2, :] = v[:, :STATE]
        rims[m, 2:3, :] = v[:, STATE:]
    spot = iota((span, LANES), 0) - (scal[20] - 3 - row * span)
    lane = iota((span, LANES), 1)
    tails = exact(tail[...])
    for half in range(2):
        hit = ((spot >= 0) & (spot < 3) & (lane == spot + 3 * half)).astype(F32).astype(BF16)
        into = mm_nt(jnp.concatenate([hit, hit, hit], 1), tails)
        total = grad[:, half * STATE : (half + 1) * STATE] + into
        for q in range(js):
            msg[q, half * chunk : (half + 1) * chunk, :] = total[
                q * chunk : (q + 1) * chunk
            ]
    for q in range(js):
        msg[q, 2 * chunk + 3 : 2 * chunk + 8, :] = jnp.zeros((5, LANES), F32)


def rim_kernel(msg, back, out):
    rows = (msg.shape[1] - 8) // 2
    out[...] = msg[...]
    for m in range(3):
        for half in range(2):
            at = (half + 1) * rows - 3 + m
            out[0, at : at + 1, :] = msg[0, at : at + 1, :] + back[m, 1 + half : 2 + half, :]


def finish_kernel(scal, pgx, back, got, out_x, out_bc, tails):
    row = scal[17]
    span, peers = pgx.shape[0], got.shape[0]
    rows = span // peers
    total = got[0, 0 : 2 * rows, :]
    for p in range(1, peers):
        total = total + got[p, 0 : 2 * rows, :]
    out_bc[:, :STATE] = total[0:rows].astype(BF16)
    out_bc[:, STATE:] = total[rows : 2 * rows].astype(BF16)
    lane = iota((1, LANES), 1)
    spot = jnp.full((1, LANES), -1, jnp.int32)
    tails[...] = jnp.zeros((LANES, LANES), F32)
    for g in range(peers):
        tails[8 * g : 8 * g + 8, :] = got[g, 2 * rows : 2 * rows + 8, :]
        where = scal[g] - 3 - row * span + lane - 8 * g
        spot = jnp.where((lane >= 8 * g) & (lane < 8 * g + 3), where, spot)
    hit = (iota((span, LANES), 0) == spot).astype(F32).astype(BF16)
    into = mm(jnp.concatenate([hit, hit, hit], 1), jnp.concatenate(split3(tails[...]), 0))
    total = pgx[...] + into
    where = iota((span, LANES), 0)
    for m in range(3):
        total = total + jnp.where(where == span - 3 + m, back[m, 0:1, :], 0.0)
    out_x[...] = total.astype(BF16)


def call(
    kernel, args, outs, scratch, scalars=1, flops=10**9, blocks=None, out_smem=0,
    out_blocks=None, aliases=None, limit=VMEM_LIMIT,
):
    vmem = pl.BlockSpec(memory_space=pltpu.VMEM)
    smem = pl.BlockSpec(memory_space=pltpu.SMEM)
    given = [smem] * scalars + [vmem] * (len(args) - scalars)
    for at, spec in (blocks or {}).items():
        given[at] = spec
    taken = [smem] * out_smem + [vmem] * (len(outs) - out_smem)
    for at, spec in (out_blocks or {}).items():
        taken[at] = spec
    return pl.pallas_call(
        kernel,
        grid=(1,) if blocks else (),
        out_shape=[jax.ShapeDtypeStruct(s, d) for s, d in outs],
        in_specs=given,
        out_specs=taken,
        input_output_aliases=aliases or {},
        scratch_shapes=[pltpu.VMEM(s, F32) for s in scratch],
        compiler_params=pltpu.CompilerParams(vmem_limit_bytes=limit),
        cost_estimate=pl.CostEstimate(flops=flops, bytes_accessed=10**6, transcendentals=0),
    )(*args)


def shards(
    prompt_x,
    prompt_bc,
    prompt_dt,
    branch_x,
    branch_bc,
    branch_dt,
    conv_x,
    conv_bc,
    a_log,
    dt_bias,
    d_skip,
    lengths,
    forks,
    holder,
    prompt_dy,
    branch_dy,
):
    count = lax.axis_size("prefix")
    js = lax.axis_size("branch")
    span = prompt_x.shape[0]
    n = branch_x.shape[1]
    heads = 2 * js
    ns = STATE // count
    chips = count // 2
    half = STATE // 2
    px = prompt_x.reshape(span, LANES)
    pbc = prompt_bc.reshape(span, 2 * STATE)
    pdt = prompt_dt.reshape(2, span)
    pdy = prompt_dy.reshape(span, LANES)
    bx = branch_x.reshape(n, js, LANES)
    bbc = branch_bc.reshape(n, 2 * STATE)
    bdt = branch_dt.reshape(heads, n)
    bdy = branch_dy.reshape(n, js, LANES)
    convx = conv_x.reshape(4, js, LANES)
    convbc = conv_bc.reshape(4, 2 * STATE)
    a_pair, bias_pair, skip_pair = (
        jnp.transpose(v.reshape(js, 2)) for v in (a_log, dt_bias, d_skip)
    )
    cores = [(i, i ^ 1) for i in range(count)]
    columns = [[i for i in range(count) if i % 2 == c] for c in range(2)]

    with jax.named_scope("setup"):
        scal, rim, step, logs, pstep, plogs, skip = call(
            setup_kernel,
            [forks, lengths, holder, bx, px, pbc, bbc, a_pair, bias_pair, skip_pair, bdt, pdt],
            [
                ((24,), jnp.int32),
                ((3, js + 5, LANES), F32),
                ((heads, n), F32),
                ((heads, n), F32),
                ((2, span), F32),
                ((2, span), F32),
                ((js, LANES), F32),
            ],
            [],
            scalars=3,
            out_smem=1,
            blocks={
                3: pl.BlockSpec((16, js, LANES), lambda i: (n // 16 - 1, 0, 0)),
                4: pl.BlockSpec((16, LANES), lambda i: (span // 16 - 1, 0)),
                5: pl.BlockSpec((16, 2 * STATE), lambda i: (span // 16 - 1, 0)),
                6: pl.BlockSpec((16, 2 * STATE), lambda i: (n // 16 - 1, 0)),
            },
        )
    rim = lax.ppermute(rim, "prefix", [(i, i + 1) for i in range(count - 1)])
    big = (n * js, LANES)
    tall = ((n + 8) * js, LANES)
    each = (half, js * LANES)
    piece = (ns, 2 * js * LANES)

    def across(v):
        return lax.ppermute(v, "prefix", cores)

    def round_chips(blocks):
        moved_on = [blocks[0]]
        for d in range(1, chips):
            pairs = [(i, (i + 2 * d) % count) for i in range(count)]
            moved_on.append(lax.ppermute(blocks[d], "prefix", pairs))
        return moved_on

    def between_chips(v):
        return lax.all_to_all(v, "prefix", 0, 0, axis_index_groups=columns, tiled=True)

    with jax.named_scope("early"):
        early_part, dys, table, run, tab, prun = call(
            early_kernel,
            [scal, px, pbc, pstep, plogs, bx, bbc, step, logs, bdy],
            [
                ((js, EARLY * LANES), F32),
                (big, F32),
                ((n, LANES), F32),
                ((heads, n), F32),
                ((span, LANES), F32),
                ((2, span), F32),
            ],
            [],
            blocks={
                5: pl.BlockSpec((16, js, LANES), lambda i: (0, 0, 0)),
                6: pl.BlockSpec((16, 2 * STATE), lambda i: (0, 0)),
            },
        )
    width = (2 * js + 3 + EARLY) * LANES
    with jax.named_scope("lead"):
        mine, other = call(
            lead_kernel,
            [
                scal, px, pbc, pdy, bbc, rim, convx, convbc, early_part, dys, table, tab,
            ],
            [((half, width), F32)] * 2,
            [
                (n + 8, 2 * STATE), (span + 8, LANES), (span + 8, 2 * STATE),
                (span, LANES), (STATE, (2 * js + 3) * LANES),
            ],
            limit=VMEM_SMALL,
        )
    theirs = across(other)
    with jax.named_scope("chip"):
        joined, keep_mine, keep_theirs = call(
            chip_kernel,
            [scal, mine, theirs],
            [((half, width), F32)] + [((half, 3 * LANES), F32)] * 2,
            [],
            limit=VMEM_SMALL,
        )
    got = between_chips(joined.reshape(chips, ns, width))
    with jax.named_scope("inner"):
        smine, sother, yi, gi, rise = call(
            inner_kernel,
            [scal, bx, bbc, rim, convx, convbc, skip, dys, table, run],
            [(each, F32)] * 2 + [(big, F32)] * 3,
            [tall, big, big, (n + 8, 2 * STATE), (STATE, js * LANES)],
            flops=10**10,
        )
    stheirs = across(sother)
    keep_far = across(keep_mine)
    with jax.named_scope("join_states"):
        (sjoined,) = call(
            join_states_kernel, [scal, keep_mine, keep_theirs, smine, stheirs], [(each, F32)], []
        )
    got, keep_far = lax.optimization_barrier((got, keep_far))
    with jax.named_scope("slices"):
        msg, adj, pst, cols, early, *ablocks = call(
            slice_kernel,
            [scal, got, convbc, sjoined],
            [
                ((js, 2 * ns + 8, LANES), F32),
                ((3, ns, js * LANES), F32),
                ((chips, ns, LANES), F32),
                ((2 * ns, LANES), F32),
                ((ns, EARLY * LANES), F32),
            ]
            + [(piece, F32)] * 4,
            [(LANES, LANES), (2 * STATE, LANES), (chips, ns, js * LANES)],
        )
    moved = lax.all_to_all(msg, "branch", 0, 0, tiled=True)
    agot = round_chips(ablocks)
    moved, *agot = lax.optimization_barrier((moved, *agot))
    width3 = (js + 9) * LANES
    with jax.named_scope("chains"):
        (msg3,) = call(
            chain_kernel,
            [scal, got, moved, *agot, adj, pst, cols, early, convx, skip],
            [((chips, ns, width3 + js * LANES), F32)],
            [(js, 6 * LANES), (chips, ns, LANES), each],
        )
    msg3, tab3 = lax.optimization_barrier((msg3, tab))
    got3 = between_chips(msg3).reshape(half, width3 + js * LANES)
    narrow = ((span, LANES), F32)
    wide2 = ((span, 2 * STATE), F32)
    with jax.named_scope("prompt_inner"):
        inner_parts = call(
            prompt_inner_kernel,
            [scal, px, pbc, pdy, rim, convx, convbc, skip, tab3, prun],
            [narrow] * 6 + [wide2],
            [(span + 8, LANES), (span + 8, 2 * STATE)],
            flops=10**10,
        )
    got3, *inner_parts = lax.optimization_barrier((got3, *inner_parts))
    theirs3 = across(got3)
    both = (half, 2 * js * LANES)
    with jax.named_scope("spread_branch"):
        fmine, fother = call(
            spread_branch_kernel,
            [scal, got3, *agot, mine, theirs, smine, stheirs],
            [(both, F32)] * 2,
            [each],
        )
    theirs3, fother = lax.optimization_barrier((theirs3, fother))
    ftheirs = across(fother)
    peers = (js, 2 * span // js + 8, LANES)
    with jax.named_scope("prompt"):
        py, pgx, out_msg, prims, rows = call(
            prompt_kernel,
            [
                scal, pdy, convx, convbc, skip, tab, *inner_parts,
                got3, theirs3, keep_mine, keep_theirs, keep_far,
            ],
            [
                ((span, LANES), BF16),
                narrow,
                (peers, F32),
                ((3, 3, LANES), F32),
                ((js, 6 * LANES), F32),
            ],
            [
                (span + 8, LANES), (span + 8, 2 * STATE), (span, LANES),
                (span, LANES), (span, STATE), (STATE, (js + 2) * LANES), (STATE, LANES),
                (STATE, 3 * LANES),
            ],
        )
    backward = [(i, i - 1) for i in range(1, count)]
    pback = lax.ppermute(prims, "prefix", backward)
    final = pl.BlockSpec((1,) + peers[1:], lambda i: (js - 1, 0, 0))
    with jax.named_scope("rim"):
        (out_msg,) = call(
            rim_kernel,
            [out_msg, pback],
            [(peers, F32)],
            [],
            scalars=0,
            blocks={0: final},
            out_blocks={0: final},
            aliases={0: 0},
        )
    end = lax.all_to_all(out_msg, "branch", 0, 0, tiled=True)
    with jax.named_scope("carry"):
        by, bgx, last, brims = call(
            carry_kernel,
            [
                scal, bbc, rim, convx, convbc, yi, gi, rise, table, rows, fmine, ftheirs,
            ],
            [
                ((n, js, LANES), BF16),
                ((n, js, LANES), BF16),
                ((3, js, LANES), F32),
                ((3, js, LANES), F32),
            ],
            [
                tall, big, (n + 8, 2 * STATE), (STATE, js * LANES), (STATE, js * LANES),
            ],
            flops=10**10,
        )
    bback = lax.ppermute(brims, "prefix", backward)
    bgx = bgx.at[-3:].set((last + bback).astype(BF16))
    with jax.named_scope("finish"):
        prompt_gx, prompt_gbc = call(
            finish_kernel,
            [scal, pgx, pback, end],
            [((span, LANES), BF16), ((span // js, 2 * STATE), BF16)],
            [(LANES, LANES)],
            limit=VMEM_SMALL,
        )
    return (
        py.reshape(prompt_x.shape),
        by.reshape(branch_x.shape),
        prompt_gx.reshape(prompt_x.shape),
        bgx.reshape(branch_x.shape),
        prompt_gbc.reshape(span // js, 1, 2 * STATE),
    )


def solution(mesh):
    return jax.shard_map(
        shards,
        mesh=mesh,
        in_specs=(
            P("prefix", "branch", "tensor", None),
            P("prefix", "tensor", None),
            P("branch", "tensor", None, "prefix"),
            P("branch", "prefix", None, "tensor", None),
            P("branch", "prefix", "tensor", None),
            P("branch", None, "tensor", None, "prefix"),
            P(None, None, "tensor", None),
            P(None, "tensor", None),
            P(None, "tensor", None),
            P(None, "tensor", None),
            P(None, "tensor", None),
            P(),
            P(),
            P(),
            P("prefix", "branch", "tensor", None),
            P("branch", "prefix", None, "tensor", None),
        ),
        out_specs=(
            P("prefix", "branch", "tensor", None),
            P("branch", "prefix", None, "tensor", None),
            P("prefix", "branch", "tensor", None),
            P("branch", "prefix", None, "tensor", None),
            P(("prefix", "branch"), "tensor", None),
        ),
        check_vma=False,
    )
```

```python
import functools

import jax
import jax.numpy as jnp
from jax import lax
from jax.experimental import pallas as pl
from jax.experimental.pallas import tpu as pltpu
from jax.sharding import PartitionSpec as P

HEAD_DIM = 64
STATE = 128
LANES = 128

F32 = jnp.float32
BF16 = jnp.bfloat16

TAIL_X = 0
ROW_X = 3
ROW_DY = 6
ROW_BC = 9
ROW_STEP = 10
EARLY = 11

VMEM_LIMIT = 56 * 1024 * 1024
VMEM_SMALL = 20 * 1024 * 1024


def split2(a):
    hi = a.astype(BF16)
    return hi, (a - hi.astype(F32)).astype(BF16)


def split3(a):
    hi = a.astype(BF16)
    rest = a - hi.astype(F32)
    mid = rest.astype(BF16)
    return hi, mid, (rest - mid.astype(F32)).astype(BF16)


def mm(a, b):
    return lax.dot_general(a, b, (((1,), (0,)), ((), ())), preferred_element_type=F32)


def mm_nt(a, b):
    return lax.dot_general(a, b, (((1,), (1,)), ((), ())), preferred_element_type=F32)


def left(a):
    hi, lo = split2(a)
    return jnp.concatenate([hi, hi, lo], axis=1)


def right(b):
    hi, lo = split2(b)
    return jnp.concatenate([hi, lo, hi], axis=0)


def right_nt(b):
    hi, lo = split2(b)
    return jnp.concatenate([hi, lo, hi], axis=1)


def exact(a):
    return jnp.concatenate(split3(a), axis=1)


def iota(shape, dim):
    return lax.broadcasted_iota(jnp.int32, shape, dim)


def picker(base, j):
    one = (iota((LANES, LANES), 0) == base + 2 * j + iota((LANES, LANES), 1) // HEAD_DIM).astype(
        F32
    ).astype(BF16)
    return jnp.concatenate([one, one, one], axis=0)


def running_sum(logs):
    size = logs.shape[1]
    upper = (iota((size, size), 0) <= iota((size, size), 1)).astype(F32).astype(BF16)
    return mm(exact(logs), jnp.concatenate([upper, upper, upper], axis=0))


def block(j):
    return pl.ds(pl.multiple_of(j * LANES, LANES), LANES)


def sigmoid(x):
    return 1.0 / (1.0 + jnp.exp(-x))


def head_column(pair, heads):
    shape = (heads, heads // 2)
    r = iota(shape, 0)
    both = jnp.where(r % 2 == 0, pair[0:1], pair[1:2])
    return jnp.sum(jnp.where(iota(shape, 1) == r // 2, both, 0.0), axis=1, keepdims=True)


def softplus(x):
    return jnp.maximum(x, 0.0) + jnp.log1p(jnp.exp(-jnp.abs(x)))


def setup_kernel(
    forks, lengths, holder, bx, px, pbc, bbc, alog, bias, gain, bdt, pdt,
    scal, rim, step, logs, pstep, plogs, skip,
):
    row, col = lax.axis_index("prefix"), lax.axis_index("branch")
    js = bx.shape[1]

    def place(b, _):
        group = lax.fori_loop(
            0, js, lambda c, t: t + (holder[c] < holder[b]).astype(jnp.int32), jnp.int32(0),
            unroll=16,
        )
        scal[group] = forks[b]

        @pl.when(group == col)
        def _():
            scal[16] = lengths[b]
            scal[20] = forks[b]

        return 0

    lax.fori_loop(0, js, place, 0)
    scal[17] = row
    scal[18] = col
    scal[19] = pdt.shape[1]
    last = bx.shape[0] - 3
    xl = px[...].astype(F32)
    bcl = pbc[...].astype(F32)
    bbl = bbc[...].astype(F32)
    for r in range(3):
        rim[r, 0:js, :] = bx[last + r].astype(F32)
        at = slice(last + r, last + r + 1)
        rim[r, js : js + 1, :] = xl[at]
        rim[r, js + 1 : js + 2, :] = bcl[at, :STATE]
        rim[r, js + 2 : js + 3, :] = bcl[at, STATE:]
        rim[r, js + 3 : js + 4, :] = bbl[at, :STATE]
        rim[r, js + 4 : js + 5, :] = bbl[at, STATE:]
    heads = bdt.shape[0]
    s = softplus(bdt[...] + head_column(bias[...], heads))
    step[...] = s
    logs[...] = -jnp.exp(head_column(alog[...], heads)) * s
    own = iota((2, js), 1) == col
    own_bias = jnp.sum(jnp.where(own, bias[...], 0.0), axis=1, keepdims=True)
    own_rate = jnp.exp(jnp.sum(jnp.where(own, alog[...], 0.0), axis=1, keepdims=True))
    s = softplus(pdt[...] + own_bias)
    pstep[...] = s
    plogs[...] = -own_rate * s
    diag = iota((js, js), 0) == iota((js, js), 1)
    first = jnp.sum(jnp.where(diag, gain[0:1], 0.0), axis=1, keepdims=True)
    second = jnp.sum(jnp.where(diag, gain[1:2], 0.0), axis=1, keepdims=True)
    skip[...] = halves(first, second, (js, LANES))


def conv_branch(bx, rim, convx, xs, xt, ds):
    js = bx.shape[1]
    for r in range(3):
        xs[(5 + r) * js : (6 + r) * js, :] = rim[r, 0:js, :]

    def fill(c, _):
        xs[pl.ds(pl.multiple_of(8 * js + c * 16 * js, 16 * js), 16 * js), :] = (
            bx[pl.ds(c * 16, 16)].astype(F32).reshape(16 * js, LANES)
        )
        return 0

    lax.fori_loop(0, bx.shape[0] // 16, fill, 0)

    def one(c, _):
        pre = jnp.zeros((16, js, LANES), F32)
        for i in range(4):
            start = pl.multiple_of((5 + i) * js + c * 16 * js, js)
            pre = pre + convx[i][None] * xs[pl.ds(start, 16 * js), :].reshape(16, js, LANES)
        sg = sigmoid(pre)
        at = pl.ds(pl.multiple_of(c * 16 * js, 16 * js), 16 * js)
        xt[at, :] = (pre * sg).reshape(16 * js, LANES)
        if ds is not None:
            ds[at, :] = (sg * (1.0 + pre * (1.0 - sg))).reshape(16 * js, LANES)
        return 0

    lax.fori_loop(0, bx.shape[0] // 16, one, 0)


def conv_rows(raw, halo_rows, taps, scratch):
    n = raw.shape[0]
    scratch[8 : 8 + n, :] = raw.astype(F32)
    for r in range(3):
        scratch[5 + r : 6 + r, :] = halo_rows[r]
    pre = jnp.zeros(raw.shape, F32)
    for i in range(4):
        pre = pre + taps[i] * scratch[5 + i : 5 + i + n, :]
    return pre


def bc_halo(rim, first):
    return [
        jnp.concatenate([rim[r, first : first + 1, :], rim[r, first + 1 : first + 2, :]], axis=1)
        for r in range(3)
    ]


def silu(x):
    return x * sigmoid(x)


def silu_slope(x):
    sg = sigmoid(x)
    return sg * (1.0 + x * (1.0 - sg))


def without_first(row, values):
    return jnp.where((row == 0) & (iota(values.shape, 1) < 3), 0.0, values)


def branch_table(step, run):
    return jnp.concatenate([step, run, jnp.zeros((64, LANES), F32)], axis=0).T


def prompt_table(step, run):
    n = step.shape[1]
    r = iota((LANES, n), 0)
    runs = jnp.where(r % 2 == 0, run[0:1], run[1:2])
    steps = jnp.where(r % 2 == 0, step[0:1], step[1:2])
    return jnp.where((r == 2) | (r == 3), steps, runs).T


def halves(first, second, shape):
    return jnp.where(iota(shape, 1) < HEAD_DIM, first, second)


def part(h, row):
    half = STATE // 2
    core = lax.rem(row, 2)
    return pl.ds(pl.multiple_of((core if h == 0 else 1 - core) * half, half), half)


def live_dy(row, length, bdy, dys):
    n, js = bdy.shape[0], bdy.shape[1]

    def fill(c, _):
        pos = row * n + c * 16 + iota((16, js, LANES), 0)
        dead = (pos >= length) | (pos < 3)
        dys[pl.ds(pl.multiple_of(c * 16 * js, 16 * js), 16 * js), :] = jnp.where(
            dead, 0.0, bdy[pl.ds(c * 16, 16)].astype(F32)
        ).reshape(16 * js, LANES)
        return 0

    lax.fori_loop(0, n // 16, fill, 0)


def early_kernel(
    scal, px, pbc, pstep, plogs, bx, bbc, bstep, blogs, bdy,
    early, dys, table, run, ptable, prun,
):
    row, length = scal[17], scal[16]
    js = bdy.shape[1]
    span = px.shape[0]
    live_dy(row, length, bdy, dys)
    step, logs = bstep[...], blogs[...]
    sums = running_sum(without_first(row, logs))
    run[...] = sums
    table[...] = branch_table(without_first(row, step), sums)
    sums = running_sum(plogs[...])
    prun[...] = sums
    ptable[...] = prompt_table(pstep[...], sums)
    first = (row == 0).astype(F32)
    lane2 = iota((js, span), 1)
    spot = jnp.zeros((js, span), jnp.int32)
    for g in range(js):
        spot = jnp.where(iota((js, span), 0) == g, scal[g] - 3 - row * span, spot)
    hits = jnp.concatenate([(lane2 == spot + r).astype(F32).astype(BF16) for r in range(3)], 0)
    tails = mm(hits, px[...])
    own_spot = scal[20] - 3 - row * span + iota((js, span), 0)
    hit = ((lane2 == own_spot) & (iota((js, span), 0) < 3)).astype(F32).astype(BF16)
    tail_bc = mm(hit, pbc[...])
    raw_bc = bbc[...].astype(F32) * first
    raw = jnp.concatenate([step, logs, jnp.zeros((64, LANES), F32)], axis=0).T
    early[...] = jnp.zeros(early.shape, F32)
    for r in range(3):
        early[:, (TAIL_X + r) * LANES : (TAIL_X + r + 1) * LANES] = tails[r * js : (r + 1) * js]
        early[:, (ROW_X + r) * LANES : (ROW_X + r + 1) * LANES] = bx[r].astype(F32) * first
        early[:, (ROW_DY + r) * LANES : (ROW_DY + r + 1) * LANES] = bdy[r].astype(F32) * (
            first * (r < length).astype(F32)
        )
        for half in range(2):
            at = slice(half * STATE, (half + 1) * STATE)
            early[2 * r + half : 2 * r + half + 1, ROW_BC * LANES : (ROW_BC + 1) * LANES] = (
                tail_bc[r : r + 1, at]
            )
            early[6 + 2 * r + half : 7 + 2 * r + half, ROW_BC * LANES : (ROW_BC + 1) * LANES] = (
                raw_bc[r : r + 1, at]
            )
    early[0:8, ROW_STEP * LANES : (ROW_STEP + 1) * LANES] = raw[0:8] * first


def lead_kernel(
    scal, px, pbc, pdy, bbc, rim, convx, convbc, early, dys, table, tab,
    mine, other, bcs, pxs, pbcs, wexp, out,
):
    row, col = scal[17], scal[18]
    js = convx.shape[1]
    n = bbc.shape[0]
    span = px.shape[0]
    taps = [convbc[i : i + 1, :] for i in range(4)]
    bc = silu(conv_rows(bbc[...], bc_halo(rim, 19), taps, bcs))
    c_t = left(bc[:, STATE:].T)

    runs = table[...]
    grown = jnp.exp(runs)
    for j in range(0, js, 2):
        dy = [
            dys[pl.ds(q, n, stride=js), :] * head_lanes(grown, 32, q) for q in (j, j + 1)
        ]
        out[:, j * LANES : (j + 2) * LANES] = mm(c_t, right(jnp.concatenate(dy, axis=1)))

    own = [convx[i, pl.ds(col, 1), :] for i in range(4)]
    x_p = silu(conv_rows(px[...], [rim[r, 16:17, :] for r in range(3)], own, pxs))
    bc_p = silu(conv_rows(pbc[...], bc_halo(rim, 17), taps, pbcs))
    b_pt = left(bc_p[:, :STATE].T)
    c_pt = left(bc_p[:, STATE:].T)
    ptable = tab[...]
    runs = halves(ptable[:, 0:1], ptable[:, 1:2], (span, LANES))
    steps = halves(ptable[:, 2:3], ptable[:, 3:4], (span, LANES))
    wexp[...] = runs
    x_hat = x_p * steps
    base = 2 * js * LANES
    out[:, base : base + LANES] = mm(b_pt, right(x_hat * jnp.exp(runs[span - 1 : span, :] - runs)))
    out[:, base + LANES : base + 2 * LANES] = mm(
        c_pt, right(pdy[...].astype(F32) * jnp.exp(runs))
    )
    lane = iota((1, LANES), 1)
    pxs[0:span, :] = x_hat

    def fork(g, acc):
        where = scal[g] - 1 - row * span
        inside = (where >= 0) & (where < span)

        @pl.when(inside)
        def _():
            w = wexp[...]
            gap = wexp[pl.ds(where, 1), :] - w
            upto = iota((span, LANES), 0) <= where
            u = jnp.exp(jnp.where(upto, gap, -1e30)) * pxs[0:span, :]
            out[:, block(js + g)] = mm(b_pt, right(u))

        @pl.when(jnp.logical_not(inside))
        def _():
            out[:, block(js + g)] = jnp.zeros((STATE, LANES), F32)

        safe = jnp.clip(where, 0, span - 1)
        return jnp.where(lane // 2 == 32 + g, tab[pl.ds(safe, 1), :], acc)

    marks = lax.fori_loop(0, js, fork, jnp.zeros((1, LANES), F32))
    misc = jnp.where(lane < 2, ptable[span - 1 : span, :], marks)
    misc = jnp.where((lane >= 32) & (lane < 64), table[n - 1 : n, :], misc)
    out[:, base + 2 * LANES : base + 3 * LANES] = jnp.broadcast_to(misc, (STATE, LANES))

    for h, half_out in enumerate((mine, other)):
        half_out[:, : base + 3 * LANES] = out[part(h, row), :]
        for q in range(half_out.shape[0] // js):
            half_out[q * js : (q + 1) * js, base + 3 * LANES :] = early[...]


def pair_falls(even, odd, column):
    both = jnp.concatenate([even[0:1, column], odd[0:1, column], jnp.zeros((6, LANES), F32)], 0)
    return both, jnp.exp(both)


def head_lanes(values, base, j):
    at = base + 2 * j
    return halves(values[:, at : at + 1], values[:, at + 1 : at + 2], values.shape)


def in_odd(scal, g, span):
    where = scal[g] - 1 - lax.div(scal[17], 2) * (2 * span)
    return (where >= span) & (where < 2 * span)


def reach_of(mark, g):
    return jnp.exp(
        halves(mark[:, 64 + 2 * g : 65 + 2 * g], mark[:, 65 + 2 * g : 66 + 2 * g], (1, LANES))
    )


def by_core(row, run):
    core = lax.rem(row, 2)
    pl.when(core == 0)(functools.partial(run, True))
    pl.when(core == 1)(functools.partial(run, False))


def chip_kernel(scal, mine, theirs, out, keep_mine, keep_theirs):
    row, span = scal[17], scal[19]
    half = theirs.shape[0]
    js = 16
    base = 2 * js * LANES
    column = slice(base + 2 * LANES, base + 3 * LANES)
    keep_mine[...] = mine[:, base : base + 3 * LANES]
    keep_theirs[...] = theirs[:, base : base + 3 * LANES]

    def join(is_even):
        even, odd = (mine, theirs) if is_even else (theirs, mine)
        both, parts = pair_falls(even, odd, column)
        for j in range(js):
            fall = head_lanes(parts, 32, j)
            at = slice(j * LANES, (j + 1) * LANES)
            out[:, at] = even[:, at] + fall[0:1] * odd[:, at]
        fall = jnp.exp(halves(both[:, 0:1], both[:, 1:2], (8, LANES)))
        state = even[:, base : base + LANES]
        at = slice(base, base + LANES)
        out[:, at] = fall[1:2] * state + odd[:, at]
        at = slice(base + LANES, base + 2 * LANES)
        out[:, at] = even[:, at] + fall[0:1] * odd[:, at]
        lane = iota((1, LANES), 1)
        late = lane < 0
        for g in range(js):
            at = slice((js + g) * LANES, (js + g + 1) * LANES)
            is_odd = in_odd(scal, g, span)
            gain = is_odd.astype(F32) * reach_of(both[1:2], g)
            out[:, at] = even[:, at] + odd[:, at] + gain * state
            late = late | ((lane // 2 == 32 + g) & is_odd)
        before = jnp.where(lane % 2 == 0, both[0:1, 0:1], both[0:1, 1:2])
        marks = jnp.where(late, before + both[1:2], both[0:1])
        misc = jnp.where(lane < 64, both[0:1] + both[1:2], marks)
        out[:, column] = jnp.broadcast_to(misc, (half, LANES))
        out[:, base + 3 * LANES :] = even[:, base + 3 * LANES :] + odd[:, base + 3 * LANES :]

    by_core(row, join)


def by_chip(row, pieces):
    chips = len(pieces)
    chip = lax.div(row, 2)
    for d, piece in enumerate(pieces):
        ns = piece.shape[0]
        yield piece, pl.multiple_of(lax.rem(chip - d + chips, chips) * ns, ns)


def spread_branch_kernel(
    scal, got, p0, p1, p2, p3, mine, theirs, smine, stheirs, to_mine, to_other, after
):
    row = scal[17]
    js = 16
    column = slice((2 * js + 2) * LANES, (2 * js + 3) * LANES)
    for piece, first in by_chip(row, (p0, p1, p2, p3)):
        after[pl.ds(first, piece.shape[0]), :] = piece[:, : js * LANES]

    def split(is_even):
        even, odd = (mine, theirs) if is_even else (theirs, mine)
        state = smine if is_even else stheirs
        to_even, to_odd = (to_mine, to_other) if is_even else (to_other, to_mine)
        _, parts = pair_falls(even, odd, column)
        for j in range(js):
            fall = head_lanes(parts, 32, j)
            at = slice(j * LANES, (j + 1) * LANES)
            start = got[:, (js + 9 + j) * LANES : (js + 10 + j) * LANES]
            to_even[:, at] = start
            to_odd[:, at] = state[:, at] + fall[0:1] * start
            end = after[:, at]
            at2 = slice((js + j) * LANES, (js + j + 1) * LANES)
            to_even[:, at2] = odd[:, at] + fall[1:2] * end
            to_odd[:, at2] = end

    by_core(row, split)


def join_states_kernel(scal, mine, theirs, smine, stheirs, out):
    row = scal[17]
    js = 16
    column = slice(2 * LANES, 3 * LANES)

    def join(is_even):
        even, odd = (mine, theirs) if is_even else (theirs, mine)
        first, second = (smine, stheirs) if is_even else (stheirs, smine)
        _, parts = pair_falls(even, odd, column)
        for j in range(js):
            fall = head_lanes(parts, 32, j)
            at = slice(j * LANES, (j + 1) * LANES)
            out[:, at] = fall[1:2] * first[:, at] + second[:, at]

    by_core(row, join)


def slice_kernel(
    scal, got, convbc, joined, msg, adj, pst, cols, early, q0, q1, q2, q3, mat, turned, aft
):
    row = scal[17]
    count, ns = got.shape[0], got.shape[1]
    js = msg.shape[0]
    span = 2 * scal[19]
    base = 2 * js * LANES
    total = got[0, :, base + 3 * LANES :]
    for p in range(1, count):
        total = total + got[p, :, base + 3 * LANES :]
    early[...] = total
    for half in range(2):
        seq = [
            early[2 * r + half : 2 * r + half + 1, ROW_BC * LANES : (ROW_BC + 1) * LANES]
            for r in range(6)
        ]
        taps = [convbc[i : i + 1, half * STATE : (half + 1) * STATE] for i in range(4)]
        mat[...] = jnp.zeros((LANES, LANES), F32)
        for s in range(3):
            mat[s : s + 1, :] = sum(taps[i] * seq[s + i] for i in range(4))
        for i in range(4):
            mat[8 + i : 9 + i, :] = taps[i]
        turned[half * STATE : (half + 1) * STATE, :] = mat[...].T
    start = pl.multiple_of((lax.rem(row, 2) * count + lax.div(row, 2)) * ns, 16)
    b_col = turned[pl.ds(start, ns), :]
    c_col = turned[pl.ds(STATE + start, ns), :]
    cols[0:ns, :] = b_col
    cols[ns : 2 * ns, :] = c_col
    c_all = silu(c_col)
    misc = got[:, 0, base + 2 * LANES : base + 3 * LANES]
    falls_all = jnp.exp(misc)
    token = early[0:8, ROW_STEP * LANES : (ROW_STEP + 1) * LANES]
    token_falls = jnp.exp(token)
    for j in range(js):
        at = slice(j * LANES, (j + 1) * LANES)
        fall = head_lanes(falls_all, 32, j)
        falls = head_lanes(token_falls, 32, j)
        a = jnp.zeros((ns, LANES), F32)
        for p in reversed(range(count)):
            aft[p, :, at] = a
            a = fall[p : p + 1] * a + got[p, :, at]
        for s in (2, 1, 0):
            dy = early[j : j + 1, (ROW_DY + s) * LANES : (ROW_DY + s + 1) * LANES]
            a = a + dy * c_all[:, s : s + 1]
            adj[s, :, at] = a
            a = falls[s : s + 1] * a
        msg[j, ns : 2 * ns, :] = a
    pfall = jnp.exp(halves(misc[:, 0:1], misc[:, 1:2], (count, LANES)))
    state = jnp.zeros((ns, LANES), F32)
    for p in range(count):
        pst[p] = state
        state = pfall[p : p + 1] * state + got[p, :, base : base + LANES]
    for g in range(js):
        holder = lax.div(scal[g] - 1, span)
        mark = got[holder, 0:1, base + 2 * LANES : base + 3 * LANES]
        reach = reach_of(mark, g)
        at = slice((js + g) * LANES, (js + g + 1) * LANES)
        msg[g, 0:ns, :] = got[holder, :, at] + reach * pst[holder]
        for r in range(3):
            msg[g, 2 * ns + r : 2 * ns + r + 1, :] = early[
                g : g + 1, (TAIL_X + r) * LANES : (TAIL_X + r + 1) * LANES
            ]
        msg[g, 2 * ns + 3 : 2 * ns + 8, :] = jnp.zeros((5, LANES), F32)
    chip = lax.div(row, 2)
    for d, q in enumerate((q0, q1, q2, q3)):
        to = lax.rem(chip + d, count)
        q[:, : js * LANES] = aft[to]
        q[:, js * LANES :] = joined[pl.ds(pl.multiple_of(to * ns, ns), ns), :]


def chain_kernel(
    scal, got, moved, s0, s1, s2, s3, adj, pst, cols, early, convx, skip,
    msg, rows, injected, states,
):
    row = scal[17]
    first = (row == 0).astype(F32)
    count, ns = got.shape[0], got.shape[1]
    js = moved.shape[0]
    span = 2 * scal[19]
    b_col, c_col = cols[0:ns, :], cols[ns : 2 * ns, :]
    b_all, c_all = silu(b_col), silu(c_col)
    base = 2 * js * LANES
    wide = js * LANES
    for piece, first_row in by_chip(row, (s0, s1, s2, s3)):
        states[pl.ds(first_row, ns), :] = piece[:, js * LANES :]
    misc = got[:, 0, base + 2 * LANES : base + 3 * LANES]
    falls_all = jnp.exp(misc)
    token = early[0:8, ROW_STEP * LANES : (ROW_STEP + 1) * LANES]
    token_falls = jnp.exp(token)
    sum_b = [jnp.zeros((ns, LANES), F32) for _ in range(3)]
    sum_c = [jnp.zeros((ns, LANES), F32) for _ in range(3)]
    for j in range(js):
        at = slice(j * LANES, (j + 1) * LANES)
        fall = head_lanes(falls_all, 32, j)
        falls = head_lanes(token_falls, 32, j)
        steps = head_lanes(token, 0, j)
        seq = [moved[j, 2 * ns + r : 2 * ns + r + 1, :] for r in range(3)] + [
            early[j : j + 1, (ROW_X + s) * LANES : (ROW_X + s + 1) * LANES] for s in range(3)
        ]
        gain = skip[j : j + 1, :] * first
        state = moved[j, 0:ns, :]
        for s in range(3):
            dy = early[j : j + 1, (ROW_DY + s) * LANES : (ROW_DY + s + 1) * LANES]
            pre = sum(convx[i, j : j + 1, :] * seq[s + i] for i in range(4))
            sg = sigmoid(pre)
            x_conv = pre * sg
            x_hat = steps[s : s + 1] * x_conv
            state = falls[s : s + 1] * state + x_hat * b_all[:, s : s + 1]
            a = adj[s, :, at]
            rows[j : j + 1, s * LANES : (s + 1) * LANES] = (
                jnp.sum(state * c_all[:, s : s + 1], axis=0, keepdims=True) + gain * x_conv
            )
            grad = steps[s : s + 1] * jnp.sum(a * b_all[:, s : s + 1], axis=0, keepdims=True)
            rows[j : j + 1, (3 + s) * LANES : (4 + s) * LANES] = (
                sg * (1.0 + pre * (1.0 - sg)) * (grad + gain * dy)
            )
            sum_c[s] = sum_c[s] + dy * state
            sum_b[s] = sum_b[s] + x_hat * a
        for p in range(count):
            msg[p, :, (js + 9 + j) * LANES : (js + 10 + j) * LANES] = state
            state = fall[p : p + 1] * state + states[p * ns : (p + 1) * ns, at]
    lane = iota((ns, LANES), 1)
    back = jnp.zeros((ns, LANES), F32)
    for which, (total, column) in enumerate(((sum_b, b_col), (sum_c, c_col))):
        grads = [
            jnp.sum(total[s], axis=1, keepdims=True) * silu_slope(column[:, s : s + 1])
            for s in range(3)
        ]
        for m in range(3):
            tail = sum(grads[s] * column[:, 8 + m - s : 9 + m - s] for s in range(m + 1))
            back = jnp.where(lane == 3 * which + m, tail, back)
    pfall = jnp.exp(halves(misc[:, 0:1], misc[:, 1:2], (count, LANES)))
    injected[...] = jnp.zeros(injected.shape, F32)
    for g in range(js):
        holder = lax.div(scal[g] - 1, span)
        mark = got[holder, 0:1, base + 2 * LANES : base + 3 * LANES]
        reach = reach_of(mark, g)
        grad = moved[g, ns : 2 * ns, :]
        injected[holder] = injected[holder] + reach * grad
        for p in range(count):
            msg[p, :, g * LANES : (g + 1) * LANES] = grad
    a = jnp.zeros((ns, LANES), F32)
    for p in reversed(range(count)):
        msg[p, :, wide + LANES : wide + 2 * LANES] = a
        a = pfall[p : p + 1] * a + got[p, :, base + LANES : base + 2 * LANES] + injected[p]
    for p in range(count):
        msg[p, :, wide : wide + LANES] = pst[p]
        msg[p, :, wide + 2 * LANES : wide + 8 * LANES] = rows[...]
        msg[p, :, wide + 8 * LANES : wide + 9 * LANES] = back


def tail_grads(lead, taps):
    return [sum(lead[s] * taps[m - s] for s in range(m + 1)) for m in range(3)]


def assemble(core, mine, theirs, lanes, full):
    half = mine.shape[0]
    full[pl.ds(pl.multiple_of(core * half, half), half), :] = mine[:, lanes]
    full[pl.ds(pl.multiple_of((1 - core) * half, half), half), :] = theirs[:, lanes]


def first_rows(mine, theirs, js, rows):
    at = slice((js + 2) * LANES, (js + 8) * LANES)
    total = mine[0:js, at] + theirs[0:js, at]
    for p in range(1, mine.shape[0] // js):
        total = total + mine[p * js : (p + 1) * js, at] + theirs[p * js : (p + 1) * js, at]
    rows[...] = total


def inner_kernel(
    scal, bx, bbc, rim, convx, convbc, skip, dys, table, wrow,
    smine, sother, yi, gi, rise,
    xs, xt, ds, bcs, out,
):
    row = scal[17]
    n, js = bx.shape[0], bx.shape[1]
    conv_branch(bx, rim, convx, xs, xt, ds)
    taps = [convbc[i : i + 1, :] for i in range(4)]
    bc = silu(conv_rows(bbc[...], bc_halo(rim, 19), taps, bcs))
    b, c = bc[:, :STATE], bc[:, STATE:]
    b_t = left(b.T)
    scores = mm_nt(left(c), right_nt(b))
    scores_t = mm_nt(left(b), right_nt(c))
    causal = iota((n, n), 0) >= iota((n, n), 1)
    causal_t = iota((n, n), 0) <= iota((n, n), 1)
    low = iota((n, LANES), 1) < HEAD_DIM

    runs = table[...]
    fall = jnp.exp(runs[n - 1 : n, :] - runs)
    faded = []
    for j in range(js):
        at = pl.ds(j, n, stride=js)
        steps = head_lanes(runs, 0, j)
        x_conv = xt[at, :]
        dy = dys[at, :]
        gain = skip[j : j + 1, :]
        x_hat = x_conv * steps
        x_hi, x_lo = split2(x_hat)
        dy_b = dy.astype(BF16)
        zero = jnp.zeros_like(dy_b)
        faded.append(x_hat * head_lanes(fall, 32, j))
        if j % 2 == 1:
            out[:, (j - 1) * LANES : (j + 1) * LANES] = mm(
                b_t, right(jnp.concatenate(faded[-2:], axis=1))
            )
        mix, mix_t = [], []
        for k in range(2):
            down = jnp.broadcast_to(runs[:, 32 + 2 * j + k : 33 + 2 * j + k], (n, n))
            along = wrow[2 * j + k : 2 * j + k + 1, :]
            mix.append(split2(jnp.exp(jnp.where(causal, down - along, -1e30)) * scores))
            mix_t.append(split2(jnp.exp(jnp.where(causal_t, along - down, -1e30)) * scores_t))
        x_blk = [jnp.where(low, x_hi, zero), jnp.where(low, zero, x_hi)]
        x_rest = [jnp.where(low, x_lo, zero), jnp.where(low, zero, x_lo)]
        d_blk = [jnp.where(low, dy_b, zero), jnp.where(low, zero, dy_b)]
        y = mm(
            jnp.concatenate([mix[0][0], mix[1][0], mix[0][0], mix[1][0], mix[0][1], mix[1][1]], 1),
            jnp.concatenate(x_blk + x_rest + x_blk, 0),
        )
        yi[at, :] = y + gain * x_conv
        g = mm(
            jnp.concatenate([mix_t[0][0], mix_t[1][0], mix_t[0][1], mix_t[1][1]], 1),
            jnp.concatenate(d_blk + d_blk, 0),
        )
        slope = ds[at, :]
        gi[at, :] = (steps * g + gain * dy) * slope
        rise[at, :] = steps * slope * head_lanes(fall, 32, j)
    for h, half_out in enumerate((smine, sother)):
        half_out[...] = out[part(h, row), :]


def carry_kernel(
    scal, bbc, rim, convx, convbc, yi, gi, rise, table, rows, fmine, ftheirs,
    by, bgx, last, rims,
    xs, ys, bcs, start, after,
):
    row, length = scal[17], scal[16]
    n, js = by.shape[0], by.shape[1]
    core = lax.rem(row, 2)
    assemble(core, fmine, ftheirs, slice(0, js * LANES), start)
    assemble(core, fmine, ftheirs, slice(js * LANES, 2 * js * LANES), after)
    taps = [convbc[i : i + 1, :] for i in range(4)]
    bc = silu(conv_rows(bbc[...], bc_halo(rim, 19), taps, bcs))
    b_l, c_l = left(bc[:, :STATE]), left(bc[:, STATE:])
    xs[n * js : (n + 8) * js, :] = jnp.zeros((8 * js, LANES), F32)

    grown = jnp.exp(table[...])
    for j in range(0, js, 2):
        both = slice(j * LANES, (j + 2) * LANES)
        y = mm(c_l, right(start[:, both]))
        g = mm(b_l, right(after[:, both]))
        for q in range(2):
            at = pl.ds(j + q, n, stride=js)
            half = slice(q * LANES, (q + 1) * LANES)
            ys[at, :] = yi[at, :] + head_lanes(grown, 32, j + q) * y[:, half]
            xs[at, :] = gi[at, :] + rise[at, :] * g[:, half]

    @pl.when(row == 0)
    def _():
        for s in range(3):
            ys[s * js : (s + 1) * js, :] = rows[:, s * LANES : (s + 1) * LANES]
            xs[s * js : (s + 1) * js, :] = rows[:, (3 + s) * LANES : (4 + s) * LANES]

    def finish(c, _):
        at = pl.multiple_of(c * 16 * js, 16 * js)
        pos = row * n + c * 16 + iota((16, js, LANES), 0)
        y = ys[pl.ds(at, 16 * js), :].reshape(16, js, LANES)
        by[pl.ds(c * 16, 16)] = jnp.where(pos < length, y, 0.0).astype(BF16)
        g = jnp.zeros((16, js, LANES), F32)
        for i in range(4):
            g = g + convx[i][None] * xs[pl.ds(at + (3 - i) * js, 16 * js), :].reshape(
                16, js, LANES
            )
        bgx[pl.ds(c * 16, 16)] = g.astype(BF16)
        return 0

    lax.fori_loop(0, n // 16, finish, 0)
    for m in range(3):
        at = n - 3 + m
        last[m] = sum(
            convx[i] * xs[(at + 3 - i) * js : (at + 4 - i) * js, :] for i in range(4)
        )
    taps_x = [convx[i] for i in range(4)]
    for m, g in enumerate(tail_grads([xs[s * js : (s + 1) * js, :] for s in range(3)], taps_x)):
        rims[m, 0:js, :] = g


def prompt_inner_kernel(
    scal, px, pbc, pdy, rim, convx, convbc, skip, tab, prun,
    yp, gp, dbp, dcp, xh, xpre, bcpre, pxs, pbcs,
):
    col = scal[18]
    span = px.shape[0]
    taps = [convbc[i : i + 1, :] for i in range(4)]
    own = [convx[i, pl.ds(col, 1), :] for i in range(4)]
    gain = skip[pl.ds(col, 1), :]
    x_pre = conv_rows(px[...], [rim[r, 16:17, :] for r in range(3)], own, pxs)
    bc_pre = conv_rows(pbc[...], bc_halo(rim, 17), taps, pbcs)
    xpre[...] = x_pre
    bcpre[...] = bc_pre
    x_p = silu(x_pre)
    bc_p = silu(bc_pre)
    b_p, c_p = bc_p[:, :STATE], bc_p[:, STATE:]
    scores = mm_nt(left(c_p), right_nt(b_p))
    scores_t = mm_nt(left(b_p), right_nt(c_p))
    ptable = tab[...]
    steps = halves(ptable[:, 2:3], ptable[:, 3:4], (span, LANES))
    x_hat = x_p * steps
    xh[...] = x_hat
    x_hi, x_lo = split2(x_hat)
    dy_b = pdy[...]
    low = iota((span, LANES), 1) < HEAD_DIM
    zero = jnp.zeros_like(x_hi)
    causal = iota((span, span), 0) >= iota((span, span), 1)
    causal_t = iota((span, span), 0) <= iota((span, span), 1)
    y = gain * x_p
    g = jnp.zeros((span, LANES), F32)
    d_s = jnp.zeros((span, span), F32)
    d_st = jnp.zeros((span, span), F32)
    for k in range(2):
        keep = low if k == 0 else jnp.logical_not(low)
        xk_hi, xk_lo = jnp.where(keep, x_hi, zero), jnp.where(keep, x_lo, zero)
        dk = jnp.where(keep, dy_b, zero)
        down = jnp.broadcast_to(ptable[:, k : k + 1], (span, span))
        along = prun[k : k + 1, :]
        decay = jnp.exp(jnp.where(causal, down - along, -1e30))
        decay_t = jnp.exp(jnp.where(causal_t, along - down, -1e30))
        m_hi, m_lo = split2(decay * scores)
        t_hi, t_lo = split2(decay_t * scores_t)
        y = y + mm(
            jnp.concatenate([m_hi, m_hi, m_lo], 1), jnp.concatenate([xk_hi, xk_lo, xk_hi], 0)
        )
        g = g + mm(jnp.concatenate([t_hi, t_lo], 1), jnp.concatenate([dk, dk], 0))
        d_two = jnp.concatenate([dk, dk], 1)
        x_two = jnp.concatenate([x_hi, x_lo], 1)
        d_s = d_s + decay * mm_nt(d_two, x_two)
        d_st = d_st + decay_t * mm_nt(x_two, d_two)
    yp[...] = y
    gp[...] = g
    dcp[...] = mm(left(d_s), right(b_p))
    dbp[...] = mm(left(d_st), right(c_p))


def prompt_kernel(
    scal, pdy, convx, convbc, skip, tab, yp, gp, dbp, dcp, xh, xpre, bcpre,
    mine, theirs, keep_mine, keep_theirs, keep_far,
    py, pgx, msg, rims, rows,
    pxs, pbcs, wexp, dxh, dbs, got, tail, near,
):
    row, col = scal[17], scal[18]
    span, js = pdy.shape[0], convx.shape[1]
    base = js * LANES
    core = lax.rem(row, 2)
    assemble(core, mine, theirs, slice(0, base + 2 * LANES), got)
    assemble(core, mine, theirs, slice(base + 8 * LANES, base + 9 * LANES), tail)
    near[part(0, row), :] = keep_theirs[...]
    near[part(1, row), :] = keep_far[...]
    first_rows(mine, theirs, js, rows)
    mark = keep_theirs[0:1, 2 * LANES : 3 * LANES]
    fall = jnp.exp(halves(mark[:, 0:1], mark[:, 1:2], (1, LANES)))
    begin, end = slice(base, base + LANES), slice(base + LANES, base + 2 * LANES)

    @pl.when(core == 1)
    def _():
        got[:, begin] = near[:, :LANES] + fall * got[:, begin]

    @pl.when(core == 0)
    def _():
        got[:, end] = near[:, LANES : 2 * LANES] + fall * got[:, end]
        for g in range(js):

            @pl.when(in_odd(scal, g, span))
            def _():
                got[:, end] += reach_of(mark, g) * got[:, g * LANES : (g + 1) * LANES]

    taps_x = [convx[i] for i in range(4)]
    fork_lead = [rows[:, (3 + s) * LANES : (4 + s) * LANES] for s in range(3)]
    chunk = span // js
    for m, v in enumerate(tail_grads(fork_lead, taps_x)):
        for q in range(js):
            msg[q, 2 * chunk + m : 2 * chunk + m + 1, :] = v[q : q + 1]
    taps = [convbc[i : i + 1, :] for i in range(4)]
    own = [convx[i, pl.ds(col, 1), :] for i in range(4)]
    gain = skip[pl.ds(col, 1), :]
    x_hat = xh[...]
    bc_p = silu(bcpre[...])
    b_l, c_l = left(bc_p[:, :STATE]), left(bc_p[:, STATE:])
    ptable = tab[...]
    runs = halves(ptable[:, 0:1], ptable[:, 1:2], (span, LANES))
    steps = halves(ptable[:, 2:3], ptable[:, 3:4], (span, LANES))
    wexp[...] = runs
    dy = pdy[...].astype(F32)
    grown = jnp.exp(runs)
    rest = jnp.exp(runs[span - 1 : span, :] - runs)
    py[...] = (yp[...] + grown * mm(c_l, right(got[:, begin]))).astype(BF16)
    dxh[...] = gp[...] + rest * mm(b_l, right(got[:, end]))
    d_c = dcp[...] + mm_nt(left(grown * dy), right_nt(got[:, begin]))
    dbs[...] = dbp[...] + mm_nt(left(rest * x_hat), right_nt(got[:, end]))

    def fork(q, _):
        where = scal[q] - 1 - row * span

        @pl.when((where >= 0) & (where < span))
        def _():
            gap = wexp[pl.ds(where, 1), :] - wexp[...]
            u = jnp.exp(jnp.where(iota((span, LANES), 0) <= where, gap, -1e30))
            grad = got[:, block(q)]
            dxh[...] += u * mm(b_l, right(grad))
            dbs[...] += mm_nt(left(u * xh[...]), right_nt(grad))

        return 0

    lax.fori_loop(0, js, fork, 0)
    pxs[0:span, :] = (steps * dxh[...] + gain * dy) * silu_slope(xpre[...])
    pxs[span : span + 8, :] = jnp.zeros((8, LANES), F32)
    pgx[...] = sum(own[i] * pxs[3 - i : 3 - i + span, :] for i in range(4))
    for m, v in enumerate(tail_grads([pxs[s : s + 1, :] for s in range(3)], own)):
        rims[m, 0:1, :] = v
    pbcs[0:span, :] = jnp.concatenate([dbs[...], d_c], axis=1) * silu_slope(bcpre[...])
    pbcs[span : span + 8, :] = jnp.zeros((8, 2 * STATE), F32)
    grad = sum(taps[i] * pbcs[3 - i : 3 - i + span, :] for i in range(4))
    for m, v in enumerate(tail_grads([pbcs[s : s + 1, :] for s in range(3)], taps)):
        rims[m, 1:2, :] = v[:, :STATE]
        rims[m, 2:3, :] = v[:, STATE:]
    spot = iota((span, LANES), 0) - (scal[20] - 3 - row * span)
    lane = iota((span, LANES), 1)
    tails = exact(tail[...])
    for half in range(2):
        hit = ((spot >= 0) & (spot < 3) & (lane == spot + 3 * half)).astype(F32).astype(BF16)
        into = mm_nt(jnp.concatenate([hit, hit, hit], 1), tails)
        total = grad[:, half * STATE : (half + 1) * STATE] + into
        for q in range(js):
            msg[q, half * chunk : (half + 1) * chunk, :] = total[
                q * chunk : (q + 1) * chunk
            ]
    for q in range(js):
        msg[q, 2 * chunk + 3 : 2 * chunk + 8, :] = jnp.zeros((5, LANES), F32)


def rim_kernel(msg, back, out):
    rows = (msg.shape[1] - 8) // 2
    out[...] = msg[...]
    for m in range(3):
        for half in range(2):
            at = (half + 1) * rows - 3 + m
            out[0, at : at + 1, :] = msg[0, at : at + 1, :] + back[m, 1 + half : 2 + half, :]


def finish_kernel(scal, pgx, back, got, out_x, out_bc, tails):
    row = scal[17]
    span, peers = pgx.shape[0], got.shape[0]
    rows = span // peers
    total = got[0, 0 : 2 * rows, :]
    for p in range(1, peers):
        total = total + got[p, 0 : 2 * rows, :]
    out_bc[:, :STATE] = total[0:rows].astype(BF16)
    out_bc[:, STATE:] = total[rows : 2 * rows].astype(BF16)
    lane = iota((1, LANES), 1)
    spot = jnp.full((1, LANES), -1, jnp.int32)
    tails[...] = jnp.zeros((LANES, LANES), F32)
    for g in range(peers):
        tails[8 * g : 8 * g + 8, :] = got[g, 2 * rows : 2 * rows + 8, :]
        where = scal[g] - 3 - row * span + lane - 8 * g
        spot = jnp.where((lane >= 8 * g) & (lane < 8 * g + 3), where, spot)
    hit = (iota((span, LANES), 0) == spot).astype(F32).astype(BF16)
    into = mm(jnp.concatenate([hit, hit, hit], 1), jnp.concatenate(split3(tails[...]), 0))
    total = pgx[...] + into
    where = iota((span, LANES), 0)
    for m in range(3):
        total = total + jnp.where(where == span - 3 + m, back[m, 0:1, :], 0.0)
    out_x[...] = total.astype(BF16)


def call(
    kernel, args, outs, scratch, scalars=1, flops=10**9, blocks=None, out_smem=0,
    out_blocks=None, aliases=None, limit=VMEM_LIMIT,
):
    vmem = pl.BlockSpec(memory_space=pltpu.VMEM)
    smem = pl.BlockSpec(memory_space=pltpu.SMEM)
    given = [smem] * scalars + [vmem] * (len(args) - scalars)
    for at, spec in (blocks or {}).items():
        given[at] = spec
    taken = [smem] * out_smem + [vmem] * (len(outs) - out_smem)
    for at, spec in (out_blocks or {}).items():
        taken[at] = spec
    return pl.pallas_call(
        kernel,
        grid=(1,) if blocks else (),
        out_shape=[jax.ShapeDtypeStruct(s, d) for s, d in outs],
        in_specs=given,
        out_specs=taken,
        input_output_aliases=aliases or {},
        scratch_shapes=[pltpu.VMEM(s, F32) for s in scratch],
        compiler_params=pltpu.CompilerParams(vmem_limit_bytes=limit),
        cost_estimate=pl.CostEstimate(flops=flops, bytes_accessed=10**6, transcendentals=0),
    )(*args)


def shards(
    prompt_x,
    prompt_bc,
    prompt_dt,
    branch_x,
    branch_bc,
    branch_dt,
    conv_x,
    conv_bc,
    a_log,
    dt_bias,
    d_skip,
    lengths,
    forks,
    holder,
    prompt_dy,
    branch_dy,
):
    count = lax.axis_size("prefix")
    js = lax.axis_size("branch")
    span = prompt_x.shape[0]
    n = branch_x.shape[1]
    heads = 2 * js
    ns = STATE // count
    chips = count // 2
    half = STATE // 2
    px = prompt_x.reshape(span, LANES)
    pbc = prompt_bc.reshape(span, 2 * STATE)
    pdt = prompt_dt.reshape(2, span)
    pdy = prompt_dy.reshape(span, LANES)
    bx = branch_x.reshape(n, js, LANES)
    bbc = branch_bc.reshape(n, 2 * STATE)
    bdt = branch_dt.reshape(heads, n)
    bdy = branch_dy.reshape(n, js, LANES)
    convx = conv_x.reshape(4, js, LANES)
    convbc = conv_bc.reshape(4, 2 * STATE)
    a_pair, bias_pair, skip_pair = (
        jnp.transpose(v.reshape(js, 2)) for v in (a_log, dt_bias, d_skip)
    )
    cores = [(i, i ^ 1) for i in range(count)]
    columns = [[i for i in range(count) if i % 2 == c] for c in range(2)]

    with jax.named_scope("setup"):
        scal, rim, step, logs, pstep, plogs, skip = call(
            setup_kernel,
            [forks, lengths, holder, bx, px, pbc, bbc, a_pair, bias_pair, skip_pair, bdt, pdt],
            [
                ((24,), jnp.int32),
                ((3, js + 5, LANES), F32),
                ((heads, n), F32),
                ((heads, n), F32),
                ((2, span), F32),
                ((2, span), F32),
                ((js, LANES), F32),
            ],
            [],
            scalars=3,
            out_smem=1,
            blocks={
                3: pl.BlockSpec((16, js, LANES), lambda i: (n // 16 - 1, 0, 0)),
                4: pl.BlockSpec((16, LANES), lambda i: (span // 16 - 1, 0)),
                5: pl.BlockSpec((16, 2 * STATE), lambda i: (span // 16 - 1, 0)),
                6: pl.BlockSpec((16, 2 * STATE), lambda i: (n // 16 - 1, 0)),
            },
        )
    rim = lax.ppermute(rim, "prefix", [(i, i + 1) for i in range(count - 1)])
    big = (n * js, LANES)
    tall = ((n + 8) * js, LANES)
    each = (half, js * LANES)
    piece = (ns, 2 * js * LANES)

    def across(v):
        return lax.ppermute(v, "prefix", cores)

    def round_chips(blocks):
        moved_on = [blocks[0]]
        for d in range(1, chips):
            pairs = [(i, (i + 2 * d) % count) for i in range(count)]
            moved_on.append(lax.ppermute(blocks[d], "prefix", pairs))
        return moved_on

    def between_chips(v):
        return lax.all_to_all(v, "prefix", 0, 0, axis_index_groups=columns, tiled=True)

    with jax.named_scope("early"):
        early_part, dys, table, run, tab, prun = call(
            early_kernel,
            [scal, px, pbc, pstep, plogs, bx, bbc, step, logs, bdy],
            [
                ((js, EARLY * LANES), F32),
                (big, F32),
                ((n, LANES), F32),
                ((heads, n), F32),
                ((span, LANES), F32),
                ((2, span), F32),
            ],
            [],
            blocks={
                5: pl.BlockSpec((16, js, LANES), lambda i: (0, 0, 0)),
                6: pl.BlockSpec((16, 2 * STATE), lambda i: (0, 0)),
            },
            limit=VMEM_SMALL,
        )
    width = (2 * js + 3 + EARLY) * LANES
    with jax.named_scope("lead"):
        mine, other = call(
            lead_kernel,
            [
                scal, px, pbc, pdy, bbc, rim, convx, convbc, early_part, dys, table, tab,
            ],
            [((half, width), F32)] * 2,
            [
                (n + 8, 2 * STATE), (span + 8, LANES), (span + 8, 2 * STATE),
                (span, LANES), (STATE, (2 * js + 3) * LANES),
            ],
            limit=VMEM_SMALL,
        )
    theirs = across(other)
    with jax.named_scope("chip"):
        joined, keep_mine, keep_theirs = call(
            chip_kernel,
            [scal, mine, theirs],
            [((half, width), F32)] + [((half, 3 * LANES), F32)] * 2,
            [],
            limit=VMEM_SMALL,
        )
    got = between_chips(joined.reshape(chips, ns, width))
    with jax.named_scope("inner"):
        smine, sother, yi, gi, rise = call(
            inner_kernel,
            [scal, bx, bbc, rim, convx, convbc, skip, dys, table, run],
            [(each, F32)] * 2 + [(big, F32)] * 3,
            [tall, big, big, (n + 8, 2 * STATE), (STATE, js * LANES)],
            flops=10**10,
        )
    stheirs = across(sother)
    keep_far = across(keep_mine)
    with jax.named_scope("join_states"):
        (sjoined,) = call(
            join_states_kernel, [scal, keep_mine, keep_theirs, smine, stheirs], [(each, F32)], []
        )
    got, keep_far = lax.optimization_barrier((got, keep_far))
    with jax.named_scope("slices"):
        msg, adj, pst, cols, early, *ablocks = call(
            slice_kernel,
            [scal, got, convbc, sjoined],
            [
                ((js, 2 * ns + 8, LANES), F32),
                ((3, ns, js * LANES), F32),
                ((chips, ns, LANES), F32),
                ((2 * ns, LANES), F32),
                ((ns, EARLY * LANES), F32),
            ]
            + [(piece, F32)] * 4,
            [(LANES, LANES), (2 * STATE, LANES), (chips, ns, js * LANES)],
        )
    moved = lax.all_to_all(msg, "branch", 0, 0, tiled=True)
    agot = round_chips(ablocks)
    moved, *agot = lax.optimization_barrier((moved, *agot))
    width3 = (js + 9) * LANES
    with jax.named_scope("chains"):
        (msg3,) = call(
            chain_kernel,
            [scal, got, moved, *agot, adj, pst, cols, early, convx, skip],
            [((chips, ns, width3 + js * LANES), F32)],
            [(js, 6 * LANES), (chips, ns, LANES), each],
        )
    msg3, tab3 = lax.optimization_barrier((msg3, tab))
    got3 = between_chips(msg3).reshape(half, width3 + js * LANES)
    narrow = ((span, LANES), F32)
    wide2 = ((span, 2 * STATE), F32)
    with jax.named_scope("prompt_inner"):
        inner_parts = call(
            prompt_inner_kernel,
            [scal, px, pbc, pdy, rim, convx, convbc, skip, tab3, prun],
            [narrow] * 6 + [wide2],
            [(span + 8, LANES), (span + 8, 2 * STATE)],
            flops=10**10,
        )
    got3, *inner_parts = lax.optimization_barrier((got3, *inner_parts))
    theirs3 = across(got3)
    both = (half, 2 * js * LANES)
    with jax.named_scope("spread_branch"):
        fmine, fother = call(
            spread_branch_kernel,
            [scal, got3, *agot, mine, theirs, smine, stheirs],
            [(both, F32)] * 2,
            [each],
        )
    theirs3, fother = lax.optimization_barrier((theirs3, fother))
    ftheirs = across(fother)
    peers = (js, 2 * span // js + 8, LANES)
    with jax.named_scope("prompt"):
        py, pgx, out_msg, prims, rows = call(
            prompt_kernel,
            [
                scal, pdy, convx, convbc, skip, tab, *inner_parts,
                got3, theirs3, keep_mine, keep_theirs, keep_far,
            ],
            [
                ((span, LANES), BF16),
                narrow,
                (peers, F32),
                ((3, 3, LANES), F32),
                ((js, 6 * LANES), F32),
            ],
            [
                (span + 8, LANES), (span + 8, 2 * STATE), (span, LANES),
                (span, LANES), (span, STATE), (STATE, (js + 2) * LANES), (STATE, LANES),
                (STATE, 3 * LANES),
            ],
        )
    backward = [(i, i - 1) for i in range(1, count)]
    pback = lax.ppermute(prims, "prefix", backward)
    final = pl.BlockSpec((1,) + peers[1:], lambda i: (js - 1, 0, 0))
    with jax.named_scope("rim"):
        (out_msg,) = call(
            rim_kernel,
            [out_msg, pback],
            [(peers, F32)],
            [],
            scalars=0,
            blocks={0: final},
            out_blocks={0: final},
            aliases={0: 0},
        )
    end = lax.all_to_all(out_msg, "branch", 0, 0, tiled=True)
    with jax.named_scope("carry"):
        by, bgx, last, brims = call(
            carry_kernel,
            [
                scal, bbc, rim, convx, convbc, yi, gi, rise, table, rows, fmine, ftheirs,
            ],
            [
                ((n, js, LANES), BF16),
                ((n, js, LANES), BF16),
                ((3, js, LANES), F32),
                ((3, js, LANES), F32),
            ],
            [
                tall, big, (n + 8, 2 * STATE), (STATE, js * LANES), (STATE, js * LANES),
            ],
            flops=10**10,
        )
    bback = lax.ppermute(brims, "prefix", backward)
    bgx = bgx.at[-3:].set((last + bback).astype(BF16))
    with jax.named_scope("finish"):
        prompt_gx, prompt_gbc = call(
            finish_kernel,
            [scal, pgx, pback, end],
            [((span, LANES), BF16), ((span // js, 2 * STATE), BF16)],
            [(LANES, LANES)],
            limit=VMEM_SMALL,
        )
    return (
        py.reshape(prompt_x.shape),
        by.reshape(branch_x.shape),
        prompt_gx.reshape(prompt_x.shape),
        bgx.reshape(branch_x.shape),
        prompt_gbc.reshape(span // js, 1, 2 * STATE),
    )


def solution(mesh):
    return jax.shard_map(
        shards,
        mesh=mesh,
        in_specs=(
            P("prefix", "branch", "tensor", None),
            P("prefix", "tensor", None),
            P("branch", "tensor", None, "prefix"),
            P("branch", "prefix", None, "tensor", None),
            P("branch", "prefix", "tensor", None),
            P("branch", None, "tensor", None, "prefix"),
            P(None, None, "tensor", None),
            P(None, "tensor", None),
            P(None, "tensor", None),
            P(None, "tensor", None),
            P(None, "tensor", None),
            P(),
            P(),
            P(),
            P("prefix", "branch", "tensor", None),
            P("branch", "prefix", None, "tensor", None),
        ),
        out_specs=(
            P("prefix", "branch", "tensor", None),
            P("branch", "prefix", None, "tensor", None),
            P("prefix", "branch", "tensor", None),
            P("branch", "prefix", None, "tensor", None),
            P(("prefix", "branch"), "tensor", None),
        ),
        check_vma=False,
    )
```
